32 devices in a mesh: dp: 8 (over z, x), mp: 4 (over y, core).
Axes of the slice: x: 2, y: 2, z: 4, core: 2. Of those that a mesh axis runs over, the one named last changes fastest.
Arguments:
- inputs: bfloat16 [8192, 768], P('dp'), may hold values from -16 to 16
- segments: int32 [8192], P('dp'), may hold values from -1 to 3, as said below
- norm1_gain: bfloat16 [768], P('dp'), may hold values from 0.099609375 to 1.8984375
- norm1_shift: bfloat16 [768], P('dp'), may hold values from -4 to 4
- qkv_weight: bfloat16 [3, 768, 768], P(None, 'dp', 'mp'), may hold values from -0.21875 to 0.21875
- qv_bias: bfloat16 [12, 128], P('mp', 'dp'), may hold values from -3 to 3
- attn_weight: bfloat16 [768, 768], P('mp', 'dp'), may hold values from -1.75 to 1.75
- attn_bias: bfloat16 [768], P('dp'), may hold values from -4 to 4
- norm2_gain: bfloat16 [768], P('dp'), may hold values from 0.099609375 to 1.8984375
- norm2_shift: bfloat16 [768], P('dp'), may hold values from -4 to 4
- fc_weight: bfloat16 [768, 3072], P('dp', 'mp'), may hold values from -0.21875 to 0.21875
- fc_bias: bfloat16 [4, 768], P('mp', 'dp'), may hold values from -6 to 6
- proj_weight: bfloat16 [3072, 768], P('mp', 'dp'), may hold values from -0.109375 to 0.109375
- proj_bias: bfloat16 [768], P('dp'), may hold values from -4 to 4
- cotangent: bfloat16 [8192, 768], P('dp'), may hold values from -16 to 16
Outputs:
- outputs: bfloat16 [8192, 768], P('dp')
- inputs_grad: bfloat16 [8192, 768], P('dp')
- norm1_gain_grad: float32 [768], P('dp')
- norm1_shift_grad: float32 [768], P('dp')
- qkv_weight_grad: float32 [3, 768, 768], P(None, 'dp', 'mp')
- qv_bias_grad: float32 [12, 128], P('mp', 'dp')
- attn_weight_grad: float32 [768, 768], P('mp', 'dp')
- attn_bias_grad: float32 [768], P('dp')
- norm2_gain_grad: float32 [768], P('dp')
- norm2_shift_grad: float32 [768], P('dp')
- fc_weight_grad: float32 [768, 3072], P('dp', 'mp')
- fc_bias_grad: float32 [4, 768], P('mp', 'dp')
- proj_weight_grad: float32 [3072, 768], P('mp', 'dp')
- proj_bias_grad: float32 [768], P('dp')
The draws below stay inside these ranges and needn't reach their ends.
Inputs may be any that keep to these rules, and one draw needn't show every extreme that they name: `segments`: in each block of 1024 slots the used slots come first and their ids never fall, starting at 0; unused slots after them hold -1. Every block uses 1024 // 2 slots or more and holds at most four sequences; in every draw one block holds a single sequence of all 1024 slots.
All inputs are finite; a program needn't handle non-finite values.
Results may differ from the reference program's by a relative error of at most 0.015.
Values may be sent and summed in bfloat16 or wider, within the bound.
No kernel may reach another device: no remote copies, remote signals or barrier semaphores. Data moves between devices by JAX's collectives and lax.ppermute only.
A program may use at most 128 MiB of HBM per device.

```python
import jax
import jax.numpy as jnp
from jax import lax

D = 768
H = 12
HD = 64
FF = 3072
CAP = 1024
N_DP = 8


def log_spread(key, shape, low_end, high_end):
    return jnp.exp(jax.random.uniform(key, shape, jnp.float32, jnp.log(low_end), jnp.log(high_end)))


def draw_inputs(key, part):
    key = jax.random.fold_in(key, 11)
    keys = jax.random.split(key, 3)
    row_scale = log_spread(keys[0], (CAP * N_DP, 1), 0.3, 3.0)
    col_scale = log_spread(keys[1], (1, D), 0.3, 3.0)
    field = jax.random.normal(keys[2], (CAP * N_DP, D), jnp.float32) * row_scale * col_scale
    return jnp.clip(field, -16.0, 16.0).astype(jnp.bfloat16)


def draw_cotangent(key, part):
    key = jax.random.fold_in(key, 13)
    keys = jax.random.split(key, 3)
    row_scale = log_spread(keys[0], (CAP * N_DP, 1), 0.3, 3.0)
    col_scale = log_spread(keys[1], (1, D), 0.3, 3.0)
    field = jax.random.normal(keys[2], (CAP * N_DP, D), jnp.float32) * row_scale * col_scale
    return jnp.clip(field, -16.0, 16.0).astype(jnp.bfloat16)


def draw_segments(key, part):
    key = jax.random.fold_in(key, 5)
    keys = jax.random.split(key, 3)
    full_slot = jax.random.randint(keys[0], (), 0, N_DP)
    slot_ids = jnp.arange(N_DP)[:, None]
    used = jax.random.randint(keys[1], (N_DP, 1), CAP // 2, CAP + 1)
    used = jnp.where(slot_ids == full_slot, CAP, used)
    cuts = jax.random.randint(keys[2], (N_DP, 3), 1, used)
    cuts = jnp.where(slot_ids == full_slot, CAP, cuts)
    places = jnp.arange(CAP)[None, :]
    ids = jnp.sum((places[:, :, None] >= cuts[:, None, :]).astype(jnp.int32), -1)
    ids = jnp.where(places < used, ids, -1)
    return ids.reshape(-1).astype(jnp.int32)


def level_of(key, extent, shards, least, largest):
    def one(dim, blocks):
        draws = jax.random.uniform(jax.random.fold_in(jax.random.fold_in(key, 6), dim), (blocks,), jnp.float32, least / len(shards), largest / len(shards))
        return jnp.repeat(jnp.exp(draws), extent[dim] // blocks).reshape((-1,) + (1,) * (len(extent) - dim - 1))

    factor_of = one(*shards[0])
    for cut in shards[1:]:
        factor_of = factor_of * one(*cut)
    return factor_of


def bell_draw(own_key, shape, deviation, reach, pieces=(), kind=jnp.bfloat16):
    level = level_of(own_key, shape, pieces, -0.22, 0.18) if pieces else 1.0
    values = jax.random.normal(own_key, shape, jnp.float32) * deviation * level
    return jnp.minimum(jnp.maximum(values, -reach), reach).astype(kind)


def setup_inputs(seed: int = 0) -> dict:
    key_of = jax.random.split(jax.random.key(seed), 16)
    inputs = draw_inputs(jax.random.fold_in(key_of[15], 71), 0)
    segments = draw_segments(jax.random.fold_in(key_of[15], 71), 0)
    norm1_gain = jnp.clip(1.0 + 0.18 * jax.random.normal(key_of[2], (D,), jnp.float32), 0.099609375, 1.8984375).astype(jnp.bfloat16)
    norm1_shift = bell_draw(key_of[3], (D,), 0.3, 4.0, ((0, 8),))
    qkv_weight = bell_draw(key_of[4], (3, D, D), D ** -0.5, 0.21875, ((1, 8), (2, 4)))
    qv_bias = bell_draw(key_of[5], (H, 2 * HD), 0.2, 3.0, ((0, 4), (1, 8)))
    attn_weight = bell_draw(key_of[6], (D, D), (D // 64) ** -0.5, 1.75, ((0, 4), (1, 8)))
    attn_bias = bell_draw(key_of[7], (D,), 0.3, 4.0, ((0, 8),))
    norm2_gain = jnp.clip(1.0 + 0.18 * jax.random.normal(key_of[8], (D,), jnp.float32), 0.099609375, 1.8984375).astype(jnp.bfloat16)
    norm2_shift = bell_draw(key_of[9], (D,), 0.3, 4.0, ((0, 8),))
    fc_weight = bell_draw(key_of[10], (D, FF), D ** -0.5, 0.21875, ((0, 8), (1, 4)))
    fc_bias = bell_draw(key_of[11], (FF // D, D), 0.5, 6.0, ((0, 4), (1, 8)))
    proj_weight = bell_draw(key_of[12], (FF, D), FF ** -0.5, 0.109375, ((0, 4), (1, 8)))
    proj_bias = bell_draw(key_of[13], (D,), 0.3, 4.0, ((0, 8),))
    cotangent = draw_cotangent(jax.random.fold_in(key_of[15], 71), 0)
    return {"inputs": inputs, "segments": segments, "norm1_gain": norm1_gain, "norm1_shift": norm1_shift, "qkv_weight": qkv_weight, "qv_bias": qv_bias, "attn_weight": attn_weight, "attn_bias": attn_bias, "norm2_gain": norm2_gain, "norm2_shift": norm2_shift, "fc_weight": fc_weight, "fc_bias": fc_bias, "proj_weight": proj_weight, "proj_bias": proj_bias, "cotangent": cotangent}


@jax.custom_vjp
def low(v):
    return lax.optimization_barrier(v.astype(jnp.bfloat16)).astype(jnp.float32)

@jax.custom_vjp
def low_back(v):
    return v

def low_keep(v):
    return (low(v), None)

def low_pass(kept, grad):
    return (grad,)

def back_keep(v):
    return (v, None)

def back_low(kept, grad):
    return (low(grad),)
low.defvjp(low_keep, low_pass)
low_back.defvjp(back_keep, back_low)
EPSILON = 1e-05
NEGATIVE = -1e+30

def matmul(left, right):
    return jnp.dot(left, right, preferred_element_type=jnp.float32, precision=lax.Precision.HIGHEST)

def layer_norm(value, gain, shift):
    average = lax.optimization_barrier(jnp.mean(value, -1, keepdims=True))
    centred = value - average
    spread = lax.optimization_barrier(jnp.mean(centred * centred, -1, keepdims=True))
    return centred * lax.rsqrt(spread + EPSILON) * gain + shift

def gelu_tanh(value):
    return 0.5 * value * (1.0 + jnp.tanh(0.7978845608028654 * (value + 0.044715 * value * value * value)))

def attend(query, keyed, valued, block_seg):
    positions = jnp.arange(CAP)
    allowed = (block_seg[:, None] == block_seg[None, :]) & (positions[None, :] <= positions[:, None])
    scores = jnp.einsum('qhd,khd->hqk', query, keyed, precision=lax.Precision.HIGHEST) * float(HD) ** (-0.5)
    scores = low_back(scores)
    scores = jnp.where(allowed[None], scores, NEGATIVE)
    highest = lax.optimization_barrier(jnp.max(scores, -1, keepdims=True))
    weights = jnp.exp(scores - highest)
    probs = low(weights / lax.optimization_barrier(jnp.sum(weights, -1, keepdims=True)))
    return jnp.einsum('hqk,khd->qhd', probs, valued, precision=lax.Precision.HIGHEST)

def slot_forward(params, block_in, block_seg):
    gain_one, shift_one, qkv_full, bias_qv, attn_full, bias_attn, gain_two, shift_two, fc_full, bias_fc, proj_full, bias_proj = params
    live = (block_seg >= 0).astype(jnp.float32)[:, None]
    first = low(layer_norm(block_in, gain_one, shift_one))
    query = low_back(low(matmul(first, qkv_full[0]) + bias_qv[:, :HD].reshape(-1)))
    keyed = low_back(low(matmul(first, qkv_full[1])))
    valued = low_back(low(matmul(first, qkv_full[2]) + bias_qv[:, HD:].reshape(-1)))
    mixed = attend(query.reshape(CAP, H, HD), keyed.reshape(CAP, H, HD), valued.reshape(CAP, H, HD), block_seg)
    mixed = low_back(low(mixed.reshape(CAP, D)))
    branch = low_back(matmul(mixed, attn_full) + bias_attn)
    middle = block_in + branch
    second = low(layer_norm(middle, gain_two, shift_two))
    hidden = low_back(matmul(second, fc_full) + bias_fc.reshape(-1))
    active = low(gelu_tanh(hidden))
    return (middle + matmul(active, proj_full) + bias_proj) * live

def reference(inputs, segments, norm1_gain, norm1_shift, qkv_weight, qv_bias, attn_weight, attn_bias, norm2_gain, norm2_shift, fc_weight, fc_bias, proj_weight, proj_bias, cotangent):
    params = tuple((member.astype(jnp.float32) for member in (norm1_gain, norm1_shift, qkv_weight, qv_bias, attn_weight, attn_bias, norm2_gain, norm2_shift, fc_weight, fc_bias, proj_weight, proj_bias)))
    inflow = inputs.astype(jnp.float32).reshape(N_DP, CAP, D)
    seg_blocks = segments.reshape(N_DP, CAP)
    checked = jax.checkpoint(slot_forward)

    def forward(weights, streams):

        def apply_slot(item):
            return checked(weights, item[0], item[1])
        return lax.map(apply_slot, (streams, seg_blocks))
    result, pullback = jax.vjp(forward, params, inflow)
    grads, input_grad = pullback(cotangent.astype(jnp.float32).reshape(N_DP, CAP, D))
    return (result.reshape(N_DP * CAP, D).astype(jnp.bfloat16), input_grad.reshape(N_DP * CAP, D).astype(jnp.bfloat16), grads[0], grads[1], grads[2], grads[3], grads[4], grads[5], grads[6], grads[7], grads[8], grads[9], grads[10], grads[11])
```

```python
import jax
import jax.numpy as jnp
from jax import lax
from jax.sharding import PartitionSpec as P

HD = 64
TILE = 128
EPSILON = 1e-05
NEGATIVE = -1e30
BF = jnp.bfloat16
F32 = jnp.float32
CORE_PAIRS = ((0, 1), (1, 0), (2, 3), (3, 2))
CHIP_PAIRS = ((0, 2), (2, 0), (1, 3), (3, 1))


def dot(left, right, left_dim, right_dim):
    return lax.dot_general(
        left, right, (((left_dim,), (right_dim,)), ((), ())), preferred_element_type=F32
    )


def swap_core(value):
    return lax.ppermute(value, "mp", CORE_PAIRS)


def swap_chip(value):
    return lax.ppermute(value, "mp", CHIP_PAIRS)


def swap_bit(value, bit):
    return lax.ppermute(value, "dp", [(i, i ^ (1 << bit)) for i in range(8)])


def ordered(flag, own, other, axis):
    return jnp.where(
        flag == 0,
        jnp.stack([own, other], axis),
        jnp.stack([other, own], axis),
    )


def bits_of(index):
    return [(index >> b) & 1 for b in range(3)]


def gather_rows(message, index, count):
    if count != 8:
        return lax.all_gather(message, "dp", axis=0)
    low, mid, high = bits_of(index)
    rows, columns = message.shape
    both = ordered(high, message, swap_bit(message, 2), 0)
    half = columns // 2
    first, second = both[:, :, :half], both[:, :, half:]
    first = ordered(mid, first, swap_bit(first, 1), 1)
    second = ordered(low, second, swap_bit(second, 0), 1)
    first = ordered(low, first, swap_bit(first, 0), 2)
    second = ordered(mid, second, swap_bit(second, 1), 1)
    full = jnp.concatenate([first, second], -1)
    return full.reshape(8, rows, columns)


def take_bit(value, flag, axis):
    return lax.dynamic_index_in_dim(value, flag, axis, keepdims=False)


def exchange_add(value, flag, bit, axis):
    sent = take_bit(value, 1 - flag, axis).astype(BF)
    kept = take_bit(value, flag, axis).astype(F32)
    return kept + swap_bit(sent, bit).astype(F32)


def scatter_rows(value, index, count):
    if count != 8:
        return lax.psum_scatter(value, "dp", scatter_dimension=0, tiled=True)
    low, mid, high = bits_of(index)
    rows, columns = value.shape
    value = value.reshape(2, 2, 2, rows // 8, columns)
    half = columns // 2
    first, second = value[..., :half], value[..., half:]
    first = exchange_add(first, low, 0, 2).astype(BF)
    second = exchange_add(second, mid, 1, 1).astype(BF)
    first = exchange_add(first, mid, 1, 1).astype(BF)
    second = exchange_add(second, low, 0, 1).astype(BF)
    both = jnp.concatenate([first, second], -1)
    return exchange_add(both, high, 2, 0)


def sum_tile(tile, count):
    if count != 8:
        return lax.psum(tile, "dp")
    for bit in range(3):
        low = tile.astype(BF)
        tile = low.astype(F32) + swap_bit(low, bit).astype(F32)
    return tile


def norm_forward(value, gain, shift):
    average = jnp.mean(value, -1, keepdims=True)
    centred = value - average
    spread = jnp.mean(centred * centred, -1, keepdims=True)
    factor = lax.rsqrt(spread + EPSILON)
    scaled = centred * factor
    return (scaled * gain + shift, scaled, factor)


def norm_backward(incoming, scaled, factor, gain):
    weighted = incoming * gain
    first_mean = jnp.mean(weighted, -1, keepdims=True)
    second_mean = jnp.mean(weighted * scaled, -1, keepdims=True)
    return factor * (weighted - first_mean - scaled * second_mean)


def own_rows(value, core):
    rows = value.shape[0]
    parts = value.reshape((rows // (2 * TILE), 2, TILE) + value.shape[1:])
    return lax.dynamic_index_in_dim(parts, core, 1, keepdims=False).reshape(
        (rows // 2,) + value.shape[1:]
    )


def all_rows(own, core):
    rows, width = own.shape
    mine = own.reshape(rows // TILE, TILE, width)
    other = swap_core(own).reshape(rows // TILE, TILE, width)
    return ordered(core, mine, other, 1).reshape(2 * rows, width)


def gelu_parts(value):
    inner = 0.7978845608028654 * (value + 0.044715 * value * value * value)
    bend = jnp.tanh(inner)
    active = 0.5 * value * (1.0 + bend)
    slope = 0.5 * (1.0 + bend) + 0.5 * value * (1.0 - bend * bend) * 0.7978845608028654 * (
        1.0 + 3 * 0.044715 * value * value
    )
    return active, slope


def body(
    inputs,
    segments,
    norm1_gain,
    norm1_shift,
    qkv_weight,
    qv_bias,
    attn_weight,
    attn_bias,
    norm2_gain,
    norm2_shift,
    fc_weight,
    fc_bias,
    proj_weight,
    proj_bias,
    cotangent,
):
    count = lax.axis_size("dp")
    index = lax.axis_index("dp")
    shard = lax.axis_index("mp")
    core = shard % 2
    rows, depth = inputs.shape
    local = depth // count
    width = qkv_weight.shape[2]
    heads = width // HD
    units = fc_weight.shape[1]

    bias_width = qv_bias.shape[1]
    bias_rows = lax.dynamic_update_slice(
        jnp.zeros((heads, 2 * HD), BF), qv_bias, (0, index * bias_width)
    )
    bias_row = bias_rows.reshape(heads, 2, HD).transpose(1, 0, 2).reshape(1, 2 * width)
    vectors = jnp.stack(
        [norm1_gain, norm1_shift, attn_bias, norm2_gain, norm2_shift, fc_bias[0], proj_bias]
    )
    placed = lax.dynamic_update_slice(
        jnp.zeros((vectors.shape[0], depth), BF), vectors, (0, index * local)
    )
    tile = jnp.concatenate([placed, jnp.pad(bias_row, ((0, 0), (0, depth - 2 * width)))], 0)
    message_a = jnp.concatenate(
        [
            jnp.concatenate(
                [qkv_weight.transpose(1, 0, 2).reshape(local, 3 * width), attn_weight.T], 1
            ),
            tile,
        ],
        0,
    )
    gathered_a = gather_rows(message_a, index, count)
    message_b, message_c = lax.optimization_barrier((fc_weight, proj_weight.T, message_a))[:2]
    gathered_b = gather_rows(message_b, index, count).reshape(depth, units)
    gathered_c = gather_rows(message_c, index, count).reshape(depth, units)
    both_a = ordered(core, gathered_a, swap_core(gathered_a), 0)
    both_b = ordered(core, gathered_b, swap_core(gathered_b), 1)
    both_c = ordered(core, gathered_c, swap_core(gathered_c), 1)
    fc_full = both_b.reshape(depth, 2 * units)
    proj_full = both_c.reshape(depth, 2 * units)
    mats = both_a[:, :, :local].reshape(2, depth, 4, width)
    mats = mats.transpose(2, 1, 0, 3).reshape(4, depth, 2 * width)
    tiles = jnp.sum(both_a[:, :, local:].astype(F32), 1)
    gain_one, shift_one, bias_attn, gain_two, shift_two = [tiles[0, i] for i in range(5)]
    bias_fc = tiles[:, 5].reshape(-1)
    bias_proj = tiles[0, 6]
    bias_q = tiles[:, 7, :width].reshape(-1)
    bias_v = tiles[:, 7, width : 2 * width].reshape(-1)
    width2 = 2 * width
    heads2 = 2 * heads

    inflow = inputs.astype(F32)
    normed_one, _, _ = norm_forward(inflow, gain_one, shift_one)
    first_all = normed_one.astype(BF)
    first_low = own_rows(first_all, core)
    query = (dot(first_low, mats[0], 1, 0) + bias_q).astype(BF)
    key = dot(first_all, mats[1], 1, 0).astype(BF)
    value = (dot(first_all, mats[2], 1, 0) + bias_v).astype(BF)
    own_count = rows // 2
    seg_own = own_rows(segments, core)
    place = jnp.arange(rows)
    place_own = own_rows(place, core)
    query_h = query.reshape(own_count, heads2, HD)
    key_h = key.reshape(rows, heads2, HD)
    value_h = value.reshape(rows, heads2, HD)
    scale = float(HD) ** -0.5
    probs_list = []
    mixed_parts = []
    for j in range(own_count // TILE):
        rs = slice(j * TILE, (j + 1) * TILE)
        end = (j + 1) * 2 * TILE
        allowed = (seg_own[rs, None] == segments[None, :end]) & (
            place[None, :end] <= place_own[rs, None]
        )
        scores = (
            jnp.einsum("qhd,khd->hqk", query_h[rs], key_h[:end], preferred_element_type=F32)
            * scale
        )
        scores = jnp.where(allowed[None], scores, NEGATIVE)
        weights = jnp.exp(scores - jnp.max(scores, -1, keepdims=True))
        probs = (weights / jnp.sum(weights, -1, keepdims=True)).astype(BF)
        probs_list.append(probs)
        mixed_parts.append(
            jnp.einsum("hqk,khd->qhd", probs, value_h[:end], preferred_element_type=F32)
        )
    mixed = jnp.concatenate(mixed_parts, 0).reshape(own_count, width2).astype(BF)
    partial = dot(mixed, mats[3], 1, 1).astype(BF)
    branch = partial.astype(F32) + swap_chip(partial).astype(F32)
    inflow_own = own_rows(inputs, core).astype(F32)
    middle = inflow_own + branch + bias_attn
    normed_two, scaled_two, factor_two = norm_forward(middle, gain_two, shift_two)
    second_low = normed_two.astype(BF)
    hidden = dot(second_low, fc_full, 1, 0) + bias_fc
    active_float, slope = gelu_parts(hidden)
    active = active_float.astype(BF)
    live = (seg_own >= 0)[:, None]
    grad_low = jnp.where(live, own_rows(cotangent, core), jnp.zeros((), BF))
    grad_float = grad_low.astype(F32)
    active_grad = dot(grad_low, proj_full, 1, 0)
    hidden_grad = (active_grad * slope).astype(BF)
    second_part = dot(hidden_grad, fc_full, 1, 1).astype(BF)
    second_grad = second_part.astype(F32) + swap_chip(second_part).astype(F32)

    mlp_part = dot(active, proj_full, 1, 1).astype(BF)
    final = middle + (mlp_part.astype(F32) + swap_chip(mlp_part).astype(F32)) + bias_proj
    outputs = all_rows(jnp.where(live, final, 0.0).astype(BF), core)

    fc_grad = dot(second_low, hidden_grad, 0, 0)
    proj_grad = dot(grad_low, active, 0, 0)
    big = jnp.stack([fc_grad.reshape(depth, 2, units), proj_grad.reshape(depth, 2, units)], 2)
    sent = take_bit(big, 1 - core, 1).astype(BF)
    big = take_bit(big, core, 1) + swap_core(sent).astype(F32)
    big = scatter_rows(big.astype(BF).reshape(depth, 2 * units), index, count).astype(F32)
    fc_weight_grad = big[:, :units]
    proj_weight_grad = big[:, units:].T

    gain_two_sum = jnp.sum(second_grad * scaled_two, 0)
    shift_two_sum = jnp.sum(second_grad, 0)
    middle_grad = grad_float + norm_backward(second_grad, scaled_two, factor_two, gain_two)
    branch_low = middle_grad.astype(BF)
    attn_grad = dot(branch_low, mixed, 0, 0)
    mixed_grad = dot(branch_low, mats[3], 1, 0).astype(BF)
    mixed_grad_h = mixed_grad.reshape(own_count, heads2, HD)
    query_parts = []
    key_grad = jnp.zeros((rows, heads2, HD), F32)
    value_grad = jnp.zeros((rows, heads2, HD), F32)
    for j in range(own_count // TILE):
        rs = slice(j * TILE, (j + 1) * TILE)
        end = (j + 1) * 2 * TILE
        probs = probs_list[j]
        prob_grad = jnp.einsum(
            "qhd,khd->hqk", mixed_grad_h[rs], value_h[:end], preferred_element_type=F32
        )
        pf = probs.astype(F32)
        inner = jnp.sum(pf * prob_grad, -1, keepdims=True)
        score_grad = (pf * (prob_grad - inner)).astype(BF)
        query_parts.append(
            jnp.einsum("hqk,khd->qhd", score_grad, key_h[:end], preferred_element_type=F32) * scale
        )
        key_grad = key_grad.at[:end].add(
            jnp.einsum("hqk,qhd->khd", score_grad, query_h[rs], preferred_element_type=F32) * scale
        )
        value_grad = value_grad.at[:end].add(
            jnp.einsum("hqk,qhd->khd", probs, mixed_grad_h[rs], preferred_element_type=F32)
        )
    query_grad = jnp.concatenate(query_parts, 0).reshape(own_count, width2).astype(BF)
    both_grad = jnp.concatenate(
        [key_grad.reshape(rows, width2), value_grad.reshape(rows, width2)], 1
    )
    both_low = own_rows(both_grad, 1 - core).astype(BF)
    both_sum = (own_rows(both_grad, core) + swap_core(both_low).astype(F32)).astype(BF)
    key_low, value_low = both_sum[:, :width2], both_sum[:, width2:]
    first_part = (
        dot(query_grad, mats[0], 1, 1) + dot(key_low, mats[1], 1, 1) + dot(value_low, mats[2], 1, 1)
    ).astype(BF)
    first_grad = first_part.astype(F32) + swap_chip(first_part).astype(F32)
    _, scaled_one, factor_one = norm_forward(inflow_own, gain_one, shift_one)
    input_part = norm_backward(first_grad, scaled_one, factor_one, gain_one)
    inputs_grad = all_rows((middle_grad + input_part).astype(BF), core)

    grads = [dot(first_low, g, 0, 0) for g in (query_grad, key_low, value_low)] + [attn_grad]
    stacked = jnp.stack([g.reshape(depth, 2, width) for g in grads], 2)
    stacked = stacked.reshape(depth, 2, 4 * width)
    sent = take_bit(stacked, 1 - core, 1).astype(BF)
    mine = take_bit(stacked, core, 1) + swap_core(sent).astype(F32)
    mine = scatter_rows(mine.astype(BF), index, count).astype(F32)
    qkv_weight_grad = mine[:, : 3 * width].reshape(local, 3, width).transpose(1, 0, 2)
    attn_weight_grad = mine[:, 3 * width :].T

    def total(v):
        return jnp.sum(v.astype(F32), 0)

    common = [
        total(first_grad * scaled_one),
        total(first_grad),
        total(branch_low),
        gain_two_sum,
        shift_two_sum,
        total(grad_low),
    ]
    fc_sums = total(hidden_grad).reshape(2, units)
    q_sums = total(query_grad).reshape(2, width)
    v_sums = total(value_low).reshape(2, width)
    pad = jnp.zeros((depth - 2 * width,), F32)
    tiles = [
        jnp.stack(common + [fc_sums[s], jnp.concatenate([q_sums[s], v_sums[s], pad])])
        for s in range(2)
    ]
    tiles = jnp.stack(tiles)
    sent = take_bit(tiles, 1 - core, 0).astype(BF)
    tile = take_bit(tiles, core, 0) + swap_core(sent).astype(F32)
    tile = sum_tile(tile, count)
    part = lax.dynamic_slice(tile, (0, index * local), (7, local))
    bias_sum = tile[7, : 2 * width].reshape(2, heads, HD).transpose(1, 0, 2).reshape(heads, 2 * HD)
    qv_bias_grad = lax.dynamic_slice(bias_sum, (0, index * bias_width), (heads, bias_width))
    return (
        outputs,
        inputs_grad,
        part[0],
        part[1],
        qkv_weight_grad,
        qv_bias_grad,
        attn_weight_grad,
        part[2],
        part[3],
        part[4],
        fc_weight_grad,
        part[6][None],
        proj_weight_grad,
        part[5],
    )


def solution(mesh):
    return jax.shard_map(
        body,
        mesh=mesh,
        in_specs=(
            P("dp", None),
            P("dp"),
            P("dp"),
            P("dp"),
            P(None, "dp", "mp"),
            P("mp", "dp"),
            P("mp", "dp"),
            P("dp"),
            P("dp"),
            P("dp"),
            P("dp", "mp"),
            P("mp", "dp"),
            P("mp", "dp"),
            P("dp"),
            P("dp", None),
        ),
        out_specs=(
            P("dp", None),
            P("dp", None),
            P("dp"),
            P("dp"),
            P(None, "dp", "mp"),
            P("mp", "dp"),
            P("mp", "dp"),
            P("dp"),
            P("dp"),
            P("dp"),
            P("dp", "mp"),
            P("mp", "dp"),
            P("mp", "dp"),
            P("dp"),
        ),
        check_vma=False,
    )
```

```python
import functools

import jax
import jax.numpy as jnp
from jax import lax
from jax.experimental import pallas as pl
from jax.experimental.pallas import tpu as pltpu
from jax.sharding import PartitionSpec as P

HD = 64
TILE = 128
EXTRA = 16
CHUNKS = 8
EPSILON = 1e-05
NEGATIVE = -1e30
BF = jnp.bfloat16
F32 = jnp.float32
CORE_PAIRS = ((0, 1), (1, 0), (2, 3), (3, 2))
CHIP_PAIRS = ((0, 2), (2, 0), (1, 3), (3, 1))
CURVE = 0.7978845608028654


def dot(left, right, left_dim, right_dim):
    return lax.dot_general(
        left, right, (((left_dim,), (right_dim,)), ((), ())), preferred_element_type=F32
    )


def swap_core(value):
    return lax.ppermute(value, "mp", CORE_PAIRS)


def swap_chip(value):
    return lax.ppermute(value, "mp", CHIP_PAIRS)


def swap_bit(value, bit):
    return lax.ppermute(value, "dp", [(i, i ^ (1 << bit)) for i in range(CHUNKS)])


def call(kernel, outs, *args, scratch=(), smem=1, flops=0, name=None):
    specs = [pl.BlockSpec(memory_space=pltpu.SMEM)] * smem
    specs += [pl.BlockSpec(memory_space=pltpu.VMEM)] * (len(args) - smem)
    size = sum(a.size * a.dtype.itemsize for a in args)
    size += sum(o.size * jnp.dtype(o.dtype).itemsize for o in outs)
    return pl.pallas_call(
        kernel,
        out_shape=outs,
        in_specs=specs,
        out_specs=[pl.BlockSpec(memory_space=pltpu.VMEM)] * len(outs),
        scratch_shapes=list(scratch),
        compiler_params=pltpu.CompilerParams(vmem_limit_bytes=56 * 1024 * 1024),
        cost_estimate=pl.CostEstimate(flops=flops, bytes_accessed=size, transcendentals=0),
        name=name,
    )(*args)


def shape(dims, dtype=BF):
    return jax.ShapeDtypeStruct(tuple(dims), dtype)


def gather_blocks(message):
    got = {0: message}
    got[4] = swap_bit(message, 2)
    got[1] = swap_bit(message, 0)
    got[2] = swap_bit(message, 1)
    got[5] = swap_bit(got[4], 0)
    got[6] = swap_bit(got[4], 1)
    got[3] = swap_bit(got[2], 0)
    got[7] = swap_bit(got[5], 1)
    return jnp.stack([got[r] for r in range(CHUNKS)])


def loop(count, step, fn):
    def run(i, carry):
        fn(pl.multiple_of(i * step, step))
        return carry

    lax.fori_loop(0, count // step, run, 0)


def norm_stats(value):
    average = jnp.mean(value, -1, keepdims=True)
    centred = value - average
    spread = jnp.mean(centred * centred, -1, keepdims=True)
    factor = lax.rsqrt(spread + EPSILON)
    return centred * factor, factor


def norm_backward(incoming, scaled, factor, gain):
    weighted = incoming * gain
    first_mean = jnp.mean(weighted, -1, keepdims=True)
    second_mean = jnp.mean(weighted * scaled, -1, keepdims=True)
    return factor * (weighted - first_mean - scaled * second_mean)


def tile_sum(ref, base):
    total = ref[0, base : base + EXTRA, :].astype(F32)
    for r in range(1, CHUNKS):
        total = total + ref[r, base : base + EXTRA, :].astype(F32)
    return total


def own_start(start, core):
    tile = start // TILE
    return pl.multiple_of((2 * tile + core) * TILE + start % TILE, 32)


def colsum(value):
    return jnp.sum(value, 0, keepdims=True)


def norm_kernel(info, x_ref, w_ref, low_ref, vec_ref):
    base = w_ref.shape[1] - EXTRA
    vec_ref[...] = tile_sum(w_ref, base)
    gain, shift = vec_ref[0:1, :], vec_ref[1:2, :]

    def run(at):
        scaled, _ = norm_stats(x_ref[pl.ds(at, 32), :].astype(F32))
        low_ref[pl.ds(at, 32), :] = (scaled * gain + shift).astype(BF)

    loop(x_ref.shape[0], 32, run)


def attend_kernel(
    info,
    low_ref,
    own_ref,
    sib_ref,
    seg_ref,
    part_ref,
    mixed_ref,
    q_ref,
    k_ref,
    v_ref,
    probs_ref,
    wq_ref,
    wk_ref,
    wv_ref,
    wo_ref,
    firstown_ref,
    proj_ref,
    s_ref,
    o_ref,
):
    flip, core = info[0], info[1]
    width = own_ref.shape[2] // 4
    base = own_ref.shape[1] - EXTRA
    rows = low_ref.shape[0]
    heads = 2 * width // HD
    own_count = rows // 2
    for r in range(CHUNKS):
        at = pl.multiple_of((r ^ flip) * base, 32)
        for side, ref in ((0, own_ref), (1, sib_ref)):
            for part, out in enumerate((wq_ref, wk_ref, wv_ref, wo_ref)):
                out[pl.ds(at, base), side * width : (side + 1) * width] = ref[
                    r, 0:base, part * width : (part + 1) * width
                ]
    vec_own = tile_sum(own_ref, base)
    vec_sib = tile_sum(sib_ref, base)
    bias_q = jnp.concatenate([vec_own[7:8, :width], vec_sib[7:8, :width]], 1)
    bias_v = jnp.concatenate(
        [vec_own[7:8, width : 2 * width], vec_sib[7:8, width : 2 * width]], 1
    )
    for j in range(own_count // TILE):
        at = own_start(j * TILE, core)
        firstown_ref[j * TILE : (j + 1) * TILE, :] = low_ref[pl.ds(at, TILE), :]
    scale = float(HD) ** -0.5
    proj_ref[0:own_count, :] = dot(firstown_ref[...], wq_ref[...], 1, 0) + bias_q
    for h in range(heads):
        q_ref[h] = (
            proj_ref[0:own_count, h * HD : (h + 1) * HD].astype(BF).astype(F32) * scale
        ).astype(BF)
    proj_ref[...] = dot(low_ref[...], wk_ref[...], 1, 0)
    for h in range(heads):
        k_ref[h] = proj_ref[:, h * HD : (h + 1) * HD].astype(BF)
    proj_ref[...] = dot(low_ref[...], wv_ref[...], 1, 0) + bias_v
    for h in range(heads):
        v_ref[h] = proj_ref[:, h * HD : (h + 1) * HD].astype(BF)
    lane = lax.broadcasted_iota(jnp.int32, (TILE, TILE), 1)
    line = lax.broadcasted_iota(jnp.int32, (TILE, TILE), 0)
    for j in range(own_count // TILE):
        end = (j + 1) * 2 * TILE
        off = TILE * j * (j + 1)
        at = own_start(j * TILE, core)
        seg_tile = jnp.broadcast_to(seg_ref[0:1, pl.ds(at, TILE)], (TILE, TILE))
        seg_col = jnp.max(jnp.where(lane == line, seg_tile, -2), -1, keepdims=True)
        place = lax.broadcasted_iota(jnp.int32, (TILE, end), 1)
        own_place = at + lax.broadcasted_iota(jnp.int32, (TILE, end), 0)
        allowed = (seg_col == seg_ref[0:1, 0:end]) & (place <= own_place)
        bias = jnp.where(allowed, 0.0, NEGATIVE)
        s_ref[heads, :, 0:end] = bias

        def run(h, carry, j=j, end=end, off=off):
            scores = dot(q_ref[h, j * TILE : (j + 1) * TILE, :], k_ref[h, 0:end, :], 1, 1)
            s_ref[0, :, 0:end] = scores
            for sub in range(4):
                sl = slice(sub * 32, sub * 32 + 32)
                sc = s_ref[0, sl, 0:end] + s_ref[heads, sl, 0:end]
                weights = jnp.exp(sc - jnp.max(sc, -1, keepdims=True))
                inverse = 1.0 / jnp.sum(weights, -1, keepdims=True)
                probs_ref[h, sl, off : off + end] = (weights * inverse).astype(BF)
            o_ref[h, j * TILE : (j + 1) * TILE, :] = dot(
                probs_ref[h, :, off : off + end], v_ref[h, 0:end, :], 1, 0
            )
            return carry

        lax.fori_loop(0, heads, run, 0)
    for h in range(heads):
        mixed_ref[:, h * HD : (h + 1) * HD] = o_ref[h].astype(BF)
    part_ref[...] = dot(mixed_ref[...], wo_ref[...], 1, 1).astype(BF)


def mlp_kernel(
    info,
    x_ref,
    seg_ref,
    cot_ref,
    part_ref,
    recv_ref,
    vec_ref,
    vecsib_ref,
    own_ref,
    sib_ref,
    da_ref,
    act_ref,
    dhid_ref,
    second_ref,
    dy_ref,
    mid_ref,
    fc_ref,
    proj_ref,
    hid_ref,
    dact_ref,
):
    flip, core = info[0], info[1]
    own_count = part_ref.shape[0]
    base = own_ref.shape[1]
    units = own_ref.shape[2] // 2
    for r in range(CHUNKS):
        at = pl.multiple_of((r ^ flip) * base, 32)
        for side, ref in ((0, own_ref), (1, sib_ref)):
            cols = slice(side * units, (side + 1) * units)
            fc_ref[pl.ds(at, base), cols] = ref[r, :, 0:units]
            proj_ref[pl.ds(at, base), cols] = ref[r, :, units : 2 * units]
    gain, shift, bias = vec_ref[3:4, :], vec_ref[4:5, :], vec_ref[2:3, :]
    sub = 32
    lane = lax.broadcasted_iota(jnp.int32, (sub, TILE), 1)
    line = lax.broadcasted_iota(jnp.int32, (sub, TILE), 0)

    def first(at):
        src = own_start(at, core)
        tile_at = pl.multiple_of((2 * (at // TILE) + core) * TILE, TILE)
        seg_tile = jnp.broadcast_to(seg_ref[0:1, pl.ds(tile_at, TILE)], (sub, TILE))
        seg_col = jnp.max(
            jnp.where(lane == line + at % TILE, seg_tile, -2), -1, keepdims=True
        )
        rows = pl.ds(at, sub)
        cot = cot_ref[pl.ds(src, sub), :].astype(F32)
        dy_ref[rows, :] = jnp.where(seg_col >= 0, cot, 0.0).astype(BF)
        middle = (
            x_ref[pl.ds(src, sub), :].astype(F32)
            + (part_ref[rows, :].astype(F32) + recv_ref[rows, :].astype(F32))
            + bias
        )
        mid_ref[rows, :] = middle
        scaled, _ = norm_stats(middle)
        second_ref[rows, :] = (scaled * gain + shift).astype(BF)

    loop(own_count, sub, first)
    step = 512
    for c in range(2 * units // step):
        cols = slice(c * step, (c + 1) * step)
        hid_ref[...] = dot(second_ref[...], fc_ref[:, cols], 1, 0)
        dact_ref[...] = dot(dy_ref[...], proj_ref[:, cols], 1, 0)
        left, right = c * step, (c + 1) * step
        pieces = []
        if left < units:
            pieces.append(vec_ref[5:6, left : min(right, units)])
        if right > units:
            pieces.append(vecsib_ref[5:6, max(left, units) - units : right - units])
        bias_fc = jnp.concatenate(pieces, 1) if len(pieces) > 1 else pieces[0]

        def gelu(at, cols=cols, bias_fc=bias_fc):
            rows = pl.ds(at, 16)
            u = hid_ref[rows, :] + bias_fc
            u2 = u * u
            bend = jnp.tanh(CURVE * u * (1.0 + 0.044715 * u2))
            half = 0.5 * (1.0 + bend)
            act_ref[rows, cols] = (u * half).astype(BF)
            slope = half + (0.5 * CURVE) * u * (1.0 - bend * bend) * (1.0 + 0.134145 * u2)
            dhid_ref[rows, cols] = (dact_ref[rows, :] * slope).astype(BF)

        loop(own_count, 16, gelu)
    da_ref[...] = dot(dhid_ref[...], fc_ref[...], 1, 1).astype(BF)


def mlp_out_kernel(info, act_ref, own_ref, sib_ref, part_ref, proj_ref):
    flip = info[0]
    base = own_ref.shape[1]
    units = own_ref.shape[2] // 2
    for r in range(CHUNKS):
        at = pl.multiple_of((r ^ flip) * base, 32)
        proj_ref[pl.ds(at, base), 0:units] = own_ref[r, :, units : 2 * units]
        proj_ref[pl.ds(at, base), units : 2 * units] = sib_ref[r, :, units : 2 * units]
    part_ref[...] = dot(act_ref[...], proj_ref[...], 1, 1).astype(BF)


def mlp_grad_kernel(
    info, act_ref, dhid_ref, second_ref, dy_ref, own_ref, sib_ref, sums_ref, acc_ref
):
    flip = info[0]
    base = own_ref.shape[1]
    units = own_ref.shape[2] // 2
    for kind, left, right in ((0, second_ref, dhid_ref), (1, dy_ref, act_ref)):
        for side, out in ((0, own_ref), (1, sib_ref)):
            acc_ref[...] = dot(left[...], right[:, side * units : (side + 1) * units], 0, 0)
            for b in range(CHUNKS):
                out[b ^ flip, :, kind * units : (kind + 1) * units] = acc_ref[
                    b * base : (b + 1) * base, :
                ].astype(BF)
    one = jnp.ones((8, act_ref.shape[0]), BF)
    fc_sums = dot(one, dhid_ref[...], 1, 0)
    sums_ref[0:8, :] = fc_sums[:, 0:units]
    sums_ref[8:16, :] = fc_sums[:, units : 2 * units]
    sums_ref[16:24, :] = dot(one, dy_ref[...], 1, 0)


def attend_back_kernel(
    info,
    mid_ref,
    dy_ref,
    da_ref,
    recv_ref,
    vec_ref,
    wo_ref,
    mixed_ref,
    q_ref,
    k_ref,
    v_ref,
    probs_ref,
    dmid_ref,
    branch_ref,
    sums_ref,
    dq_ref,
    keep_ref,
    send_ref,
    dm_ref,
    do_ref,
    dkt_ref,
    dvt_ref,
    dqh_ref,
    dp_ref,
    ds_ref,
    delta_ref,
):
    core = info[1]
    own_count = mid_ref.shape[0]
    heads = q_ref.shape[0]
    rows = k_ref.shape[1]
    gain = vec_ref[3:4, :]
    sums_ref[...] = jnp.zeros_like(sums_ref)
    sub = 32

    def first(at):
        rs = pl.ds(at, sub)
        scaled, factor = norm_stats(mid_ref[rs, :])
        incoming = da_ref[rs, :].astype(F32) + recv_ref[rs, :].astype(F32)
        dmid = dy_ref[rs, :].astype(F32) + norm_backward(incoming, scaled, factor, gain)
        dmid_ref[rs, :] = dmid
        low = dmid.astype(BF)
        branch_ref[rs, :] = low
        sums_ref[2:3, :] += colsum(low.astype(F32))
        sums_ref[3:4, :] += colsum(incoming * scaled)
        sums_ref[4:5, :] += colsum(incoming)

    loop(own_count, sub, first)
    dm_ref[...] = dot(branch_ref[...], wo_ref[...], 1, 0).astype(BF)
    for h in range(heads):
        cols = slice(h * HD, (h + 1) * HD)
        do_ref[h] = dm_ref[:, cols]
        delta_ref[h] = jnp.broadcast_to(
            jnp.sum(
                dm_ref[:, cols].astype(F32) * mixed_ref[:, cols].astype(F32), -1, keepdims=True
            ),
            (own_count, TILE),
        )
    scale = float(HD) ** -0.5

    def head(h, carry):
        for j in reversed(range(own_count // TILE)):
            end = (j + 1) * 2 * TILE
            off = TILE * j * (j + 1)
            rs = slice(j * TILE, (j + 1) * TILE)
            dp_ref[:, 0:end] = dot(do_ref[h, rs, :], v_ref[h, 0:end, :], 1, 1)
            for s in range(4):
                sl = slice(s * 32, s * 32 + 32)
                delta = delta_ref[h, j * TILE + s * 32 : j * TILE + s * 32 + 32, 0:1]
                p = probs_ref[h, sl, off : off + end].astype(F32)
                ds_ref[sl, 0:end] = (p * (dp_ref[sl, 0:end] - delta)).astype(BF)
            ds = ds_ref[:, 0:end]
            dqh_ref[h, rs, :] = dot(ds, k_ref[h, 0:end, :], 1, 0) * scale
            dk = dot(q_ref[h, rs, :], ds, 0, 0)
            dv = dot(do_ref[h, rs, :], probs_ref[h, :, off : off + end], 0, 0)
            if j == own_count // TILE - 1:
                dkt_ref[h] = dk
                dvt_ref[h] = dv
            else:
                dkt_ref[h, :, 0:end] += dk
                dvt_ref[h, :, 0:end] += dv
        return carry

    lax.fori_loop(0, heads, head, 0)
    width2 = heads * HD
    for h in range(heads):
        dq_ref[:, h * HD : (h + 1) * HD] = dqh_ref[h].astype(BF)
        twin = (h + heads // 2) % heads
        for j in range(own_count // TILE):
            mine = pl.multiple_of((2 * j + core) * TILE, TILE)
            yours = pl.multiple_of((2 * j + 1 - core) * TILE, TILE)
            cols = slice(j * TILE, (j + 1) * TILE)
            for part, ref in ((0, dkt_ref), (1, dvt_ref)):
                at = part * width2
                keep_ref[at + h * HD : at + (h + 1) * HD, cols] = ref[h, :, pl.ds(mine, TILE)]
                send_ref[at + twin * HD : at + (twin + 1) * HD, cols] = ref[
                    h, :, pl.ds(yours, TILE)
                ].astype(BF)


def attn_grad_kernel(info, branch_ref, mixed_ref, out_ref):
    out_ref[...] = dot(branch_ref[...], mixed_ref[...], 0, 0)


def first_grad_kernel(
    info, dq_ref, keep_ref, got_ref, wq_ref, wk_ref, wv_ref, part_ref, dkv_ref
):
    width2 = dq_ref.shape[1]
    dkv_ref[...] = (keep_ref[...] + got_ref[...].astype(F32)).astype(BF)
    part_ref[...] = (
        dot(dq_ref[...], wq_ref[...], 1, 1)
        + dot(dkv_ref[0:width2, :], wk_ref[...], 0, 1)
        + dot(dkv_ref[width2 : 2 * width2, :], wv_ref[...], 0, 1)
    ).astype(BF)


def qkv_grad_kernel(
    info,
    first_ref,
    dq_ref,
    dkv_ref,
    attn_ref,
    part_ref,
    x_ref,
    mlp_sums_ref,
    att_sums_ref,
    own_ref,
    sib_ref,
    tile_own_ref,
    tile_sib_ref,
    sum_ref,
):
    flip, core = info[0], info[1]
    width2 = dq_ref.shape[1]
    width = width2 // 2
    base = own_ref.shape[1]
    for part in range(4):
        if part == 0:
            whole = dot(first_ref[...], dq_ref[...], 0, 0)
        elif part == 3:
            whole = attn_ref[...]
        else:
            whole = dot(
                first_ref[...], dkv_ref[(part - 1) * width2 : part * width2, :], 0, 1
            )
        for b in range(CHUNKS):
            rows = slice(b * base, (b + 1) * base)
            cols = slice(part * width, (part + 1) * width)
            own_ref[b ^ flip, :, cols] = whole[rows, 0:width].astype(BF)
            sib_ref[b ^ flip, :, cols] = whole[rows, width:width2].astype(BF)
    sum_ref[...] = jnp.zeros_like(sum_ref)

    def run(at):
        src = own_start(at, core)
        scaled, _ = norm_stats(x_ref[pl.ds(src, 32), :].astype(F32))
        incoming = part_ref[pl.ds(at, 32), :].astype(F32)
        sum_ref[0:1, :] += colsum(incoming * scaled)
        sum_ref[1:2, :] += colsum(incoming)

    loop(part_ref.shape[0], 32, run)
    ones = jnp.ones((8, dq_ref.shape[0]), BF)
    qs = dot(ones, dq_ref[...], 1, 0)[0:1, :]
    vs = dot(ones, dkv_ref[width2 : 2 * width2, :], 1, 1)[0:1, :]
    sum_ref[2:5, :] = att_sums_ref[2:5, :]
    sum_ref[6:7, :] = mlp_sums_ref[16:17, :]
    for side, out in ((0, tile_own_ref), (1, tile_sib_ref)):
        sl = slice(side * width, (side + 1) * width)
        sum_ref[5:6, :] = mlp_sums_ref[8 * side : 8 * side + 1, :]
        sum_ref[7:8, 0:width] = qs[:, sl]
        sum_ref[7:8, width : 2 * width] = vs[:, sl]
        out[...] = sum_ref[...].astype(BF)


def final_kernel(info, x_ref, part_ref, recv_ref, dmid_ref, vec_ref, out_ref):
    core = info[1]
    gain = vec_ref[0:1, :]

    def run(at):
        src = own_start(at, core)
        rs = pl.ds(at, 32)
        scaled, factor = norm_stats(x_ref[pl.ds(src, 32), :].astype(F32))
        incoming = part_ref[rs, :].astype(F32) + recv_ref[rs, :].astype(F32)
        out_ref[rs, :] = (
            dmid_ref[rs, :] + norm_backward(incoming, scaled, factor, gain)
        ).astype(BF)

    loop(part_ref.shape[0], 32, run)


def output_kernel(info, seg_ref, mid_ref, part_ref, recv_ref, vec_ref, out_ref):
    core = info[1]
    bias = vec_ref[6:7, :]
    sub = 32
    lane = lax.broadcasted_iota(jnp.int32, (sub, TILE), 1)
    line = lax.broadcasted_iota(jnp.int32, (sub, TILE), 0)

    def run(at):
        tile_at = pl.multiple_of((2 * (at // TILE) + core) * TILE, TILE)
        seg_tile = jnp.broadcast_to(seg_ref[0:1, pl.ds(tile_at, TILE)], (sub, TILE))
        seg_col = jnp.max(
            jnp.where(lane == line + at % TILE, seg_tile, -2), -1, keepdims=True
        )
        rs = pl.ds(at, sub)
        final = (
            mid_ref[rs, :]
            + (part_ref[rs, :].astype(F32) + recv_ref[rs, :].astype(F32))
            + bias
        )
        out_ref[rs, :] = jnp.where(seg_col >= 0, final, 0.0).astype(BF)

    loop(part_ref.shape[0], sub, run)


def merge_kernel(info, own_ref, got_ref, out_ref):
    core = info[1]
    for j in range(own_ref.shape[0] // TILE):
        sl = slice(j * TILE, (j + 1) * TILE)
        mine = pl.multiple_of((2 * j + core) * TILE, TILE)
        yours = pl.multiple_of((2 * j + 1 - core) * TILE, TILE)
        out_ref[pl.ds(mine, TILE), :] = own_ref[sl, :]
        out_ref[pl.ds(yours, TILE), :] = got_ref[sl, :]


def all_rows(info, own):
    return call(
        merge_kernel,
        [shape((2 * own.shape[0], own.shape[1]))],
        info,
        own,
        swap_core(own),
        name="merge",
    )[0]


def scatter_first_kernel(info, own_ref, got_ref, *refs):
    tiles, (keep_a, send_a, keep_b, send_b) = refs[:-4], refs[-4:]
    base = own_ref.shape[1]
    half = own_ref.shape[2] // 2
    for keep, send, bit, at in ((keep_a, send_a, 0, 0), (keep_b, send_b, 1, half)):
        cols = slice(at, at + half)
        kept, sent = 0, 0
        for r in range(CHUNKS):
            value = own_ref[r, :, cols].astype(F32) + got_ref[r, :, cols].astype(F32)
            if (r >> bit) & 1:
                send[sent * base : (sent + 1) * base, :] = value.astype(BF)
                sent += 1
            else:
                keep[kept * base : (kept + 1) * base, :] = value
                kept += 1
        if tiles:
            value = tiles[0][:, cols].astype(F32) + tiles[1][:, cols].astype(F32)
            value = value + tiles[2][:, cols].astype(F32)
            send[4 * base : 4 * base + EXTRA, :] = value.astype(BF)
            keep[4 * base : 4 * base + EXTRA, :] = value


def scatter_second_kernel(
    tiled, info, keep_a, got_a, keep_b, got_b, next_a, send_a, next_b, send_b
):
    extra = EXTRA if tiled else 0
    base = (keep_a.shape[0] - extra) // 4
    for keep, got, left, send, order in (
        (keep_a, got_a, next_a, send_a, (0, 1, 0, 1)),
        (keep_b, got_b, next_b, send_b, (0, 1, 0, 1)),
    ):
        kept, sent = 0, 0
        for r in range(4):
            rows = slice(r * base, (r + 1) * base)
            value = keep[rows, :] + got[rows, :].astype(F32)
            if order[r]:
                send[sent * base : (sent + 1) * base, :] = value.astype(BF)
                sent += 1
            else:
                left[kept * base : (kept + 1) * base, :] = value
                kept += 1
        if tiled:
            low = keep[4 * base : 4 * base + extra, :].astype(BF).astype(F32)
            value = low + got[4 * base : 4 * base + extra, :].astype(F32)
            send[2 * base : 2 * base + extra, :] = value.astype(BF)
            left[2 * base : 2 * base + extra, :] = value


def scatter_third_kernel(tiled, info, keep_a, got_a, keep_b, got_b, left, send):
    extra = EXTRA if tiled else 0
    base = (keep_a.shape[0] - extra) // 2
    half = keep_a.shape[1]
    for keep, got, at in ((keep_a, got_a, 0), (keep_b, got_b, half)):
        cols = slice(at, at + half)
        left[0:base, cols] = keep[0:base, :] + got[0:base, :].astype(F32)
        send[0:base, cols] = (
            keep[base : 2 * base, :] + got[base : 2 * base, :].astype(F32)
        ).astype(BF)
        if tiled:
            rows = slice(2 * base, 2 * base + extra)
            value = keep[rows, :].astype(BF).astype(F32) + got[rows, :].astype(F32)
            left[base : base + extra, cols] = value
            send[base : base + extra, cols] = value.astype(BF)


def scatter_last_kernel(tiled, info, left, got, out):
    extra = EXTRA if tiled else 0
    base = left.shape[0] - extra
    out[0:base, :] = left[0:base, :] + got[0:base, :].astype(F32)
    if tiled:
        rows = slice(base, base + extra)
        out[rows, :] = left[rows, :].astype(BF).astype(F32) + got[rows, :].astype(F32)


def scatter_blocks(info, own, sib, count, tiles=None):
    got = swap_core(sib)
    base, columns = own.shape[1:]
    tiled = tiles is not None
    extra = EXTRA if tiled else 0
    if count != CHUNKS:
        total = own.astype(F32) + got.astype(F32)
        total = lax.psum_scatter(
            total.reshape(CHUNKS * base, columns), "dp", scatter_dimension=0, tiled=True
        )
        if not tiled:
            return total, None
        return total, lax.psum(sum(t.astype(F32) for t in tiles), "dp")
    half = columns // 2
    rows = 4 * base + extra
    keep_a, send_a, keep_b, send_b = call(
        scatter_first_kernel,
        [shape((rows, half), F32), shape((rows, half))] * 2,
        info,
        own,
        got,
        *(tiles or ()),
        name="scatter_first",
    )
    rows = 2 * base + extra
    keep_a, send_a, keep_b, send_b = call(
        functools.partial(scatter_second_kernel, tiled),
        [shape((rows, half), F32), shape((rows, half))] * 2,
        info,
        keep_a,
        swap_bit(send_a, 0),
        keep_b,
        swap_bit(send_b, 1),
        name="scatter_second",
    )
    rows = base + extra
    left, send = call(
        functools.partial(scatter_third_kernel, tiled),
        [shape((rows, columns), F32), shape((rows, columns))],
        info,
        keep_a,
        swap_bit(send_a, 1),
        keep_b,
        swap_bit(send_b, 0),
        name="scatter_third",
    )
    out = call(
        functools.partial(scatter_last_kernel, tiled),
        [shape((rows, columns), F32)],
        info,
        left,
        swap_bit(send, 2),
        name="scatter_last",
    )[0]
    return out[:base], (out[base:] if tiled else None)


def body(
    inputs,
    segments,
    norm1_gain,
    norm1_shift,
    qkv_weight,
    qv_bias,
    attn_weight,
    attn_bias,
    norm2_gain,
    norm2_shift,
    fc_weight,
    fc_bias,
    proj_weight,
    proj_bias,
    cotangent,
):
    count = lax.axis_size("dp")
    index = lax.axis_index("dp")
    core = lax.axis_index("mp") % 2
    rows, depth = inputs.shape
    local = depth // count
    width = qkv_weight.shape[2]
    heads = width // HD
    units = fc_weight.shape[1]
    width2 = 2 * width
    heads2 = 2 * heads
    own_count = rows // 2
    base = depth // CHUNKS
    flip = index if count == CHUNKS else jnp.zeros_like(index)
    info = jnp.stack([flip, core]).astype(jnp.int32)
    seg_row = segments.reshape(1, rows)

    bias_width = qv_bias.shape[1]
    bias_rows = lax.dynamic_update_slice(
        jnp.zeros((heads, 2 * HD), BF), qv_bias, (0, index * bias_width)
    )
    bias_row = bias_rows.reshape(heads, 2, HD).transpose(1, 0, 2).reshape(1, width2)
    vectors = jnp.stack(
        [norm1_gain, norm1_shift, attn_bias, norm2_gain, norm2_shift, fc_bias[0], proj_bias]
    )
    placed = lax.dynamic_update_slice(
        jnp.zeros((vectors.shape[0], depth), BF), vectors, (0, index * local)
    )
    tile = jnp.concatenate(
        [
            placed,
            jnp.pad(bias_row, ((0, EXTRA - vectors.shape[0] - 1), (0, depth - width2))),
        ],
        0,
    )
    mats = jnp.concatenate(
        [qkv_weight.transpose(1, 0, 2).reshape(local, 3 * width), attn_weight.T], 1
    )
    wide = jnp.concatenate([fc_weight, proj_weight.T], 1)
    if count == CHUNKS:
        own_a = gather_blocks(jnp.concatenate([mats, tile], 0))
        wide = lax.optimization_barrier((wide, own_a))[0]
        own_b = gather_blocks(wide)
    else:
        full = lax.all_gather(mats, "dp", axis=0, tiled=True).reshape(CHUNKS, base, depth)
        total = jnp.sum(lax.all_gather(tile, "dp", axis=0).astype(F32), 0).astype(BF)
        total = jnp.pad(total[None], ((0, CHUNKS - 1), (0, 0), (0, 0)))
        own_a = jnp.concatenate([full, total], 1)
        own_b = lax.all_gather(wide, "dp", axis=0, tiled=True).reshape(CHUNKS, base, 2 * units)
    sib_a = swap_core(own_a)
    first_low, vec = call(
        norm_kernel,
        [shape((rows, depth)), shape((EXTRA, depth), F32)],
        info,
        inputs,
        own_a,
        name="norm_first",
    )
    pairs = heads2 * TILE * (own_count // TILE) * (own_count // TILE + 1) * TILE
    weight = shape((depth, width2))
    part, mixed, q, k, v, probs, wq, wk, wv, wo, first_own = call(
        attend_kernel,
        [
            shape((own_count, depth)),
            shape((own_count, width2)),
            shape((heads2, own_count, HD)),
            shape((heads2, rows, HD)),
            shape((heads2, rows, HD)),
            shape((heads2, TILE, TILE * (own_count // TILE) * (own_count // TILE + 1))),
            weight,
            weight,
            weight,
            weight,
            shape((own_count, depth)),
        ],
        info,
        first_low,
        own_a,
        sib_a,
        seg_row,
        scratch=[
            pltpu.VMEM((rows, width2), F32),
            pltpu.VMEM((heads2 + 1, TILE, rows), F32),
            pltpu.VMEM((heads2, own_count, HD), F32),
        ],
        flops=4 * pairs * HD + 5 * rows * depth * width2,
        name="attend",
    )
    got = swap_chip(part)
    sib_b = swap_core(own_b)
    vec_sib = jnp.sum(sib_a[:, base:].astype(F32), 0)
    hid = shape((own_count, 2 * units))
    da, act, dhid, second, dy, middle = call(
        mlp_kernel,
        [
            shape((own_count, depth)),
            hid,
            hid,
            shape((own_count, depth)),
            shape((own_count, depth)),
            shape((own_count, depth), F32),
        ],
        info,
        inputs,
        seg_row,
        cotangent,
        part,
        got,
        vec,
        vec_sib,
        own_b,
        sib_b,
        scratch=[
            pltpu.VMEM((depth, 2 * units), BF),
            pltpu.VMEM((depth, 2 * units), BF),
            pltpu.VMEM((own_count, 512), F32),
            pltpu.VMEM((own_count, 512), F32),
        ],
        flops=12 * own_count * depth * units,
        name="mlp",
    )
    da_got = swap_chip(da)
    mlp_part = call(
        mlp_out_kernel,
        [shape((own_count, depth))],
        info,
        act,
        own_b,
        sib_b,
        scratch=[pltpu.VMEM((depth, 2 * units), BF)],
        flops=4 * own_count * depth * units,
        name="mlp_out",
    )[0]
    grad_own, grad_sib, mlp_sums = call(
        mlp_grad_kernel,
        [
            shape((CHUNKS, base, 2 * units)),
            shape((CHUNKS, base, 2 * units)),
            shape((24, depth), F32),
        ],
        info,
        act,
        dhid,
        second,
        dy,
        scratch=[pltpu.VMEM((depth, units), F32)],
        flops=8 * own_count * depth * units,
        name="mlp_grad",
    )
    big, _ = scatter_blocks(info, grad_own, grad_sib, count)
    fc_weight_grad = big[:, :units]
    proj_weight_grad = big[:, units:].T

    dmid, branch, att_sums, dq, keep, send = call(
        attend_back_kernel,
        [
            shape((own_count, depth), F32),
            shape((own_count, depth)),
            shape((8, depth), F32),
            shape((own_count, width2)),
            shape((2 * width2, own_count), F32),
            shape((2 * width2, own_count)),
        ],
        info,
        middle,
        dy,
        da,
        da_got,
        vec,
        wo,
        mixed,
        q,
        k,
        v,
        probs,
        scratch=[
            pltpu.VMEM((own_count, width2), BF),
            pltpu.VMEM((heads2, own_count, HD), BF),
            pltpu.VMEM((heads2, HD, rows), F32),
            pltpu.VMEM((heads2, HD, rows), F32),
            pltpu.VMEM((heads2, own_count, HD), F32),
            pltpu.VMEM((TILE, rows), F32),
            pltpu.VMEM((TILE, rows), BF),
            pltpu.VMEM((heads2, own_count, TILE), F32),
        ],
        flops=8 * pairs * HD,
        name="attend_back",
    )
    keep_got = swap_core(send)
    attn_full = call(
        attn_grad_kernel,
        [shape((depth, width2), F32)],
        info,
        branch,
        mixed,
        flops=2 * own_count * depth * width2,
        name="attn_grad",
    )[0]
    first_part, dkv = call(
        first_grad_kernel,
        [shape((own_count, depth)), shape((2 * width2, own_count))],
        info,
        dq,
        keep,
        keep_got,
        wq,
        wk,
        wv,
        flops=6 * own_count * depth * width2,
        name="first_grad",
    )
    first_got = swap_chip(first_part)
    qkv_own, qkv_sib, tile_own, tile_sib = call(
        qkv_grad_kernel,
        [shape((CHUNKS, base, 4 * width))] * 2 + [shape((EXTRA, depth))] * 2,
        info,
        first_own,
        dq,
        dkv,
        attn_full,
        first_part,
        inputs,
        mlp_sums,
        att_sums,
        scratch=[pltpu.VMEM((EXTRA, depth), F32)],
        flops=6 * own_count * depth * width2,
        name="qkv_grad",
    )
    mask = (jnp.arange(EXTRA) < 2)[:, None]
    tile_got = swap_core(tile_sib)
    part_sum = jnp.where(mask, tile_own.astype(F32) + tile_got.astype(F32), 0.0).astype(BF)
    other = swap_chip(part_sum)
    mine, tile = scatter_blocks(info, qkv_own, qkv_sib, count, (tile_own, tile_got, other))
    inputs_low = call(
        final_kernel,
        [shape((own_count, depth))],
        info,
        inputs,
        first_part,
        first_got,
        dmid,
        vec,
        name="final",
    )[0]
    inputs_grad = all_rows(info, inputs_low)
    out_low = call(
        output_kernel,
        [shape((own_count, depth))],
        info,
        seg_row,
        middle,
        mlp_part,
        swap_chip(mlp_part),
        vec,
        name="output",
    )[0]
    outputs = all_rows(info, out_low)

    qkv_weight_grad = mine[:, : 3 * width].reshape(local, 3, width).transpose(1, 0, 2)
    attn_weight_grad = mine[:, 3 * width :].T
    parts = lax.dynamic_slice(tile, (0, index * local), (7, local))
    bias_sum = tile[7, :width2].reshape(2, heads, HD).transpose(1, 0, 2).reshape(heads, 2 * HD)
    qv_bias_grad = lax.dynamic_slice(bias_sum, (0, index * bias_width), (heads, bias_width))
    return (
        outputs,
        inputs_grad,
        parts[0],
        parts[1],
        qkv_weight_grad,
        qv_bias_grad,
        attn_weight_grad,
        parts[2],
        parts[3],
        parts[4],
        fc_weight_grad,
        parts[5][None],
        proj_weight_grad,
        parts[6],
    )


def solution(mesh):
    return jax.shard_map(
        body,
        mesh=mesh,
        in_specs=(
            P("dp", None),
            P("dp"),
            P("dp"),
            P("dp"),
            P(None, "dp", "mp"),
            P("mp", "dp"),
            P("mp", "dp"),
            P("dp"),
            P("dp"),
            P("dp"),
            P("dp", "mp"),
            P("mp", "dp"),
            P("mp", "dp"),
            P("dp"),
            P("dp", None),
        ),
        out_specs=(
            P("dp", None),
            P("dp", None),
            P("dp"),
            P("dp"),
            P(None, "dp", "mp"),
            P("mp", "dp"),
            P("mp", "dp"),
            P("dp"),
            P("dp"),
            P("dp"),
            P("dp", "mp"),
            P("mp", "dp"),
            P("mp", "dp"),
            P("dp"),
        ),
        check_vma=False,
    )
```

```python
import functools

import jax
import jax.numpy as jnp
from jax import lax
from jax.experimental import pallas as pl
from jax.experimental.pallas import tpu as pltpu
from jax.sharding import PartitionSpec as P

HD = 64
TILE = 128
EXTRA = 16
CHUNKS = 8
EPSILON = 1e-05
NEGATIVE = -1e30
BF = jnp.bfloat16
F32 = jnp.float32
CORE_PAIRS = ((0, 1), (1, 0), (2, 3), (3, 2))
CHIP_PAIRS = ((0, 2), (2, 0), (1, 3), (3, 1))
CURVE = 0.7978845608028654


def dot(left, right, left_dim, right_dim):
    return lax.dot_general(
        left, right, (((left_dim,), (right_dim,)), ((), ())), preferred_element_type=F32
    )


def swap_core(value):
    return lax.ppermute(value, "mp", CORE_PAIRS)


def swap_chip(value):
    return lax.ppermute(value, "mp", CHIP_PAIRS)


def swap_mask(value, mask):
    return lax.ppermute(value, "dp", [(i, i ^ mask) for i in range(CHUNKS)])


def swap_bit(value, bit):
    return swap_mask(value, 1 << bit)


def call(kernel, outs, *args, scratch=(), smem=1, flops=0, name=None, after=()):
    first, behind = len(args), len(args) + len(after)

    def run(*refs):
        kernel(*refs[:first], *refs[behind:])

    specs = [pl.BlockSpec(memory_space=pltpu.SMEM)] * smem
    specs += [pl.BlockSpec(memory_space=pltpu.VMEM)] * (len(args) - smem)
    specs += [pl.BlockSpec(memory_space=pl.ANY)] * len(after)
    size = sum(a.size * a.dtype.itemsize for a in args)
    size += sum(o.size * jnp.dtype(o.dtype).itemsize for o in outs)
    return pl.pallas_call(
        run,
        out_shape=outs,
        in_specs=specs,
        out_specs=[pl.BlockSpec(memory_space=pltpu.VMEM)] * len(outs),
        scratch_shapes=list(scratch),
        compiler_params=pltpu.CompilerParams(vmem_limit_bytes=56 * 1024 * 1024),
        cost_estimate=pl.CostEstimate(flops=0, bytes_accessed=1024, transcendentals=0),
        name=name,
    )(*args, *after)


def shape(dims, dtype=BF):
    return jax.ShapeDtypeStruct(tuple(dims), dtype)


def gather_blocks(message, behind=None):
    got = {0: message}
    got[4] = swap_mask(message, 4)
    got[2] = swap_mask(message, 2)
    got[1] = swap_mask(message, 1)
    four, two = got[4], got[2]
    if behind is not None:
        four, two = lax.optimization_barrier((four, two, behind))[:2]
    got[7] = swap_mask(four, 3)
    got[5] = swap_mask(four, 1)
    got[6] = swap_mask(four, 2)
    got[3] = swap_mask(two, 1)
    return [got[r] for r in range(CHUNKS)]


def loop(count, step, fn, unroll=4):
    def run(i, carry):
        fn(pl.multiple_of(i * step, step))
        return carry

    lax.fori_loop(0, count // step, run, 0, unroll=unroll)


def norm_stats(value):
    average = jnp.mean(value, -1, keepdims=True)
    centred = value - average
    spread = jnp.mean(centred * centred, -1, keepdims=True)
    factor = lax.rsqrt(spread + EPSILON)
    return centred * factor, factor


def norm_backward(incoming, scaled, factor, gain):
    weighted = incoming * gain
    first_mean = jnp.mean(weighted, -1, keepdims=True)
    second_mean = jnp.mean(weighted * scaled, -1, keepdims=True)
    return factor * (weighted - first_mean - scaled * second_mean)


def tile_sum(ref, base):
    total = ref[0, base : base + EXTRA, :].astype(F32)
    for r in range(1, CHUNKS):
        total = total + ref[r, base : base + EXTRA, :].astype(F32)
    return total


def own_start(start, core):
    tile = start // TILE
    return pl.multiple_of((2 * tile + core) * TILE + start % TILE, 32)


def colsum(value):
    return jnp.sum(value, 0, keepdims=True)


def norm_kernel(info, x_ref, w_ref, low_ref, vec_ref):
    base = w_ref.shape[1] - EXTRA
    vec_ref[...] = tile_sum(w_ref, base)
    gain, shift = vec_ref[0:1, :], vec_ref[1:2, :]

    def run(at):
        scaled, _ = norm_stats(x_ref[pl.ds(at, 32), :].astype(F32))
        low_ref[pl.ds(at, 32), :] = (scaled * gain + shift).astype(BF)

    loop(x_ref.shape[0], 32, run)


def attend_kernel(
    info,
    low_ref,
    own_ref,
    sib_ref,
    seg_ref,
    part_ref,
    mixed_ref,
    q_ref,
    k_ref,
    v_ref,
    probs_ref,
    wq_ref,
    wk_ref,
    wv_ref,
    wo_ref,
    firstown_ref,
    proj_ref,
    s_ref,
    o_ref,
):
    flip, core = info[0], info[1]
    width = own_ref.shape[2] // 4
    base = own_ref.shape[1] - EXTRA
    rows = low_ref.shape[0]
    heads = 2 * width // HD
    own_count = rows // 2
    for r in range(CHUNKS):
        at = pl.multiple_of((r ^ flip) * base, 32)
        for side, ref in ((0, own_ref), (1, sib_ref)):
            for part, out in enumerate((wq_ref, wk_ref, wv_ref, wo_ref)):
                out[pl.ds(at, base), side * width : (side + 1) * width] = ref[
                    r, 0:base, part * width : (part + 1) * width
                ]
    vec_own = tile_sum(own_ref, base)
    vec_sib = tile_sum(sib_ref, base)
    bias_q = jnp.concatenate([vec_own[7:8, :width], vec_sib[7:8, :width]], 1)
    bias_v = jnp.concatenate(
        [vec_own[7:8, width : 2 * width], vec_sib[7:8, width : 2 * width]], 1
    )
    for j in range(own_count // TILE):
        at = own_start(j * TILE, core)
        firstown_ref[j * TILE : (j + 1) * TILE, :] = low_ref[pl.ds(at, TILE), :]
    scale = float(HD) ** -0.5
    proj_ref[0:own_count, :] = dot(firstown_ref[...], wq_ref[...], 1, 0) + bias_q
    for h in range(heads):
        q_ref[h] = (
            proj_ref[0:own_count, h * HD : (h + 1) * HD].astype(BF).astype(F32) * scale
        ).astype(BF)
    proj_ref[...] = dot(low_ref[...], wk_ref[...], 1, 0)
    for h in range(heads):
        k_ref[h] = proj_ref[:, h * HD : (h + 1) * HD].astype(BF)
    proj_ref[...] = dot(low_ref[...], wv_ref[...], 1, 0) + bias_v
    for h in range(heads):
        v_ref[h] = proj_ref[:, h * HD : (h + 1) * HD].astype(BF)
    lane = lax.broadcasted_iota(jnp.int32, (TILE, TILE), 1)
    line = lax.broadcasted_iota(jnp.int32, (TILE, TILE), 0)
    for j in range(own_count // TILE):
        end = (j + 1) * 2 * TILE
        off = TILE * j * (j + 1)
        at = own_start(j * TILE, core)
        seg_tile = jnp.broadcast_to(seg_ref[0:1, pl.ds(at, TILE)], (TILE, TILE))
        seg_col = jnp.max(jnp.where(lane == line, seg_tile, -2), -1, keepdims=True)
        place = lax.broadcasted_iota(jnp.int32, (TILE, end), 1)
        own_place = at + lax.broadcasted_iota(jnp.int32, (TILE, end), 0)
        allowed = (seg_col == seg_ref[0:1, 0:end]) & (place <= own_place)
        bias = jnp.where(allowed, 0.0, NEGATIVE)
        s_ref[heads, :, 0:end] = bias

        def run(h, carry, j=j, end=end, off=off):
            scores = dot(q_ref[h, j * TILE : (j + 1) * TILE, :], k_ref[h, 0:end, :], 1, 1)
            s_ref[0, :, 0:end] = scores
            for sub in range(4):
                sl = slice(sub * 32, sub * 32 + 32)
                sc = s_ref[0, sl, 0:end] + s_ref[heads, sl, 0:end]
                weights = jnp.exp(sc - jnp.max(sc, -1, keepdims=True))
                inverse = 1.0 / jnp.sum(weights, -1, keepdims=True)
                probs_ref[h, sl, off : off + end] = (weights * inverse).astype(BF)
            o_ref[h, j * TILE : (j + 1) * TILE, :] = dot(
                probs_ref[h, :, off : off + end], v_ref[h, 0:end, :], 1, 0
            )
            return carry

        lax.fori_loop(0, heads, run, 0)
    for h in range(heads):
        mixed_ref[:, h * HD : (h + 1) * HD] = o_ref[h].astype(BF)
    part_ref[...] = dot(mixed_ref[...], wo_ref[...], 1, 1).astype(BF)


def mlp_kernel(
    info,
    x_ref,
    seg_ref,
    cot_ref,
    part_ref,
    recv_ref,
    vec_ref,
    vecsib_ref,
    *refs,
):
    own_refs, sib_refs = refs[:CHUNKS], refs[CHUNKS : 2 * CHUNKS]
    da_ref, act_ref, dhid_ref, second_ref, dy_ref, mid_ref, proj_ref = refs[2 * CHUNKS : -3]
    fc_ref, hid_ref, dact_ref = refs[-3:]
    flip, core = info[0], info[1]
    own_count = part_ref.shape[0]
    base = own_refs[0].shape[0]
    units = own_refs[0].shape[1] // 2
    for r in range(CHUNKS):
        at = pl.multiple_of((r ^ flip) * base, 32)
        for side, ref in ((0, own_refs[r]), (1, sib_refs[r])):
            cols = slice(side * units, (side + 1) * units)
            fc_ref[pl.ds(at, base), cols] = ref[:, 0:units]
            proj_ref[pl.ds(at, base), cols] = ref[:, units : 2 * units]
    gain, shift, bias = vec_ref[3:4, :], vec_ref[4:5, :], vec_ref[2:3, :]
    sub = 32
    lane = lax.broadcasted_iota(jnp.int32, (sub, TILE), 1)
    line = lax.broadcasted_iota(jnp.int32, (sub, TILE), 0)

    def first(at):
        src = own_start(at, core)
        tile_at = pl.multiple_of((2 * (at // TILE) + core) * TILE, TILE)
        seg_tile = jnp.broadcast_to(seg_ref[0:1, pl.ds(tile_at, TILE)], (sub, TILE))
        seg_col = jnp.max(
            jnp.where(lane == line + at % TILE, seg_tile, -2), -1, keepdims=True
        )
        rows = pl.ds(at, sub)
        cot = cot_ref[pl.ds(src, sub), :].astype(F32)
        dy_ref[rows, :] = jnp.where(seg_col >= 0, cot, 0.0).astype(BF)
        middle = (
            x_ref[pl.ds(src, sub), :].astype(F32)
            + (part_ref[rows, :].astype(F32) + recv_ref[rows, :].astype(F32))
            + bias
        )
        mid_ref[rows, :] = middle
        scaled, _ = norm_stats(middle)
        second_ref[rows, :] = (scaled * gain + shift).astype(BF)

    loop(own_count, sub, first)
    step = 512
    for c in range(2 * units // step):
        cols = slice(c * step, (c + 1) * step)
        hid_ref[...] = dot(second_ref[...], fc_ref[:, cols], 1, 0)
        dact_ref[...] = dot(dy_ref[...], proj_ref[:, cols], 1, 0)
        left, right = c * step, (c + 1) * step
        pieces = []
        if left < units:
            pieces.append(vec_ref[5:6, left : min(right, units)])
        if right > units:
            pieces.append(vecsib_ref[5:6, max(left, units) - units : right - units])
        bias_fc = jnp.concatenate(pieces, 1) if len(pieces) > 1 else pieces[0]

        def gelu(at, cols=cols, bias_fc=bias_fc):
            rows = pl.ds(at, 16)
            u = hid_ref[rows, :] + bias_fc
            u2 = u * u
            bend = jnp.tanh(CURVE * u * (1.0 + 0.044715 * u2))
            half = 0.5 * (1.0 + bend)
            act_ref[rows, cols] = (u * half).astype(BF)
            slope = half + (0.5 * CURVE) * u * (1.0 - bend * bend) * (1.0 + 0.134145 * u2)
            dhid_ref[rows, cols] = (dact_ref[rows, :] * slope).astype(BF)

        loop(own_count, 16, gelu)
    da_ref[...] = dot(dhid_ref[...], fc_ref[...], 1, 1).astype(BF)


def mlp_grad_kernel(
    info,
    act_ref,
    dhid_ref,
    second_ref,
    dy_ref,
    proj_ref,
    part_ref,
    own_ref,
    sib_a_ref,
    sib_b_ref,
    sib_c_ref,
    sib_d_ref,
    sums_ref,
    acc_ref,
):
    flip = info[0]
    sib_refs = ((sib_a_ref, sib_b_ref), (sib_c_ref, sib_d_ref))
    part_ref[...] = dot(act_ref[...], proj_ref[...], 1, 1).astype(BF)
    base = own_ref.shape[1]
    units = own_ref.shape[2] // 2
    for kind, left, right in ((0, second_ref, dhid_ref), (1, dy_ref, act_ref)):
        for side in range(2):
            acc_ref[...] = dot(left[...], right[:, side * units : (side + 1) * units], 0, 0)
            for r in range(CHUNKS):
                at = pl.multiple_of((r ^ flip) * base, 32)
                block = acc_ref[pl.ds(at, base), :].astype(BF)
                if side:
                    sib_refs[kind][r // 4][r % 4] = block
                else:
                    own_ref[r, :, kind * units : (kind + 1) * units] = block
    one = jnp.ones((8, act_ref.shape[0]), BF)
    fc_sums = dot(one, dhid_ref[...], 1, 0)
    sums_ref[0:8, :] = fc_sums[:, 0:units]
    sums_ref[8:16, :] = fc_sums[:, units : 2 * units]
    sums_ref[16:24, :] = dot(one, dy_ref[...], 1, 0)


def attend_back_kernel(
    info,
    mid_ref,
    dy_ref,
    da_ref,
    recv_ref,
    vec_ref,
    wo_ref,
    mixed_ref,
    q_ref,
    k_ref,
    v_ref,
    probs_ref,
    dmid_ref,
    branch_ref,
    sums_ref,
    dq_ref,
    keep_ref,
    send_k_ref,
    send_v_ref,
    dm_ref,
    do_ref,
    dkt_ref,
    dvt_ref,
    dqh_ref,
    dp_ref,
    ds_ref,
    delta_ref,
):
    core = info[1]
    own_count = mid_ref.shape[0]
    heads = q_ref.shape[0]
    rows = k_ref.shape[1]
    gain = vec_ref[3:4, :]
    sums_ref[...] = jnp.zeros_like(sums_ref)
    sub = 32

    def first(at):
        rs = pl.ds(at, sub)
        scaled, factor = norm_stats(mid_ref[rs, :])
        incoming = da_ref[rs, :].astype(F32) + recv_ref[rs, :].astype(F32)
        dmid = dy_ref[rs, :].astype(F32) + norm_backward(incoming, scaled, factor, gain)
        dmid_ref[rs, :] = dmid
        low = dmid.astype(BF)
        branch_ref[rs, :] = low
        sums_ref[2:3, :] += colsum(low.astype(F32))
        sums_ref[3:4, :] += colsum(incoming * scaled)
        sums_ref[4:5, :] += colsum(incoming)

    loop(own_count, sub, first)
    dm_ref[...] = dot(branch_ref[...], wo_ref[...], 1, 0).astype(BF)
    for h in range(heads):
        cols = slice(h * HD, (h + 1) * HD)
        do_ref[h] = dm_ref[:, cols]
        delta_ref[h] = jnp.broadcast_to(
            jnp.sum(
                dm_ref[:, cols].astype(F32) * mixed_ref[:, cols].astype(F32), -1, keepdims=True
            ),
            (own_count, TILE),
        )
    scale = float(HD) ** -0.5

    def head(h, carry):
        for j in reversed(range(own_count // TILE)):
            end = (j + 1) * 2 * TILE
            off = TILE * j * (j + 1)
            rs = slice(j * TILE, (j + 1) * TILE)
            dp_ref[:, 0:end] = dot(do_ref[h, rs, :], v_ref[h, 0:end, :], 1, 1)
            for s in range(4):
                sl = slice(s * 32, s * 32 + 32)
                delta = delta_ref[h, j * TILE + s * 32 : j * TILE + s * 32 + 32, 0:1]
                p = probs_ref[h, sl, off : off + end].astype(F32)
                ds_ref[sl, 0:end] = (p * (dp_ref[sl, 0:end] - delta)).astype(BF)
            ds = ds_ref[:, 0:end]
            dqh_ref[h, rs, :] = dot(ds, k_ref[h, 0:end, :], 1, 0) * scale
            dk = dot(q_ref[h, rs, :], ds, 0, 0)
            dv = dot(do_ref[h, rs, :], probs_ref[h, :, off : off + end], 0, 0)
            if j == own_count // TILE - 1:
                dkt_ref[h] = dk
                dvt_ref[h] = dv
            else:
                dkt_ref[h, :, 0:end] += dk
                dvt_ref[h, :, 0:end] += dv
        return carry

    lax.fori_loop(0, heads, head, 0)
    width2 = heads * HD
    for h in range(heads):
        dq_ref[:, h * HD : (h + 1) * HD] = dqh_ref[h].astype(BF)
        twin = (h + heads // 2) % heads
        for j in range(own_count // TILE):
            mine = pl.multiple_of((2 * j + core) * TILE, TILE)
            yours = pl.multiple_of((2 * j + 1 - core) * TILE, TILE)
            cols = slice(j * TILE, (j + 1) * TILE)
            for part, ref, send in ((0, dkt_ref, send_k_ref), (1, dvt_ref, send_v_ref)):
                at = part * width2
                keep_ref[at + h * HD : at + (h + 1) * HD, cols] = ref[h, :, pl.ds(mine, TILE)]
                send[twin * HD : (twin + 1) * HD, cols] = ref[h, :, pl.ds(yours, TILE)].astype(BF)


def attn_grad_kernel(info, branch_ref, mixed_ref, out_ref):
    out_ref[...] = dot(branch_ref[...], mixed_ref[...], 0, 0)


def first_grad_kernel(
    info, dq_ref, keep_ref, got_k_ref, got_v_ref, wq_ref, wk_ref, wv_ref, part_ref, dkv_ref
):
    width2 = dq_ref.shape[1]
    for p, got in enumerate((got_k_ref, got_v_ref)):
        rows = slice(p * width2, (p + 1) * width2)
        dkv_ref[rows, :] = (keep_ref[rows, :] + got[...].astype(F32)).astype(BF)
    part_ref[...] = (
        dot(dq_ref[...], wq_ref[...], 1, 1)
        + dot(dkv_ref[0:width2, :], wk_ref[...], 0, 1)
        + dot(dkv_ref[width2 : 2 * width2, :], wv_ref[...], 0, 1)
    ).astype(BF)


def qkv_grad_kernel(
    info,
    first_ref,
    dq_ref,
    dkv_ref,
    attn_ref,
    part_ref,
    x_ref,
    mlp_sums_ref,
    att_sums_ref,
    own_ref,
    sib_a_ref,
    sib_b_ref,
    tile_own_ref,
    tile_sib_ref,
    whole_ref,
    sum_ref,
):
    flip, core = info[0], info[1]
    width2 = dq_ref.shape[1]
    width = width2 // 2
    base = own_ref.shape[1]
    for part in range(4):
        if part == 0:
            whole = dot(first_ref[...], dq_ref[...], 0, 0)
        elif part == 3:
            whole = attn_ref[...]
        else:
            whole = dot(
                first_ref[...], dkv_ref[(part - 1) * width2 : part * width2, :], 0, 1
            )
        whole_ref[...] = whole
        cols = slice(part * width, (part + 1) * width)
        for r in range(CHUNKS):
            at = pl.multiple_of((r ^ flip) * base, 32)
            block = whole_ref[pl.ds(at, base), :].astype(BF)
            own_ref[r, :, cols] = block[:, 0:width]
            (sib_a_ref, sib_b_ref)[r // 4][r % 4, :, cols] = block[:, width:width2]
    sum_ref[...] = jnp.zeros_like(sum_ref)

    def run(at):
        src = own_start(at, core)
        scaled, _ = norm_stats(x_ref[pl.ds(src, 32), :].astype(F32))
        incoming = part_ref[pl.ds(at, 32), :].astype(F32)
        sum_ref[0:1, :] += colsum(incoming * scaled)
        sum_ref[1:2, :] += colsum(incoming)

    loop(part_ref.shape[0], 32, run)
    ones = jnp.ones((8, dq_ref.shape[0]), BF)
    qs = dot(ones, dq_ref[...], 1, 0)[0:1, :]
    vs = dot(ones, dkv_ref[width2 : 2 * width2, :], 1, 1)[0:1, :]
    sum_ref[2:5, :] = att_sums_ref[2:5, :]
    sum_ref[6:7, :] = mlp_sums_ref[16:17, :]
    for side, out in ((0, tile_own_ref), (1, tile_sib_ref)):
        sl = slice(side * width, (side + 1) * width)
        sum_ref[5:6, :] = mlp_sums_ref[8 * side : 8 * side + 1, :]
        sum_ref[7:8, 0:width] = qs[:, sl]
        sum_ref[7:8, width : 2 * width] = vs[:, sl]
        out[...] = sum_ref[...].astype(BF)


def final_kernel(info, x_ref, part_ref, recv_ref, dmid_ref, vec_ref, out_ref):
    core = info[1]
    gain = vec_ref[0:1, :]

    def run(at):
        src = own_start(at, core)
        rs = pl.ds(at, 32)
        scaled, factor = norm_stats(x_ref[pl.ds(src, 32), :].astype(F32))
        incoming = part_ref[rs, :].astype(F32) + recv_ref[rs, :].astype(F32)
        out_ref[rs, :] = (
            dmid_ref[rs, :] + norm_backward(incoming, scaled, factor, gain)
        ).astype(BF)

    loop(part_ref.shape[0], 32, run)


def output_kernel(info, seg_ref, mid_ref, part_ref, recv_ref, vec_ref, out_ref):
    core = info[1]
    bias = vec_ref[6:7, :]
    sub = 32
    lane = lax.broadcasted_iota(jnp.int32, (sub, TILE), 1)
    line = lax.broadcasted_iota(jnp.int32, (sub, TILE), 0)

    def run(at):
        tile_at = pl.multiple_of((2 * (at // TILE) + core) * TILE, TILE)
        seg_tile = jnp.broadcast_to(seg_ref[0:1, pl.ds(tile_at, TILE)], (sub, TILE))
        seg_col = jnp.max(
            jnp.where(lane == line + at % TILE, seg_tile, -2), -1, keepdims=True
        )
        rs = pl.ds(at, sub)
        final = (
            mid_ref[rs, :]
            + (part_ref[rs, :].astype(F32) + recv_ref[rs, :].astype(F32))
            + bias
        )
        out_ref[rs, :] = jnp.where(seg_col >= 0, final, 0.0).astype(BF)

    loop(part_ref.shape[0], sub, run)


def merge_kernel(info, own_ref, got_ref, out_ref):
    core = info[1]
    for j in range(own_ref.shape[0] // TILE):
        sl = slice(j * TILE, (j + 1) * TILE)
        mine = pl.multiple_of((2 * j + core) * TILE, TILE)
        yours = pl.multiple_of((2 * j + 1 - core) * TILE, TILE)
        out_ref[pl.ds(mine, TILE), :] = own_ref[sl, :]
        out_ref[pl.ds(yours, TILE), :] = got_ref[sl, :]


def all_rows(info, own):
    return call(
        merge_kernel,
        [shape((2 * own.shape[0], own.shape[1]))],
        info,
        own,
        swap_core(own),
        name="merge",
    )[0]


def scatter_first_kernel(pieces, info, own_ref, *refs):
    got_refs, refs = refs[:pieces], refs[pieces:]
    tiles, (keep_a, send_a, keep_b, send_b) = refs[:-4], refs[-4:]
    base = own_ref.shape[1]
    half = own_ref.shape[2] // 2
    for side, keep, send in ((0, keep_a, send_a), (1, keep_b, send_b)):
        cols = slice(side * half, (side + 1) * half)
        got_cols = cols if pieces == 2 else slice(0, half)
        kept, sent = 0, 0
        for r in range(CHUNKS):
            got = got_refs[r // 4 if pieces == 2 else 2 * side + r // 4]
            value = own_ref[r, :, cols].astype(F32) + got[r % 4, :, got_cols].astype(F32)
            if (r >> side) & 1:
                send[sent * base : (sent + 1) * base, :] = value.astype(BF)
                sent += 1
            else:
                keep[kept * base : (kept + 1) * base, :] = value
                kept += 1
        if tiles:
            value = tiles[0][:, cols].astype(F32) + tiles[1][:, cols].astype(F32)
            send[4 * base : 4 * base + EXTRA, :] = value.astype(BF)
            keep[4 * base : 4 * base + EXTRA, :] = value


def scatter_second_kernel(
    tiled, info, keep_a, got_a, keep_b, got_b, next_a, send_a, next_b, send_b
):
    extra = EXTRA if tiled else 0
    base = (keep_a.shape[0] - extra) // 4
    for keep, got, left, send, order in (
        (keep_a, got_a, next_a, send_a, (0, 1, 0, 1)),
        (keep_b, got_b, next_b, send_b, (0, 1, 0, 1)),
    ):
        kept, sent = 0, 0
        for r in range(4):
            rows = slice(r * base, (r + 1) * base)
            value = keep[rows, :] + got[rows, :].astype(F32)
            if order[r]:
                send[sent * base : (sent + 1) * base, :] = value.astype(BF)
                sent += 1
            else:
                left[kept * base : (kept + 1) * base, :] = value
                kept += 1
        if tiled:
            low = keep[4 * base : 4 * base + extra, :].astype(BF).astype(F32)
            value = low + got[4 * base : 4 * base + extra, :].astype(F32)
            send[2 * base : 2 * base + extra, :] = value.astype(BF)
            left[2 * base : 2 * base + extra, :] = value


def scatter_third_kernel(tiled, info, keep_a, got_a, keep_b, got_b, left, send):
    extra = EXTRA if tiled else 0
    base = (keep_a.shape[0] - extra) // 2
    half = keep_a.shape[1]
    for keep, got, at in ((keep_a, got_a, 0), (keep_b, got_b, half)):
        cols = slice(at, at + half)
        left[0:base, cols] = keep[0:base, :] + got[0:base, :].astype(F32)
        send[0:base, cols] = (
            keep[base : 2 * base, :] + got[base : 2 * base, :].astype(F32)
        ).astype(BF)
        if tiled:
            rows = slice(2 * base, 2 * base + extra)
            value = keep[rows, :].astype(BF).astype(F32) + got[rows, :].astype(F32)
            left[base : base + extra, cols] = value
            send[base : base + extra, cols] = value.astype(BF)


def scatter_big_kernel(info, left, got, fc_ref, proj_ref):
    units = fc_ref.shape[1]
    total = left[...] + got[...].astype(F32)
    fc_ref[...] = total[:, :units]
    proj_ref[...] = jnp.transpose(total[:, units:])


def scatter_small_kernel(info, left, got, qkv_ref, attn_ref, tile_ref):
    base = left.shape[0] - EXTRA
    width = qkv_ref.shape[2]
    total = left[0:base, :] + got[0:base, :].astype(F32)
    for p in range(3):
        qkv_ref[p] = total[:, p * width : (p + 1) * width]
    attn_ref[...] = jnp.transpose(total[:, 3 * width :])
    rows = slice(base, base + EXTRA)
    tile_ref[...] = left[rows, :].astype(BF).astype(F32) + got[rows, :].astype(F32)


def scatter_start(info, own, sib, tiles=(), after=()):
    base, columns = own.shape[1:]
    half = columns // 2
    rows = 4 * base + (EXTRA if tiles else 0)
    return call(
        functools.partial(scatter_first_kernel, len(sib)),
        [shape((rows, half), F32), shape((rows, half))] * 2,
        info,
        own,
        *[swap_core(piece) for piece in sib],
        *tiles,
        name="scatter_first",
        after=after,
    )


def scatter_send(state, bits):
    keep_a, send_a, keep_b, send_b = state
    return keep_a, swap_bit(send_a, bits[0]), keep_b, swap_bit(send_b, bits[1])


def scatter_middle(info, state, tiled, after=()):
    half = state[0].shape[1]
    extra = EXTRA if tiled else 0
    rows = (state[0].shape[0] - extra) // 2 + extra
    return call(
        functools.partial(scatter_second_kernel, tiled),
        [shape((rows, half), F32), shape((rows, half))] * 2,
        info,
        *state,
        name="scatter_second",
        after=after,
    )


def scatter_late(info, state, tiled, after=()):
    half = state[0].shape[1]
    extra = EXTRA if tiled else 0
    rows = (state[0].shape[0] - extra) // 2 + extra
    left, send = call(
        functools.partial(scatter_third_kernel, tiled),
        [shape((rows, 2 * half), F32), shape((rows, 2 * half))],
        info,
        *state,
        name="scatter_third",
        after=after,
    )
    return left, swap_bit(send, 2)


def scatter_plain(own, sib):
    if len(sib) == 4:
        sib = [jnp.concatenate([sib[i], sib[i + 2]], 2) for i in range(2)]
    sib = jnp.concatenate(sib, 0)
    total = own.astype(F32) + swap_core(sib).astype(F32)
    total = total.reshape(total.shape[0] * total.shape[1], total.shape[2])
    return lax.psum_scatter(total, "dp", scatter_dimension=0, tiled=True)


def body(
    inputs,
    segments,
    norm1_gain,
    norm1_shift,
    qkv_weight,
    qv_bias,
    attn_weight,
    attn_bias,
    norm2_gain,
    norm2_shift,
    fc_weight,
    fc_bias,
    proj_weight,
    proj_bias,
    cotangent,
):
    count = lax.axis_size("dp")
    index = lax.axis_index("dp")
    core = lax.axis_index("mp") % 2
    rows, depth = inputs.shape
    local = depth // count
    width = qkv_weight.shape[2]
    heads = width // HD
    units = fc_weight.shape[1]
    width2 = 2 * width
    heads2 = 2 * heads
    own_count = rows // 2
    base = depth // CHUNKS
    flip = index if count == CHUNKS else jnp.zeros_like(index)
    info = jnp.stack([flip, core]).astype(jnp.int32)
    seg_row = segments.reshape(1, rows)

    bias_width = qv_bias.shape[1]
    bias_rows = lax.dynamic_update_slice(
        jnp.zeros((heads, 2 * HD), BF), qv_bias, (0, index * bias_width)
    )
    bias_row = bias_rows.reshape(heads, 2, HD).transpose(1, 0, 2).reshape(1, width2)
    vectors = jnp.stack(
        [norm1_gain, norm1_shift, attn_bias, norm2_gain, norm2_shift, fc_bias[0], proj_bias]
    )
    placed = lax.dynamic_update_slice(
        jnp.zeros((vectors.shape[0], depth), BF), vectors, (0, index * local)
    )
    tile = jnp.concatenate(
        [
            placed,
            jnp.pad(bias_row, ((0, EXTRA - vectors.shape[0] - 1), (0, depth - width2))),
        ],
        0,
    )
    mats = jnp.concatenate(
        [qkv_weight.transpose(1, 0, 2).reshape(local, 3 * width), attn_weight.T], 1
    )
    wide = jnp.concatenate([fc_weight, proj_weight.T], 1)
    if count == CHUNKS:
        own_a = jnp.stack(gather_blocks(jnp.concatenate([mats, tile], 0)))
        wide = lax.optimization_barrier((wide, own_a))[0]
    else:
        full = lax.all_gather(mats, "dp", axis=0, tiled=True).reshape(CHUNKS, base, depth)
        total = jnp.sum(lax.all_gather(tile, "dp", axis=0).astype(F32), 0).astype(BF)
        total = jnp.pad(total[None], ((0, CHUNKS - 1), (0, 0), (0, 0)))
        own_a = jnp.concatenate([full, total], 1)
        own_b = lax.all_gather(wide, "dp", axis=0, tiled=True).reshape(CHUNKS, base, 2 * units)
        own_b = [own_b[r] for r in range(CHUNKS)]
    sib_a = swap_core(own_a)
    first_low, vec = call(
        norm_kernel,
        [shape((rows, depth)), shape((EXTRA, depth), F32)],
        info,
        inputs,
        own_a,
        name="norm_first",
    )
    if count == CHUNKS:
        blocks = gather_blocks(wide, first_low)
    pairs = heads2 * TILE * (own_count // TILE) * (own_count // TILE + 1) * TILE
    weight = shape((depth, width2))
    part, mixed, q, k, v, probs, wq, wk, wv, wo, first_own = call(
        attend_kernel,
        [
            shape((own_count, depth)),
            shape((own_count, width2)),
            shape((heads2, own_count, HD)),
            shape((heads2, rows, HD)),
            shape((heads2, rows, HD)),
            shape((heads2, TILE, TILE * (own_count // TILE) * (own_count // TILE + 1))),
            weight,
            weight,
            weight,
            weight,
            shape((own_count, depth)),
        ],
        info,
        first_low,
        own_a,
        sib_a,
        seg_row,
        scratch=[
            pltpu.VMEM((rows, width2), F32),
            pltpu.VMEM((heads2 + 1, TILE, rows), F32),
            pltpu.VMEM((heads2, own_count, HD), F32),
        ],
        flops=4 * pairs * HD + 5 * rows * depth * width2,
        name="attend",
    )
    got = swap_chip(part)
    if count == CHUNKS:
        own_b = lax.optimization_barrier((blocks, part))[0]
    sib_b = [swap_core(block) for block in own_b]
    vec_sib = jnp.sum(sib_a[:, base:].astype(F32), 0)
    hid = shape((own_count, 2 * units))
    da, act, dhid, second, dy, middle, proj_full = call(
        mlp_kernel,
        [
            shape((own_count, depth)),
            hid,
            hid,
            shape((own_count, depth)),
            shape((own_count, depth)),
            shape((own_count, depth), F32),
            shape((depth, 2 * units)),
        ],
        info,
        inputs,
        seg_row,
        cotangent,
        part,
        got,
        vec,
        vec_sib,
        *own_b,
        *sib_b,
        scratch=[
            pltpu.VMEM((depth, 2 * units), BF),
            pltpu.VMEM((own_count, 512), F32),
            pltpu.VMEM((own_count, 512), F32),
        ],
        flops=12 * own_count * depth * units,
        name="mlp",
    )
    da_got = swap_chip(da)
    mlp_part, grad_own, *grad_sib, mlp_sums = call(
        mlp_grad_kernel,
        [
            shape((own_count, depth)),
            shape((CHUNKS, base, 2 * units)),
            *[shape((CHUNKS // 2, base, units))] * 4,
            shape((24, depth), F32),
        ],
        info,
        act,
        dhid,
        second,
        dy,
        proj_full,
        scratch=[pltpu.VMEM((depth, units), F32)],
        flops=12 * own_count * depth * units,
        name="mlp_grad",
    )
    mlp_got = swap_chip(mlp_part)
    exact = count == CHUNKS
    if exact:
        big_state = scatter_start(info, grad_own, grad_sib)
        big_sent = big_state[1]
        big_state = scatter_send(big_state, (0, 1))
    else:
        big = scatter_plain(grad_own, grad_sib)
        fc_weight_grad, proj_weight_grad = big[:, :units], big[:, units:].T

    dmid, branch, att_sums, dq, keep, *send = call(
        attend_back_kernel,
        [
            shape((own_count, depth), F32),
            shape((own_count, depth)),
            shape((8, depth), F32),
            shape((own_count, width2)),
            shape((2 * width2, own_count), F32),
            *[shape((width2, own_count))] * 2,
        ],
        info,
        middle,
        dy,
        da,
        da_got,
        vec,
        wo,
        mixed,
        q,
        k,
        v,
        probs,
        scratch=[
            pltpu.VMEM((own_count, width2), BF),
            pltpu.VMEM((heads2, own_count, HD), BF),
            pltpu.VMEM((heads2, HD, rows), F32),
            pltpu.VMEM((heads2, HD, rows), F32),
            pltpu.VMEM((heads2, own_count, HD), F32),
            pltpu.VMEM((TILE, rows), F32),
            pltpu.VMEM((TILE, rows), BF),
            pltpu.VMEM((heads2, own_count, TILE), F32),
        ],
        flops=8 * pairs * HD,
        name="attend_back",
        after=(big_sent,) if exact else (),
    )
    keep_got = [swap_core(piece) for piece in send]
    attn_full = call(
        attn_grad_kernel,
        [shape((depth, width2), F32)],
        info,
        branch,
        mixed,
        flops=2 * own_count * depth * width2,
        name="attn_grad",
        after=(mlp_got, big_state[1], big_state[3]) if exact else (),
    )[0]
    first_part, dkv = call(
        first_grad_kernel,
        [shape((own_count, depth)), shape((2 * width2, own_count))],
        info,
        dq,
        keep,
        *keep_got,
        wq,
        wk,
        wv,
        flops=6 * own_count * depth * width2,
        name="first_grad",
        after=(attn_full,),
    )
    first_got = swap_chip(first_part)
    qkv_own, *qkv_sib, tile_own, tile_sib = call(
        qkv_grad_kernel,
        [
            shape((CHUNKS, base, 4 * width)),
            *[shape((CHUNKS // 2, base, 4 * width))] * 2,
            *[shape((EXTRA, depth))] * 2,
        ],
        info,
        first_own,
        dq,
        dkv,
        attn_full,
        first_part,
        inputs,
        mlp_sums,
        att_sums,
        scratch=[pltpu.VMEM((depth, width2), F32), pltpu.VMEM((EXTRA, depth), F32)],
        flops=6 * own_count * depth * width2,
        name="qkv_grad",
    )
    tiles = (tile_own, swap_core(tile_sib))
    if exact:
        big_state = scatter_middle(info, big_state, False, after=(qkv_own,))
        small_state = scatter_start(info, qkv_own, qkv_sib, tiles, after=(big_state[0],))
        small_sent = small_state[1]
        big_state = scatter_send(big_state, (1, 0))
        small_state = scatter_send(small_state, (0, 1))
        big_last = scatter_late(info, big_state, False)
        small_state = scatter_middle(info, small_state, True, after=(big_last[0],))
        small_state = scatter_send(small_state, (1, 0))
        fc_weight_grad, proj_weight_grad = call(
            scatter_big_kernel,
            [shape((local, units), F32), shape((units, local), F32)],
            info,
            *big_last,
            name="scatter_big",
        )
        small_last = scatter_late(info, small_state, True)
        qkv_weight_grad, attn_weight_grad, tile = call(
            scatter_small_kernel,
            [
                shape((3, local, width), F32),
                shape((width, local), F32),
                shape((EXTRA, depth), F32),
            ],
            info,
            *small_last,
            name="scatter_small",
            after=(fc_weight_grad,),
        )
    else:
        mine = scatter_plain(qkv_own, qkv_sib)
        qkv_weight_grad = mine[:, : 3 * width].reshape(local, 3, width).transpose(1, 0, 2)
        attn_weight_grad = mine[:, 3 * width :].T
        tile = lax.psum(tiles[0].astype(F32) + tiles[1].astype(F32), "dp")
    tile_got = swap_chip(tile.astype(BF)).astype(F32)
    mask = (jnp.arange(EXTRA) < 2)[:, None]
    tile = jnp.where(mask, tile.astype(BF).astype(F32) + tile_got, tile)
    inputs_low = call(
        final_kernel,
        [shape((own_count, depth))],
        info,
        inputs,
        first_part,
        first_got,
        dmid,
        vec,
        name="final",
        after=(small_sent,) if exact else (),
    )[0]
    inputs_grad = all_rows(info, inputs_low)
    out_low = call(
        output_kernel,
        [shape((own_count, depth))],
        info,
        seg_row,
        middle,
        mlp_part,
        mlp_got,
        vec,
        name="output",
    )[0]
    outputs = all_rows(info, out_low)

    parts = lax.dynamic_slice(tile, (0, index * local), (7, local))
    bias_sum = tile[7, :width2].reshape(2, heads, HD).transpose(1, 0, 2).reshape(heads, 2 * HD)
    qv_bias_grad = lax.dynamic_slice(bias_sum, (0, index * bias_width), (heads, bias_width))
    return (
        outputs,
        inputs_grad,
        parts[0],
        parts[1],
        qkv_weight_grad,
        qv_bias_grad,
        attn_weight_grad,
        parts[2],
        parts[3],
        parts[4],
        fc_weight_grad,
        parts[5][None],
        proj_weight_grad,
        parts[6],
    )


def solution(mesh):
    return jax.shard_map(
        body,
        mesh=mesh,
        in_specs=(
            P("dp", None),
            P("dp"),
            P("dp"),
            P("dp"),
            P(None, "dp", "mp"),
            P("mp", "dp"),
            P("mp", "dp"),
            P("dp"),
            P("dp"),
            P("dp"),
            P("dp", "mp"),
            P("mp", "dp"),
            P("mp", "dp"),
            P("dp"),
            P("dp", None),
        ),
        out_specs=(
            P("dp", None),
            P("dp", None),
            P("dp"),
            P("dp"),
            P(None, "dp", "mp"),
            P("mp", "dp"),
            P("mp", "dp"),
            P("dp"),
            P("dp"),
            P("dp"),
            P("dp", "mp"),
            P("mp", "dp"),
            P("mp", "dp"),
            P("dp"),
        ),
        check_vma=False,
    )
```

```python
import functools

import jax
import jax.numpy as jnp
from jax import lax
from jax.experimental import pallas as pl
from jax.experimental.pallas import tpu as pltpu
from jax.sharding import PartitionSpec as P

HD = 64
TILE = 128
EXTRA = 16
CHUNKS = 8
EPSILON = 1e-05
NEGATIVE = -1e30
BF = jnp.bfloat16
F32 = jnp.float32
CORE_PAIRS = ((0, 1), (1, 0), (2, 3), (3, 2))
CHIP_PAIRS = ((0, 2), (2, 0), (1, 3), (3, 1))
CURVE = 0.7978845608028654


def dot(left, right, left_dim, right_dim):
    return lax.dot_general(
        left, right, (((left_dim,), (right_dim,)), ((), ())), preferred_element_type=F32
    )


def swap_core(value):
    return lax.ppermute(value, "mp", CORE_PAIRS)


def swap_chip(value):
    return lax.ppermute(value, "mp", CHIP_PAIRS)


def swap_mask(value, mask):
    return lax.ppermute(value, "dp", [(i, i ^ mask) for i in range(CHUNKS)])


def swap_bit(value, bit):
    return swap_mask(value, 1 << bit)


def call(kernel, outs, *args, scratch=(), smem=1, cost=0, name=None, after=()):
    first, behind = len(args), len(args) + len(after)

    def run(*refs):
        kernel(*refs[:first], *refs[behind:])

    specs = [pl.BlockSpec(memory_space=pltpu.SMEM)] * smem
    specs += [pl.BlockSpec(memory_space=pltpu.VMEM)] * (len(args) - smem)
    specs += [pl.BlockSpec(memory_space=pl.ANY)] * len(after)
    return pl.pallas_call(
        run,
        out_shape=outs,
        in_specs=specs,
        out_specs=[pl.BlockSpec(memory_space=pltpu.VMEM)] * len(outs),
        scratch_shapes=list(scratch),
        compiler_params=pltpu.CompilerParams(vmem_limit_bytes=56 * 1024 * 1024),
        cost_estimate=pl.CostEstimate(flops=cost * 10**9, bytes_accessed=1024, transcendentals=0),
        name=name,
    )(*args, *after)


def shape(dims, dtype=BF):
    return jax.ShapeDtypeStruct(tuple(dims), dtype)


def gather_blocks(message, behind=None):
    got = {0: message}
    got[4] = swap_mask(message, 4)
    got[2] = swap_mask(message, 2)
    got[1] = swap_mask(message, 1)
    four, two = got[4], got[2]
    if behind is not None:
        four, two = lax.optimization_barrier((four, two, behind))[:2]
    got[7] = swap_mask(four, 3)
    got[5] = swap_mask(four, 1)
    got[6] = swap_mask(four, 2)
    got[3] = swap_mask(two, 1)
    return [got[r] for r in range(CHUNKS)]


def loop(count, step, fn, unroll=4):
    def run(i, carry):
        fn(pl.multiple_of(i * step, step))
        return carry

    lax.fori_loop(0, count // step, run, 0, unroll=unroll)


def norm_backward(incoming, scaled, factor, gain):
    weighted = incoming * gain
    first_mean = jnp.mean(weighted, -1, keepdims=True)
    second_mean = jnp.mean(weighted * scaled, -1, keepdims=True)
    return factor * (weighted - first_mean - scaled * second_mean)


def tile_sum(ref, base):
    total = ref[0, base : base + EXTRA, :].astype(F32)
    for r in range(1, CHUNKS):
        total = total + ref[r, base : base + EXTRA, :].astype(F32)
    return total


def own_start(start, core):
    tile = start // TILE
    return pl.multiple_of((2 * tile + core) * TILE + start % TILE, 32)


def colsum(value):
    return jnp.sum(value, 0, keepdims=True)


def spread_stats(value):
    average = jnp.mean(value, -1, keepdims=True)
    centred = value - average
    factor = lax.rsqrt(jnp.mean(centred * centred, -1, keepdims=True) + EPSILON)
    rows = value.shape[0]
    return jnp.concatenate(
        [jnp.broadcast_to(average, (rows, TILE)), jnp.broadcast_to(factor, (rows, TILE))], 1
    )


def stats_kernel(info, x_ref, stat_ref):
    def run(at):
        rs = pl.ds(at, 32)
        stat_ref[rs, :] = spread_stats(x_ref[rs, :].astype(F32))

    loop(x_ref.shape[0], 32, run)


def project_kernel(
    info,
    x_ref,
    stat_ref,
    own_ref,
    sib_ref,
    q_ref,
    k_ref,
    v_ref,
    wq_ref,
    wk_ref,
    wv_ref,
    wo_ref,
    firstown_ref,
    vec_ref,
    vecsib_ref,
    low_ref,
    proj_ref,
):
    flip, core = info[0], info[1]
    width = own_ref.shape[2] // 4
    base = own_ref.shape[1] - EXTRA
    rows = low_ref.shape[0]
    heads = 2 * width // HD
    own_count = rows // 2
    vec_ref[...] = tile_sum(own_ref, base)
    vecsib_ref[...] = tile_sum(sib_ref, base)
    gain, shift = vec_ref[0:1, :], vec_ref[1:2, :]

    def norm(at):
        rs = pl.ds(at, 32)
        scaled = (x_ref[rs, :].astype(F32) - stat_ref[rs, 0:1]) * stat_ref[rs, TILE : TILE + 1]
        low_ref[rs, :] = (scaled * gain + shift).astype(BF)

    loop(rows, 32, norm)
    for r in range(CHUNKS):
        at = pl.multiple_of((r ^ flip) * base, 32)
        for side, ref in ((0, own_ref), (1, sib_ref)):
            for part, out in enumerate((wq_ref, wk_ref, wv_ref, wo_ref)):
                out[pl.ds(at, base), side * width : (side + 1) * width] = ref[
                    r, 0:base, part * width : (part + 1) * width
                ]
    bias_q = jnp.concatenate([vec_ref[7:8, :width], vecsib_ref[7:8, :width]], 1)
    bias_v = jnp.concatenate(
        [vec_ref[7:8, width : 2 * width], vecsib_ref[7:8, width : 2 * width]], 1
    )
    for j in range(own_count // TILE):
        at = own_start(j * TILE, core)
        firstown_ref[j * TILE : (j + 1) * TILE, :] = low_ref[pl.ds(at, TILE), :]
    scale = float(HD) ** -0.5
    proj_ref[0:own_count, :] = dot(firstown_ref[...], wq_ref[...], 1, 0) + bias_q
    for h in range(heads):
        q_ref[h] = (
            proj_ref[0:own_count, h * HD : (h + 1) * HD].astype(BF).astype(F32) * scale
        ).astype(BF)
    proj_ref[...] = dot(low_ref[...], wk_ref[...], 1, 0)
    for h in range(heads):
        k_ref[h] = proj_ref[:, h * HD : (h + 1) * HD].astype(BF)
    proj_ref[...] = dot(low_ref[...], wv_ref[...], 1, 0) + bias_v
    for h in range(heads):
        v_ref[h] = proj_ref[:, h * HD : (h + 1) * HD].astype(BF)


def attend_kernel(
    info, q_ref, k_ref, v_ref, wo_ref, seg_ref, part_ref, mixed_ref, probs_ref, s_ref, o_ref
):
    core = info[1]
    heads, own_count = q_ref.shape[:2]
    lane = lax.broadcasted_iota(jnp.int32, (TILE, TILE), 1)
    line = lax.broadcasted_iota(jnp.int32, (TILE, TILE), 0)
    for j in range(own_count // TILE):
        end = (j + 1) * 2 * TILE
        off = TILE * j * (j + 1)
        at = own_start(j * TILE, core)
        seg_tile = jnp.broadcast_to(seg_ref[0:1, pl.ds(at, TILE)], (TILE, TILE))
        seg_col = jnp.max(jnp.where(lane == line, seg_tile, -2), -1, keepdims=True)
        place = lax.broadcasted_iota(jnp.int32, (TILE, end), 1)
        own_place = at + lax.broadcasted_iota(jnp.int32, (TILE, end), 0)
        allowed = (seg_col == seg_ref[0:1, 0:end]) & (place <= own_place)
        bias = jnp.where(allowed, 0.0, NEGATIVE)
        s_ref[heads, :, 0:end] = bias

        def run(h, carry, j=j, end=end, off=off):
            scores = dot(q_ref[h, j * TILE : (j + 1) * TILE, :], k_ref[h, 0:end, :], 1, 1)
            s_ref[h, :, 0:end] = scores
            for sub in range(4):
                sl = slice(sub * 32, sub * 32 + 32)
                sc = s_ref[h, sl, 0:end] + s_ref[heads, sl, 0:end]
                weights = jnp.exp(sc - jnp.max(sc, -1, keepdims=True))
                inverse = 1.0 / jnp.sum(weights, -1, keepdims=True)
                probs_ref[h, sl, off : off + end] = (weights * inverse).astype(BF)
            o_ref[h, j * TILE : (j + 1) * TILE, :] = dot(
                probs_ref[h, :, off : off + end], v_ref[h, 0:end, :], 1, 0
            )
            return carry

        lax.fori_loop(0, heads, run, 0, unroll=True)
    for h in range(heads):
        mixed_ref[:, h * HD : (h + 1) * HD] = o_ref[h].astype(BF)
    part_ref[...] = dot(mixed_ref[...], wo_ref[...], 1, 1).astype(BF)


def mlp_pre_kernel(info, seg_ref, cot_ref, *refs):
    own_refs, sib_refs = refs[:CHUNKS], refs[CHUNKS : 2 * CHUNKS]
    fc_ref, proj_ref, dy_ref, dact_ref = refs[2 * CHUNKS :]
    flip, core = info[0], info[1]
    own_count = dy_ref.shape[0]
    base = own_refs[0].shape[0]
    units = own_refs[0].shape[1] // 2
    sub = 32
    lane = lax.broadcasted_iota(jnp.int32, (sub, TILE), 1)
    line = lax.broadcasted_iota(jnp.int32, (sub, TILE), 0)

    def mask(at):
        src = own_start(at, core)
        tile_at = pl.multiple_of((2 * (at // TILE) + core) * TILE, TILE)
        seg_tile = jnp.broadcast_to(seg_ref[0:1, pl.ds(tile_at, TILE)], (sub, TILE))
        seg_col = jnp.max(
            jnp.where(lane == line + at % TILE, seg_tile, -2), -1, keepdims=True
        )
        cot = cot_ref[pl.ds(src, sub), :].astype(F32)
        dy_ref[pl.ds(at, sub), :] = jnp.where(seg_col >= 0, cot, 0.0).astype(BF)

    loop(own_count, sub, mask)
    for r in range(CHUNKS):
        at = pl.multiple_of((r ^ flip) * base, 32)
        for side, ref in ((0, own_refs[r]), (1, sib_refs[r])):
            cols = slice(side * units, (side + 1) * units)
            fc_ref[pl.ds(at, base), cols] = ref[:, 0:units]
            proj_ref[pl.ds(at, base), cols] = ref[:, units : 2 * units]
    for side in range(2):
        cols = slice(side * units, (side + 1) * units)
        dact_ref[:, cols] = dot(dy_ref[...], proj_ref[:, cols], 1, 0).astype(BF)


def mlp_kernel(
    info,
    x_ref,
    part_ref,
    recv_ref,
    vec_ref,
    vecsib_ref,
    fc_ref,
    dact_ref,
    da_ref,
    act_ref,
    dhid_ref,
    second_ref,
    mid_ref,
    stat_ref,
    hid_ref,
):
    core = info[1]
    own_count = part_ref.shape[0]
    units = fc_ref.shape[1] // 2
    gain, shift, bias = vec_ref[3:4, :], vec_ref[4:5, :], vec_ref[2:3, :]
    sub = 32

    def first(at):
        src = own_start(at, core)
        rows = pl.ds(at, sub)
        middle = (
            x_ref[pl.ds(src, sub), :].astype(F32)
            + (part_ref[rows, :].astype(F32) + recv_ref[rows, :].astype(F32))
            + bias
        )
        mid_ref[rows, :] = middle
        stats = spread_stats(middle)
        stat_ref[rows, :] = stats
        scaled = (middle - stats[:, 0:1]) * stats[:, TILE : TILE + 1]
        second_ref[rows, :] = (scaled * gain + shift).astype(BF)

    loop(own_count, sub, first)
    for side, biases in ((0, vec_ref), (1, vecsib_ref)):
        cols = slice(side * units, (side + 1) * units)
        hid_ref[...] = dot(second_ref[...], fc_ref[:, cols], 1, 0)
        bias_fc = biases[5:6, :]

        def gelu(at, cols=cols, bias_fc=bias_fc):
            rows = pl.ds(at, 16)
            u = hid_ref[rows, :] + bias_fc
            u2 = u * u
            bend = jnp.tanh(CURVE * u * (1.0 + 0.044715 * u2))
            half = 0.5 * (1.0 + bend)
            act_ref[rows, cols] = (u * half).astype(BF)
            slope = half + (0.5 * CURVE) * u * (1.0 - bend * bend) * (1.0 + 0.134145 * u2)
            dhid_ref[rows, cols] = (dact_ref[rows, cols].astype(F32) * slope).astype(BF)

        loop(own_count, 16, gelu)
    da_ref[...] = dot(dhid_ref[...], fc_ref[...], 1, 1).astype(BF)


def mlp_grad_kernel(
    info,
    act_ref,
    dhid_ref,
    second_ref,
    dy_ref,
    proj_ref,
    part_ref,
    own_ref,
    sib_a_ref,
    sib_b_ref,
    sib_c_ref,
    sib_d_ref,
    sums_ref,
    acc_ref,
):
    flip = info[0]
    sib_refs = ((sib_a_ref, sib_b_ref), (sib_c_ref, sib_d_ref))
    part_ref[...] = dot(act_ref[...], proj_ref[...], 1, 1).astype(BF)
    base = own_ref.shape[1]
    units = own_ref.shape[2] // 2
    for kind, left, right in ((0, second_ref, dhid_ref), (1, dy_ref, act_ref)):
        for side in range(2):
            acc_ref[...] = dot(left[...], right[:, side * units : (side + 1) * units], 0, 0)
            for r in range(CHUNKS):
                at = pl.multiple_of((r ^ flip) * base, 32)
                block = acc_ref[pl.ds(at, base), :].astype(BF)
                if side:
                    sib_refs[kind][r // 4][r % 4] = block
                else:
                    own_ref[r, :, kind * units : (kind + 1) * units] = block
    one = jnp.ones((8, act_ref.shape[0]), BF)
    fc_sums = dot(one, dhid_ref[...], 1, 0)
    sums_ref[0:8, :] = fc_sums[:, 0:units]
    sums_ref[8:16, :] = fc_sums[:, units : 2 * units]
    sums_ref[16:24, :] = dot(one, dy_ref[...], 1, 0)


def attend_back_kernel(
    info,
    mid_ref,
    stat_ref,
    dy_ref,
    da_ref,
    recv_ref,
    vec_ref,
    wo_ref,
    mixed_ref,
    q_ref,
    k_ref,
    v_ref,
    probs_ref,
    dmid_ref,
    branch_ref,
    sums_ref,
    dq_ref,
    keep_ref,
    send_k_ref,
    send_v_ref,
    dm_ref,
    do_ref,
    dkt_ref,
    dvt_ref,
    dqh_ref,
    dp_ref,
    ds_ref,
    delta_ref,
):
    core = info[1]
    own_count = mid_ref.shape[0]
    heads = q_ref.shape[0]
    rows = k_ref.shape[1]
    gain = vec_ref[3:4, :]
    sums_ref[...] = jnp.zeros_like(sums_ref)
    sub = 32

    def first(at):
        rs = pl.ds(at, sub)
        factor = stat_ref[rs, TILE : TILE + 1]
        scaled = (mid_ref[rs, :] - stat_ref[rs, 0:1]) * factor
        incoming = da_ref[rs, :].astype(F32) + recv_ref[rs, :].astype(F32)
        dmid = dy_ref[rs, :].astype(F32) + norm_backward(incoming, scaled, factor, gain)
        dmid_ref[rs, :] = dmid
        low = dmid.astype(BF)
        branch_ref[rs, :] = low
        sums_ref[2:3, :] += colsum(low.astype(F32))
        sums_ref[3:4, :] += colsum(incoming * scaled)
        sums_ref[4:5, :] += colsum(incoming)

    loop(own_count, sub, first)
    dm_ref[...] = dot(branch_ref[...], wo_ref[...], 1, 0).astype(BF)
    for h in range(heads):
        cols = slice(h * HD, (h + 1) * HD)
        do_ref[h] = dm_ref[:, cols]
        delta_ref[h] = jnp.broadcast_to(
            jnp.sum(
                dm_ref[:, cols].astype(F32) * mixed_ref[:, cols].astype(F32), -1, keepdims=True
            ),
            (own_count, TILE),
        )
    scale = float(HD) ** -0.5

    def head(h, carry):
        for j in reversed(range(own_count // TILE)):
            end = (j + 1) * 2 * TILE
            off = TILE * j * (j + 1)
            rs = slice(j * TILE, (j + 1) * TILE)
            dp_ref[h, :, 0:end] = dot(do_ref[h, rs, :], v_ref[h, 0:end, :], 1, 1)
            for s in range(4):
                sl = slice(s * 32, s * 32 + 32)
                delta = delta_ref[h, j * TILE + s * 32 : j * TILE + s * 32 + 32, 0:1]
                p = probs_ref[h, sl, off : off + end].astype(F32)
                ds_ref[h, sl, 0:end] = (p * (dp_ref[h, sl, 0:end] - delta)).astype(BF)
            ds = ds_ref[h, :, 0:end]
            dqh_ref[h, rs, :] = dot(ds, k_ref[h, 0:end, :], 1, 0) * scale
            dk = dot(q_ref[h, rs, :], ds, 0, 0)
            dv = dot(do_ref[h, rs, :], probs_ref[h, :, off : off + end], 0, 0)
            if j == own_count // TILE - 1:
                dkt_ref[h] = dk
                dvt_ref[h] = dv
            else:
                dkt_ref[h, :, 0:end] += dk
                dvt_ref[h, :, 0:end] += dv
        return carry

    lax.fori_loop(0, heads, head, 0, unroll=2)
    width2 = heads * HD
    for h in range(heads):
        dq_ref[:, h * HD : (h + 1) * HD] = dqh_ref[h].astype(BF)
        twin = (h + heads // 2) % heads
        for j in range(own_count // TILE):
            mine = pl.multiple_of((2 * j + core) * TILE, TILE)
            yours = pl.multiple_of((2 * j + 1 - core) * TILE, TILE)
            cols = slice(j * TILE, (j + 1) * TILE)
            for part, ref, send in ((0, dkt_ref, send_k_ref), (1, dvt_ref, send_v_ref)):
                at = part * width2
                keep_ref[at + h * HD : at + (h + 1) * HD, cols] = ref[h, :, pl.ds(mine, TILE)]
                send[twin * HD : (twin + 1) * HD, cols] = ref[h, :, pl.ds(yours, TILE)].astype(BF)


def attn_grad_kernel(info, branch_ref, mixed_ref, out_ref):
    out_ref[...] = dot(branch_ref[...], mixed_ref[...], 0, 0)


def first_grad_kernel(
    info, dq_ref, keep_ref, got_k_ref, got_v_ref, wq_ref, wk_ref, wv_ref, part_ref, dkv_ref
):
    width2 = dq_ref.shape[1]
    for p, got in enumerate((got_k_ref, got_v_ref)):
        rows = slice(p * width2, (p + 1) * width2)
        dkv_ref[rows, :] = (keep_ref[rows, :] + got[...].astype(F32)).astype(BF)
    part_ref[...] = (
        dot(dq_ref[...], wq_ref[...], 1, 1)
        + dot(dkv_ref[0:width2, :], wk_ref[...], 0, 1)
        + dot(dkv_ref[width2 : 2 * width2, :], wv_ref[...], 0, 1)
    ).astype(BF)


def qkv_grad_kernel(
    info,
    first_ref,
    dq_ref,
    dkv_ref,
    attn_ref,
    part_ref,
    x_ref,
    stat_ref,
    mlp_sums_ref,
    att_sums_ref,
    own_ref,
    sib_a_ref,
    sib_b_ref,
    tile_own_ref,
    tile_sib_ref,
    whole_ref,
    sum_ref,
):
    flip, core = info[0], info[1]
    width2 = dq_ref.shape[1]
    width = width2 // 2
    base = own_ref.shape[1]
    for part in range(4):
        if part == 0:
            whole = dot(first_ref[...], dq_ref[...], 0, 0)
        elif part == 3:
            whole = attn_ref[...]
        else:
            whole = dot(
                first_ref[...], dkv_ref[(part - 1) * width2 : part * width2, :], 0, 1
            )
        whole_ref[...] = whole
        cols = slice(part * width, (part + 1) * width)
        for r in range(CHUNKS):
            at = pl.multiple_of((r ^ flip) * base, 32)
            block = whole_ref[pl.ds(at, base), :].astype(BF)
            own_ref[r, :, cols] = block[:, 0:width]
            (sib_a_ref, sib_b_ref)[r // 4][r % 4, :, cols] = block[:, width:width2]
    sum_ref[...] = jnp.zeros_like(sum_ref)

    def run(at):
        src = own_start(at, core)
        rs = pl.ds(src, 32)
        scaled = (x_ref[rs, :].astype(F32) - stat_ref[rs, 0:1]) * stat_ref[rs, TILE : TILE + 1]
        incoming = part_ref[pl.ds(at, 32), :].astype(F32)
        sum_ref[0:1, :] += colsum(incoming * scaled)
        sum_ref[1:2, :] += colsum(incoming)

    loop(part_ref.shape[0], 32, run)
    ones = jnp.ones((8, dq_ref.shape[0]), BF)
    qs = dot(ones, dq_ref[...], 1, 0)[0:1, :]
    vs = dot(ones, dkv_ref[width2 : 2 * width2, :], 1, 1)[0:1, :]
    sum_ref[2:5, :] = att_sums_ref[2:5, :]
    sum_ref[6:7, :] = mlp_sums_ref[16:17, :]
    for side, out in ((0, tile_own_ref), (1, tile_sib_ref)):
        sl = slice(side * width, (side + 1) * width)
        sum_ref[5:6, :] = mlp_sums_ref[8 * side : 8 * side + 1, :]
        sum_ref[7:8, 0:width] = qs[:, sl]
        sum_ref[7:8, width : 2 * width] = vs[:, sl]
        out[...] = sum_ref[...].astype(BF)


def final_kernel(info, x_ref, stat_ref, part_ref, recv_ref, dmid_ref, vec_ref, out_ref):
    core = info[1]
    gain = vec_ref[0:1, :]

    def run(at):
        src = own_start(at, core)
        rs = pl.ds(at, 32)
        factor = stat_ref[pl.ds(src, 32), TILE : TILE + 1]
        scaled = (x_ref[pl.ds(src, 32), :].astype(F32) - stat_ref[pl.ds(src, 32), 0:1]) * factor
        incoming = part_ref[rs, :].astype(F32) + recv_ref[rs, :].astype(F32)
        out_ref[rs, :] = (
            dmid_ref[rs, :] + norm_backward(incoming, scaled, factor, gain)
        ).astype(BF)

    loop(part_ref.shape[0], 32, run)


def output_kernel(info, seg_ref, mid_ref, part_ref, recv_ref, vec_ref, out_ref):
    core = info[1]
    bias = vec_ref[6:7, :]
    sub = 32
    lane = lax.broadcasted_iota(jnp.int32, (sub, TILE), 1)
    line = lax.broadcasted_iota(jnp.int32, (sub, TILE), 0)

    def run(at):
        tile_at = pl.multiple_of((2 * (at // TILE) + core) * TILE, TILE)
        seg_tile = jnp.broadcast_to(seg_ref[0:1, pl.ds(tile_at, TILE)], (sub, TILE))
        seg_col = jnp.max(
            jnp.where(lane == line + at % TILE, seg_tile, -2), -1, keepdims=True
        )
        rs = pl.ds(at, sub)
        final = (
            mid_ref[rs, :]
            + (part_ref[rs, :].astype(F32) + recv_ref[rs, :].astype(F32))
            + bias
        )
        out_ref[rs, :] = jnp.where(seg_col >= 0, final, 0.0).astype(BF)

    loop(part_ref.shape[0], sub, run)


def merge_kernel(info, own_ref, got_ref, out_ref):
    core = info[1]
    for j in range(own_ref.shape[0] // TILE):
        sl = slice(j * TILE, (j + 1) * TILE)
        mine = pl.multiple_of((2 * j + core) * TILE, TILE)
        yours = pl.multiple_of((2 * j + 1 - core) * TILE, TILE)
        out_ref[pl.ds(mine, TILE), :] = own_ref[sl, :]
        out_ref[pl.ds(yours, TILE), :] = got_ref[sl, :]


def all_rows(info, own):
    return call(
        merge_kernel,
        [shape((2 * own.shape[0], own.shape[1]))],
        info,
        own,
        swap_core(own),
        name="merge",
    )[0]


def scatter_first_kernel(pieces, info, own_ref, *refs):
    got_refs, refs = refs[:pieces], refs[pieces:]
    tiles, (keep_a, send_a, keep_b, send_b) = refs[:-4], refs[-4:]
    base = own_ref.shape[1]
    half = own_ref.shape[2] // 2
    for side, keep, send in ((0, keep_a, send_a), (1, keep_b, send_b)):
        cols = slice(side * half, (side + 1) * half)
        got_cols = cols if pieces == 2 else slice(0, half)
        kept, sent = 0, 0
        for r in range(CHUNKS):
            got = got_refs[r // 4 if pieces == 2 else 2 * side + r // 4]
            value = own_ref[r, :, cols].astype(F32) + got[r % 4, :, got_cols].astype(F32)
            if (r >> side) & 1:
                send[sent * base : (sent + 1) * base, :] = value.astype(BF)
                sent += 1
            else:
                keep[kept * base : (kept + 1) * base, :] = value
                kept += 1
        if tiles:
            value = tiles[0][:, cols].astype(F32) + tiles[1][:, cols].astype(F32)
            send[4 * base : 4 * base + EXTRA, :] = value.astype(BF)
            keep[4 * base : 4 * base + EXTRA, :] = value


def scatter_second_kernel(
    tiled, info, keep_a, got_a, keep_b, got_b, next_a, send_a, next_b, send_b
):
    extra = EXTRA if tiled else 0
    base = (keep_a.shape[0] - extra) // 4
    for keep, got, left, send, order in (
        (keep_a, got_a, next_a, send_a, (0, 1, 0, 1)),
        (keep_b, got_b, next_b, send_b, (0, 1, 0, 1)),
    ):
        kept, sent = 0, 0
        for r in range(4):
            rows = slice(r * base, (r + 1) * base)
            value = keep[rows, :] + got[rows, :].astype(F32)
            if order[r]:
                send[sent * base : (sent + 1) * base, :] = value.astype(BF)
                sent += 1
            else:
                left[kept * base : (kept + 1) * base, :] = value
                kept += 1
        if tiled:
            low = keep[4 * base : 4 * base + extra, :].astype(BF).astype(F32)
            value = low + got[4 * base : 4 * base + extra, :].astype(F32)
            send[2 * base : 2 * base + extra, :] = value.astype(BF)
            left[2 * base : 2 * base + extra, :] = value


def scatter_third_kernel(tiled, info, keep_a, got_a, keep_b, got_b, left, send):
    extra = EXTRA if tiled else 0
    base = (keep_a.shape[0] - extra) // 2
    half = keep_a.shape[1]
    for keep, got, at in ((keep_a, got_a, 0), (keep_b, got_b, half)):
        cols = slice(at, at + half)
        left[0:base, cols] = keep[0:base, :] + got[0:base, :].astype(F32)
        send[0:base, cols] = (
            keep[base : 2 * base, :] + got[base : 2 * base, :].astype(F32)
        ).astype(BF)
        if tiled:
            rows = slice(2 * base, 2 * base + extra)
            value = keep[rows, :].astype(BF).astype(F32) + got[rows, :].astype(F32)
            left[base : base + extra, cols] = value
            send[base : base + extra, cols] = value.astype(BF)


def scatter_big_kernel(info, left, got, fc_ref, proj_ref):
    units = fc_ref.shape[1]
    total = left[...] + got[...].astype(F32)
    fc_ref[...] = total[:, :units]
    proj_ref[...] = jnp.transpose(total[:, units:])


def scatter_small_kernel(info, left, got, qkv_ref, attn_ref, tile_ref):
    base = left.shape[0] - EXTRA
    width = qkv_ref.shape[2]
    total = left[0:base, :] + got[0:base, :].astype(F32)
    for p in range(3):
        qkv_ref[p] = total[:, p * width : (p + 1) * width]
    attn_ref[...] = jnp.transpose(total[:, 3 * width :])
    rows = slice(base, base + EXTRA)
    tile_ref[...] = left[rows, :].astype(BF).astype(F32) + got[rows, :].astype(F32)


def scatter_start(info, own, sib, tiles=(), after=()):
    base, columns = own.shape[1:]
    half = columns // 2
    rows = 4 * base + (EXTRA if tiles else 0)
    return call(
        functools.partial(scatter_first_kernel, len(sib)),
        [shape((rows, half), F32), shape((rows, half))] * 2,
        info,
        own,
        *[swap_core(piece) for piece in sib],
        *tiles,
        name="scatter_first",
        after=after,
    )


def scatter_send(state, bits):
    keep_a, send_a, keep_b, send_b = state
    return keep_a, swap_bit(send_a, bits[0]), keep_b, swap_bit(send_b, bits[1])


def scatter_middle(info, state, tiled, after=()):
    half = state[0].shape[1]
    extra = EXTRA if tiled else 0
    rows = (state[0].shape[0] - extra) // 2 + extra
    return call(
        functools.partial(scatter_second_kernel, tiled),
        [shape((rows, half), F32), shape((rows, half))] * 2,
        info,
        *state,
        name="scatter_second",
        after=after,
    )


def scatter_late(info, state, tiled, after=()):
    half = state[0].shape[1]
    extra = EXTRA if tiled else 0
    rows = (state[0].shape[0] - extra) // 2 + extra
    left, send = call(
        functools.partial(scatter_third_kernel, tiled),
        [shape((rows, 2 * half), F32), shape((rows, 2 * half))],
        info,
        *state,
        name="scatter_third",
        after=after,
    )
    return left, swap_bit(send, 2)


def scatter_plain(own, sib):
    if len(sib) == 4:
        sib = [jnp.concatenate([sib[i], sib[i + 2]], 2) for i in range(2)]
    sib = jnp.concatenate(sib, 0)
    total = own.astype(F32) + swap_core(sib).astype(F32)
    total = total.reshape(total.shape[0] * total.shape[1], total.shape[2])
    return lax.psum_scatter(total, "dp", scatter_dimension=0, tiled=True)


def body(
    inputs,
    segments,
    norm1_gain,
    norm1_shift,
    qkv_weight,
    qv_bias,
    attn_weight,
    attn_bias,
    norm2_gain,
    norm2_shift,
    fc_weight,
    fc_bias,
    proj_weight,
    proj_bias,
    cotangent,
):
    count = lax.axis_size("dp")
    index = lax.axis_index("dp")
    core = lax.axis_index("mp") % 2
    rows, depth = inputs.shape
    local = depth // count
    width = qkv_weight.shape[2]
    heads = width // HD
    units = fc_weight.shape[1]
    width2 = 2 * width
    heads2 = 2 * heads
    own_count = rows // 2
    base = depth // CHUNKS
    flip = index if count == CHUNKS else jnp.zeros_like(index)
    info = jnp.stack([flip, core]).astype(jnp.int32)
    seg_row = segments.reshape(1, rows)

    stat_one = call(
        stats_kernel, [shape((rows, 2 * TILE), F32)], info, inputs, name="stats"
    )[0]

    bias_width = qv_bias.shape[1]
    bias_rows = lax.dynamic_update_slice(
        jnp.zeros((heads, 2 * HD), BF), qv_bias, (0, index * bias_width)
    )
    bias_row = bias_rows.reshape(heads, 2, HD).transpose(1, 0, 2).reshape(1, width2)
    vectors = jnp.stack(
        [norm1_gain, norm1_shift, attn_bias, norm2_gain, norm2_shift, fc_bias[0], proj_bias]
    )
    placed = lax.dynamic_update_slice(
        jnp.zeros((vectors.shape[0], depth), BF), vectors, (0, index * local)
    )
    tile = jnp.concatenate(
        [
            placed,
            jnp.pad(bias_row, ((0, EXTRA - vectors.shape[0] - 1), (0, depth - width2))),
        ],
        0,
    )
    mats = jnp.concatenate(
        [qkv_weight.transpose(1, 0, 2).reshape(local, 3 * width), attn_weight.T], 1
    )
    wide = jnp.concatenate([fc_weight, proj_weight.T], 1)
    if count == CHUNKS:
        own_a = jnp.stack(gather_blocks(jnp.concatenate([mats, tile], 0), stat_one))
        wide = lax.optimization_barrier((wide, own_a))[0]
    else:
        full = lax.all_gather(mats, "dp", axis=0, tiled=True).reshape(CHUNKS, base, depth)
        total = jnp.sum(lax.all_gather(tile, "dp", axis=0).astype(F32), 0).astype(BF)
        total = jnp.pad(total[None], ((0, CHUNKS - 1), (0, 0), (0, 0)))
        own_a = jnp.concatenate([full, total], 1)
        own_b = lax.all_gather(wide, "dp", axis=0, tiled=True).reshape(CHUNKS, base, 2 * units)
        own_b = [own_b[r] for r in range(CHUNKS)]
    sib_a = swap_core(own_a)
    weight = shape((depth, width2))
    q, k, v, wq, wk, wv, wo, first_own, vec, vec_sib = call(
        project_kernel,
        [
            shape((heads2, own_count, HD)),
            shape((heads2, rows, HD)),
            shape((heads2, rows, HD)),
            weight,
            weight,
            weight,
            weight,
            shape((own_count, depth)),
            shape((EXTRA, depth), F32),
            shape((EXTRA, depth), F32),
        ],
        info,
        inputs,
        stat_one,
        own_a,
        sib_a,
        scratch=[pltpu.VMEM((rows, depth), BF), pltpu.VMEM((rows, width2), F32)],
        cost=8,
        name="project",
    )
    if count == CHUNKS:
        blocks = gather_blocks(wide, q)
    tiles = own_count // TILE
    part, mixed, probs = call(
        attend_kernel,
        [
            shape((own_count, depth)),
            shape((own_count, width2)),
            shape((heads2, TILE, TILE * tiles * (tiles + 1))),
        ],
        info,
        q,
        k,
        v,
        wo,
        seg_row,
        scratch=[
            pltpu.VMEM((heads2 + 1, TILE, rows), F32),
            pltpu.VMEM((heads2, own_count, HD), F32),
        ],
        cost=16,
        name="attend",
    )
    got = swap_chip(part)
    if count == CHUNKS:
        own_b = lax.optimization_barrier((blocks, part))[0]
    sib_b = [swap_core(block) for block in own_b]
    hid = shape((own_count, 2 * units))
    full = shape((depth, 2 * units))
    fc_full, proj_full, dy, dact = call(
        mlp_pre_kernel,
        [full, full, shape((own_count, depth)), hid],
        info,
        seg_row,
        cotangent,
        *own_b,
        *sib_b,
        name="mlp_pre",
    )
    da, act, dhid, second, middle, stat_two = call(
        mlp_kernel,
        [
            shape((own_count, depth)),
            hid,
            hid,
            shape((own_count, depth)),
            shape((own_count, depth), F32),
            shape((own_count, 2 * TILE), F32),
        ],
        info,
        inputs,
        part,
        got,
        vec,
        vec_sib,
        fc_full,
        dact,
        scratch=[pltpu.VMEM((own_count, units), F32)],
        cost=10,
        name="mlp",
    )
    da_got = swap_chip(da)
    mlp_part, grad_own, *grad_sib, mlp_sums = call(
        mlp_grad_kernel,
        [
            shape((own_count, depth)),
            shape((CHUNKS, base, 2 * units)),
            *[shape((CHUNKS // 2, base, units))] * 4,
            shape((24, depth), F32),
        ],
        info,
        act,
        dhid,
        second,
        dy,
        proj_full,
        scratch=[pltpu.VMEM((depth, units), F32)],
        cost=9,
        name="mlp_grad",
    )
    mlp_got = swap_chip(mlp_part)
    exact = count == CHUNKS
    if exact:
        big_state = scatter_start(info, grad_own, grad_sib)
        big_sent = big_state[1]
        big_state = scatter_send(big_state, (0, 1))
    else:
        big = scatter_plain(grad_own, grad_sib)
        fc_weight_grad, proj_weight_grad = big[:, :units], big[:, units:].T

    dmid, branch, att_sums, dq, keep, *send = call(
        attend_back_kernel,
        [
            shape((own_count, depth), F32),
            shape((own_count, depth)),
            shape((8, depth), F32),
            shape((own_count, width2)),
            shape((2 * width2, own_count), F32),
            *[shape((width2, own_count))] * 2,
        ],
        info,
        middle,
        stat_two,
        dy,
        da,
        da_got,
        vec,
        wo,
        mixed,
        q,
        k,
        v,
        probs,
        scratch=[
            pltpu.VMEM((own_count, width2), BF),
            pltpu.VMEM((heads2, own_count, HD), BF),
            pltpu.VMEM((heads2, HD, rows), F32),
            pltpu.VMEM((heads2, HD, rows), F32),
            pltpu.VMEM((heads2, own_count, HD), F32),
            pltpu.VMEM((heads2, TILE, rows), F32),
            pltpu.VMEM((heads2, TILE, rows), BF),
            pltpu.VMEM((heads2, own_count, TILE), F32),
        ],
        cost=18,
        name="attend_back",
        after=(big_sent,) if exact else (),
    )
    keep_got = [swap_core(piece) for piece in send]
    attn_full = call(
        attn_grad_kernel,
        [shape((depth, width2), F32)],
        info,
        branch,
        mixed,
        name="attn_grad",
        after=(mlp_got, big_state[1], big_state[3]) if exact else (),
    )[0]
    first_part, dkv = call(
        first_grad_kernel,
        [shape((own_count, depth)), shape((2 * width2, own_count))],
        info,
        dq,
        keep,
        *keep_got,
        wq,
        wk,
        wv,
        name="first_grad",
        after=(attn_full,),
    )
    first_got = swap_chip(first_part)
    qkv_own, *qkv_sib, tile_own, tile_sib = call(
        qkv_grad_kernel,
        [
            shape((CHUNKS, base, 4 * width)),
            *[shape((CHUNKS // 2, base, 4 * width))] * 2,
            *[shape((EXTRA, depth))] * 2,
        ],
        info,
        first_own,
        dq,
        dkv,
        attn_full,
        first_part,
        inputs,
        stat_one,
        mlp_sums,
        att_sums,
        scratch=[pltpu.VMEM((depth, width2), F32), pltpu.VMEM((EXTRA, depth), F32)],
        cost=7,
        name="qkv_grad",
    )
    finish = lambda after: call(
        final_kernel,
        [shape((own_count, depth))],
        info,
        inputs,
        stat_one,
        first_part,
        first_got,
        dmid,
        vec,
        name="final",
        after=after,
    )[0]
    tiles = (tile_own, swap_core(tile_sib))
    if exact:
        big_state = scatter_middle(info, big_state, False, after=(qkv_own,))
        small_state = scatter_start(info, qkv_own, qkv_sib, tiles, after=(big_state[0],))
        small_sent = small_state[1]
        big_state = scatter_send(big_state, (1, 0))
        small_state = scatter_send(small_state, (0, 1))
        big_last = scatter_late(info, big_state, False)
        inputs_low = finish((small_sent,))
        small_state = scatter_middle(info, small_state, True, after=(big_last[0], inputs_low))
        small_state = scatter_send(small_state, (1, 0))
        fc_weight_grad, proj_weight_grad = call(
            scatter_big_kernel,
            [shape((local, units), F32), shape((units, local), F32)],
            info,
            *big_last,
            name="scatter_big",
        )
        small_last = scatter_late(info, small_state, True)
        qkv_weight_grad, attn_weight_grad, tile = call(
            scatter_small_kernel,
            [
                shape((3, local, width), F32),
                shape((width, local), F32),
                shape((EXTRA, depth), F32),
            ],
            info,
            *small_last,
            name="scatter_small",
            after=(fc_weight_grad,),
        )
    else:
        inputs_low = finish(())
        mine = scatter_plain(qkv_own, qkv_sib)
        qkv_weight_grad = mine[:, : 3 * width].reshape(local, 3, width).transpose(1, 0, 2)
        attn_weight_grad = mine[:, 3 * width :].T
        tile = lax.psum(tiles[0].astype(F32) + tiles[1].astype(F32), "dp")
    tile_got = swap_chip(tile.astype(BF)).astype(F32)
    mask = (jnp.arange(EXTRA) < 2)[:, None]
    tile = jnp.where(mask, tile.astype(BF).astype(F32) + tile_got, tile)
    inputs_grad = all_rows(info, inputs_low)
    out_low = call(
        output_kernel,
        [shape((own_count, depth))],
        info,
        seg_row,
        middle,
        mlp_part,
        mlp_got,
        vec,
        name="output",
        after=(inputs_low,),
    )[0]
    outputs = all_rows(info, out_low)

    parts = lax.dynamic_slice(tile, (0, index * local), (7, local))
    bias_sum = tile[7, :width2].reshape(2, heads, HD).transpose(1, 0, 2).reshape(heads, 2 * HD)
    qv_bias_grad = lax.dynamic_slice(bias_sum, (0, index * bias_width), (heads, bias_width))
    return (
        outputs,
        inputs_grad,
        parts[0],
        parts[1],
        qkv_weight_grad,
        qv_bias_grad,
        attn_weight_grad,
        parts[2],
        parts[3],
        parts[4],
        fc_weight_grad,
        parts[5][None],
        proj_weight_grad,
        parts[6],
    )


def solution(mesh):
    return jax.shard_map(
        body,
        mesh=mesh,
        in_specs=(
            P("dp", None),
            P("dp"),
            P("dp"),
            P("dp"),
            P(None, "dp", "mp"),
            P("mp", "dp"),
            P("mp", "dp"),
            P("dp"),
            P("dp"),
            P("dp"),
            P("dp", "mp"),
            P("mp", "dp"),
            P("mp", "dp"),
            P("dp"),
            P("dp", None),
        ),
        out_specs=(
            P("dp", None),
            P("dp", None),
            P("dp"),
            P("dp"),
            P(None, "dp", "mp"),
            P("mp", "dp"),
            P("mp", "dp"),
            P("dp"),
            P("dp"),
            P("dp"),
            P("dp", "mp"),
            P("mp", "dp"),
            P("mp", "dp"),
            P("dp"),
        ),
        check_vma=False,
    )
```

```python
import functools

import jax
import jax.numpy as jnp
from jax import lax
from jax.experimental import pallas as pl
from jax.experimental.pallas import tpu as pltpu
from jax.sharding import PartitionSpec as P

HD = 64
TILE = 128
EXTRA = 16
CHUNKS = 8
EPSILON = 1e-05
NEGATIVE = -1e30
BF = jnp.bfloat16
F32 = jnp.float32
CORE_PAIRS = ((0, 1), (1, 0), (2, 3), (3, 2))
CHIP_PAIRS = ((0, 2), (2, 0), (1, 3), (3, 1))
CURVE = 0.7978845608028654


def dot(left, right, left_dim, right_dim):
    return lax.dot_general(
        left, right, (((left_dim,), (right_dim,)), ((), ())), preferred_element_type=F32
    )


def swap_core(value):
    return lax.ppermute(value, "mp", CORE_PAIRS)


def swap_chip(value):
    return lax.ppermute(value, "mp", CHIP_PAIRS)


def swap_mask(value, mask):
    return lax.ppermute(value, "dp", [(i, i ^ mask) for i in range(CHUNKS)])


def swap_bit(value, bit):
    return swap_mask(value, 1 << bit)


def call(kernel, outs, *args, scratch=(), smem=1, cost=0, name=None, after=()):
    first, behind = len(args), len(args) + len(after)

    def run(*refs):
        kernel(*refs[:first], *refs[behind:])

    specs = [pl.BlockSpec(memory_space=pltpu.SMEM)] * smem
    specs += [pl.BlockSpec(memory_space=pltpu.VMEM)] * (len(args) - smem)
    specs += [pl.BlockSpec(memory_space=pl.ANY)] * len(after)
    return pl.pallas_call(
        run,
        out_shape=outs,
        in_specs=specs,
        out_specs=[pl.BlockSpec(memory_space=pltpu.VMEM)] * len(outs),
        scratch_shapes=list(scratch),
        compiler_params=pltpu.CompilerParams(vmem_limit_bytes=56 * 1024 * 1024),
        cost_estimate=pl.CostEstimate(flops=cost * 10**9, bytes_accessed=1024, transcendentals=0),
        name=name,
    )(*args, *after)


def shape(dims, dtype=BF):
    return jax.ShapeDtypeStruct(tuple(dims), dtype)


def gather_blocks(message, behind, far=None):
    got = {0: message}
    got[4] = swap_mask(message, 4) if far is None else far
    got[2] = swap_mask(message, 2)
    got[1] = swap_mask(message, 1)
    four, two = lax.optimization_barrier((got[4], got[2], behind))[:2]
    got[7] = swap_mask(four, 3)
    got[5] = swap_mask(four, 1)
    got[6] = swap_mask(four, 2)
    got[3] = swap_mask(two, 1)
    return [got[r] for r in range(CHUNKS)]


def loop(count, step, fn, unroll=4):
    def run(i, carry):
        fn(pl.multiple_of(i * step, step))
        return carry

    lax.fori_loop(0, count // step, run, 0, unroll=unroll)


def norm_backward(incoming, scaled, factor, gain):
    weighted = incoming * gain
    first_mean = jnp.mean(weighted, -1, keepdims=True)
    second_mean = jnp.mean(weighted * scaled, -1, keepdims=True)
    return factor * (weighted - first_mean - scaled * second_mean)


def tile_sum(ref, base):
    total = ref[0, base : base + EXTRA, :].astype(F32)
    for r in range(1, CHUNKS):
        total = total + ref[r, base : base + EXTRA, :].astype(F32)
    return total


def own_start(start, core):
    tile = start // TILE
    return pl.multiple_of((2 * tile + core) * TILE + start % TILE, 32)


def colsum(value):
    return jnp.sum(value, 0, keepdims=True)


def spread_stats(value):
    average = jnp.mean(value, -1, keepdims=True)
    centred = value - average
    factor = lax.rsqrt(jnp.mean(centred * centred, -1, keepdims=True) + EPSILON)
    rows = value.shape[0]
    return jnp.concatenate(
        [jnp.broadcast_to(average, (rows, TILE)), jnp.broadcast_to(factor, (rows, TILE))], 1
    )


def stats_kernel(info, x_ref, stat_ref):
    def run(at):
        rs = pl.ds(at, 32)
        stat_ref[rs, :] = spread_stats(x_ref[rs, :].astype(F32))

    loop(x_ref.shape[0], 32, run)


def project_kernel(
    info,
    x_ref,
    stat_ref,
    own_ref,
    sib_ref,
    q_ref,
    k_ref,
    v_ref,
    wq_ref,
    wk_ref,
    wv_ref,
    wo_ref,
    firstown_ref,
    vec_ref,
    vecsib_ref,
    low_ref,
    proj_ref,
):
    flip, core = info[0], info[1]
    width = own_ref.shape[2] // 4
    base = own_ref.shape[1] - EXTRA
    rows = low_ref.shape[0]
    heads = 2 * width // HD
    own_count = rows // 2
    vec_ref[...] = tile_sum(own_ref, base)
    vecsib_ref[...] = tile_sum(sib_ref, base)
    gain, shift = vec_ref[0:1, :], vec_ref[1:2, :]

    def norm(at):
        rs = pl.ds(at, 32)
        scaled = (x_ref[rs, :].astype(F32) - stat_ref[rs, 0:1]) * stat_ref[rs, TILE : TILE + 1]
        low_ref[rs, :] = (scaled * gain + shift).astype(BF)

    loop(rows, 32, norm)
    for r in range(CHUNKS):
        at = pl.multiple_of((r ^ flip) * base, 32)
        for side, ref in ((0, own_ref), (1, sib_ref)):
            for part, out in enumerate((wq_ref, wk_ref, wv_ref, wo_ref)):
                out[pl.ds(at, base), side * width : (side + 1) * width] = ref[
                    r, 0:base, part * width : (part + 1) * width
                ]
    bias_q = jnp.concatenate([vec_ref[7:8, :width], vecsib_ref[7:8, :width]], 1)
    bias_v = jnp.concatenate(
        [vec_ref[7:8, width : 2 * width], vecsib_ref[7:8, width : 2 * width]], 1
    )
    for j in range(own_count // TILE):
        at = own_start(j * TILE, core)
        firstown_ref[j * TILE : (j + 1) * TILE, :] = low_ref[pl.ds(at, TILE), :]
    scale = float(HD) ** -0.5
    proj_ref[0:own_count, :] = dot(firstown_ref[...], wq_ref[...], 1, 0) + bias_q
    for h in range(heads):
        q_ref[h] = (
            proj_ref[0:own_count, h * HD : (h + 1) * HD].astype(BF).astype(F32) * scale
        ).astype(BF)
    proj_ref[...] = dot(low_ref[...], wk_ref[...], 1, 0)
    for h in range(heads):
        k_ref[h] = proj_ref[:, h * HD : (h + 1) * HD].astype(BF)
    proj_ref[...] = dot(low_ref[...], wv_ref[...], 1, 0) + bias_v
    for h in range(heads):
        v_ref[h] = proj_ref[:, h * HD : (h + 1) * HD].astype(BF)


def attend_kernel(
    info, q_ref, k_ref, v_ref, wo_ref, seg_ref, part_ref, mixed_ref, probs_ref, s_ref, o_ref
):
    core = info[1]
    heads, own_count = q_ref.shape[:2]
    lane = lax.broadcasted_iota(jnp.int32, (TILE, TILE), 1)
    line = lax.broadcasted_iota(jnp.int32, (TILE, TILE), 0)
    for j in range(own_count // TILE):
        end = (j + 1) * 2 * TILE
        off = TILE * j * (j + 1)
        at = own_start(j * TILE, core)
        seg_tile = jnp.broadcast_to(seg_ref[0:1, pl.ds(at, TILE)], (TILE, TILE))
        seg_col = jnp.max(jnp.where(lane == line, seg_tile, -2), -1, keepdims=True)
        place = lax.broadcasted_iota(jnp.int32, (TILE, end), 1)
        own_place = at + lax.broadcasted_iota(jnp.int32, (TILE, end), 0)
        allowed = (seg_col == seg_ref[0:1, 0:end]) & (place <= own_place)
        bias = jnp.where(allowed, 0.0, NEGATIVE)
        s_ref[heads, :, 0:end] = bias

        def run(h, carry, j=j, end=end, off=off):
            scores = dot(q_ref[h, j * TILE : (j + 1) * TILE, :], k_ref[h, 0:end, :], 1, 1)
            s_ref[h, :, 0:end] = scores
            for sub in range(4):
                sl = slice(sub * 32, sub * 32 + 32)
                sc = s_ref[h, sl, 0:end] + s_ref[heads, sl, 0:end]
                weights = jnp.exp(sc - jnp.max(sc, -1, keepdims=True))
                inverse = 1.0 / jnp.sum(weights, -1, keepdims=True)
                probs_ref[h, sl, off : off + end] = (weights * inverse).astype(BF)
            o_ref[h, j * TILE : (j + 1) * TILE, :] = dot(
                probs_ref[h, :, off : off + end], v_ref[h, 0:end, :], 1, 0
            )
            return carry

        lax.fori_loop(0, heads, run, 0, unroll=True)
    for h in range(heads):
        mixed_ref[:, h * HD : (h + 1) * HD] = o_ref[h].astype(BF)
    part_ref[...] = dot(mixed_ref[...], wo_ref[...], 1, 1).astype(BF)


def mlp_pre_kernel(info, seg_ref, cot_ref, *refs):
    own_refs, sib_refs = refs[:CHUNKS], refs[CHUNKS : 2 * CHUNKS]
    fc_ref, proj_ref, dy_ref, dact_ref = refs[2 * CHUNKS :]
    flip, core = info[0], info[1]
    own_count = dy_ref.shape[0]
    base = own_refs[0].shape[0]
    units = own_refs[0].shape[1] // 2
    sub = 32
    lane = lax.broadcasted_iota(jnp.int32, (sub, TILE), 1)
    line = lax.broadcasted_iota(jnp.int32, (sub, TILE), 0)

    def mask(at):
        src = own_start(at, core)
        tile_at = pl.multiple_of((2 * (at // TILE) + core) * TILE, TILE)
        seg_tile = jnp.broadcast_to(seg_ref[0:1, pl.ds(tile_at, TILE)], (sub, TILE))
        seg_col = jnp.max(
            jnp.where(lane == line + at % TILE, seg_tile, -2), -1, keepdims=True
        )
        cot = cot_ref[pl.ds(src, sub), :].astype(F32)
        dy_ref[pl.ds(at, sub), :] = jnp.where(seg_col >= 0, cot, 0.0).astype(BF)

    loop(own_count, sub, mask)
    for r in range(CHUNKS):
        at = pl.multiple_of((r ^ flip) * base, 32)
        for side, ref in ((0, own_refs[r]), (1, sib_refs[r])):
            cols = slice(side * units, (side + 1) * units)
            fc_ref[pl.ds(at, base), cols] = ref[:, 0:units]
            proj_ref[pl.ds(at, base), cols] = ref[:, units : 2 * units]
    for side in range(2):
        cols = slice(side * units, (side + 1) * units)
        dact_ref[:, cols] = dot(dy_ref[...], proj_ref[:, cols], 1, 0).astype(BF)


def mlp_kernel(
    info,
    x_ref,
    part_ref,
    recv_ref,
    vec_ref,
    vecsib_ref,
    fc_ref,
    dact_ref,
    da_ref,
    act_ref,
    dhid_ref,
    second_ref,
    mid_ref,
    stat_ref,
    hid_ref,
):
    core = info[1]
    own_count = part_ref.shape[0]
    units = fc_ref.shape[1] // 2
    gain, shift, bias = vec_ref[3:4, :], vec_ref[4:5, :], vec_ref[2:3, :]
    sub = 32

    def first(at):
        src = own_start(at, core)
        rows = pl.ds(at, sub)
        middle = (
            x_ref[pl.ds(src, sub), :].astype(F32)
            + (part_ref[rows, :].astype(F32) + recv_ref[rows, :].astype(F32))
            + bias
        )
        mid_ref[rows, :] = middle
        stats = spread_stats(middle)
        stat_ref[rows, :] = stats
        scaled = (middle - stats[:, 0:1]) * stats[:, TILE : TILE + 1]
        second_ref[rows, :] = (scaled * gain + shift).astype(BF)

    loop(own_count, sub, first)
    for side, biases in ((0, vec_ref), (1, vecsib_ref)):
        cols = slice(side * units, (side + 1) * units)
        hid_ref[...] = dot(second_ref[...], fc_ref[:, cols], 1, 0)
        bias_fc = biases[5:6, :]

        def gelu(at, cols=cols, bias_fc=bias_fc):
            rows = pl.ds(at, 16)
            u = hid_ref[rows, :] + bias_fc
            u2 = u * u
            bend = jnp.tanh(CURVE * u * (1.0 + 0.044715 * u2))
            half = 0.5 * (1.0 + bend)
            act_ref[rows, cols] = (u * half).astype(BF)
            slope = half + (0.5 * CURVE) * u * (1.0 - bend * bend) * (1.0 + 0.134145 * u2)
            dhid_ref[rows, cols] = (dact_ref[rows, cols].astype(F32) * slope).astype(BF)

        loop(own_count, 16, gelu)
    da_ref[...] = dot(dhid_ref[...], fc_ref[...], 1, 1).astype(BF)


def mlp_grad_kernel(
    info,
    act_ref,
    dhid_ref,
    second_ref,
    dy_ref,
    proj_ref,
    part_ref,
    own_ref,
    sib_a_ref,
    sib_b_ref,
    sib_c_ref,
    sib_d_ref,
    sums_ref,
    acc_ref,
):
    flip = info[0]
    sib_refs = ((sib_a_ref, sib_b_ref), (sib_c_ref, sib_d_ref))
    part_ref[...] = dot(act_ref[...], proj_ref[...], 1, 1).astype(BF)
    base = own_ref.shape[1]
    units = own_ref.shape[2] // 2
    for kind, left, right in ((0, second_ref, dhid_ref), (1, dy_ref, act_ref)):
        for side in range(2):
            acc_ref[...] = dot(left[...], right[:, side * units : (side + 1) * units], 0, 0)
            for r in range(CHUNKS):
                at = pl.multiple_of((r ^ flip) * base, 32)
                block = acc_ref[pl.ds(at, base), :].astype(BF)
                if side:
                    sib_refs[kind][r // 4][r % 4] = block
                else:
                    own_ref[r, :, kind * units : (kind + 1) * units] = block
    one = jnp.ones((8, act_ref.shape[0]), BF)
    fc_sums = dot(one, dhid_ref[...], 1, 0)
    sums_ref[0:8, :] = fc_sums[:, 0:units]
    sums_ref[8:16, :] = fc_sums[:, units : 2 * units]
    sums_ref[16:24, :] = dot(one, dy_ref[...], 1, 0)


def attend_back_kernel(
    info,
    mid_ref,
    stat_ref,
    dy_ref,
    da_ref,
    recv_ref,
    vec_ref,
    wo_ref,
    mixed_ref,
    q_ref,
    k_ref,
    v_ref,
    probs_ref,
    dmid_ref,
    branch_ref,
    sums_ref,
    dq_ref,
    keep_ref,
    send_k_ref,
    send_v_ref,
    dm_ref,
    do_ref,
    dkt_ref,
    dvt_ref,
    dqh_ref,
    dp_ref,
    ds_ref,
    delta_ref,
):
    core = info[1]
    own_count = mid_ref.shape[0]
    heads = q_ref.shape[0]
    rows = k_ref.shape[1]
    gain = vec_ref[3:4, :]
    sums_ref[...] = jnp.zeros_like(sums_ref)
    sub = 32

    def first(at):
        rs = pl.ds(at, sub)
        factor = stat_ref[rs, TILE : TILE + 1]
        scaled = (mid_ref[rs, :] - stat_ref[rs, 0:1]) * factor
        incoming = da_ref[rs, :].astype(F32) + recv_ref[rs, :].astype(F32)
        dmid = dy_ref[rs, :].astype(F32) + norm_backward(incoming, scaled, factor, gain)
        dmid_ref[rs, :] = dmid
        low = dmid.astype(BF)
        branch_ref[rs, :] = low
        sums_ref[2:3, :] += colsum(low.astype(F32))
        sums_ref[3:4, :] += colsum(incoming * scaled)
        sums_ref[4:5, :] += colsum(incoming)

    loop(own_count, sub, first)
    dm_ref[...] = dot(branch_ref[...], wo_ref[...], 1, 0).astype(BF)
    for h in range(heads):
        cols = slice(h * HD, (h + 1) * HD)
        do_ref[h] = dm_ref[:, cols]
        delta_ref[h] = jnp.broadcast_to(
            jnp.sum(
                dm_ref[:, cols].astype(F32) * mixed_ref[:, cols].astype(F32), -1, keepdims=True
            ),
            (own_count, TILE),
        )
    scale = float(HD) ** -0.5

    def head(h, carry):
        for j in reversed(range(own_count // TILE)):
            end = (j + 1) * 2 * TILE
            off = TILE * j * (j + 1)
            rs = slice(j * TILE, (j + 1) * TILE)
            dp_ref[h, :, 0:end] = dot(do_ref[h, rs, :], v_ref[h, 0:end, :], 1, 1)
            for s in range(4):
                sl = slice(s * 32, s * 32 + 32)
                delta = delta_ref[h, j * TILE + s * 32 : j * TILE + s * 32 + 32, 0:1]
                p = probs_ref[h, sl, off : off + end].astype(F32)
                ds_ref[h, sl, 0:end] = (p * (dp_ref[h, sl, 0:end] - delta)).astype(BF)
            ds = ds_ref[h, :, 0:end]
            dqh_ref[h, rs, :] = dot(ds, k_ref[h, 0:end, :], 1, 0) * scale
            dk = dot(q_ref[h, rs, :], ds, 0, 0)
            dv = dot(do_ref[h, rs, :], probs_ref[h, :, off : off + end], 0, 0)
            if j == own_count // TILE - 1:
                dkt_ref[h] = dk
                dvt_ref[h] = dv
            else:
                dkt_ref[h, :, 0:end] += dk
                dvt_ref[h, :, 0:end] += dv
        return carry

    lax.fori_loop(0, heads, head, 0, unroll=2)
    width2 = heads * HD
    for h in range(heads):
        dq_ref[:, h * HD : (h + 1) * HD] = dqh_ref[h].astype(BF)
        twin = (h + heads // 2) % heads
        for j in range(own_count // TILE):
            mine = pl.multiple_of((2 * j + core) * TILE, TILE)
            yours = pl.multiple_of((2 * j + 1 - core) * TILE, TILE)
            cols = slice(j * TILE, (j + 1) * TILE)
            for part, ref, send in ((0, dkt_ref, send_k_ref), (1, dvt_ref, send_v_ref)):
                at = part * width2
                keep_ref[at + h * HD : at + (h + 1) * HD, cols] = ref[h, :, pl.ds(mine, TILE)]
                send[twin * HD : (twin + 1) * HD, cols] = ref[h, :, pl.ds(yours, TILE)].astype(BF)


def attn_grad_kernel(info, branch_ref, mixed_ref, out_ref):
    out_ref[...] = dot(branch_ref[...], mixed_ref[...], 0, 0)


def first_grad_kernel(
    info, dq_ref, keep_ref, got_k_ref, got_v_ref, wq_ref, wk_ref, wv_ref, part_ref, dkv_ref
):
    width2 = dq_ref.shape[1]
    for p, got in enumerate((got_k_ref, got_v_ref)):
        rows = slice(p * width2, (p + 1) * width2)
        dkv_ref[rows, :] = (keep_ref[rows, :] + got[...].astype(F32)).astype(BF)
    part_ref[...] = (
        dot(dq_ref[...], wq_ref[...], 1, 1)
        + dot(dkv_ref[0:width2, :], wk_ref[...], 0, 1)
        + dot(dkv_ref[width2 : 2 * width2, :], wv_ref[...], 0, 1)
    ).astype(BF)


def qkv_grad_kernel(
    info,
    first_ref,
    dq_ref,
    dkv_ref,
    attn_ref,
    part_ref,
    x_ref,
    stat_ref,
    mlp_sums_ref,
    att_sums_ref,
    own_ref,
    sib_a_ref,
    sib_b_ref,
    tile_own_ref,
    tile_sib_ref,
    whole_ref,
    sum_ref,
):
    flip, core = info[0], info[1]
    width2 = dq_ref.shape[1]
    width = width2 // 2
    base = own_ref.shape[1]
    for part in range(4):
        if part == 0:
            whole = dot(first_ref[...], dq_ref[...], 0, 0)
        elif part == 3:
            whole = attn_ref[...]
        else:
            whole = dot(
                first_ref[...], dkv_ref[(part - 1) * width2 : part * width2, :], 0, 1
            )
        whole_ref[...] = whole
        cols = slice(part * width, (part + 1) * width)
        for r in range(CHUNKS):
            at = pl.multiple_of((r ^ flip) * base, 32)
            block = whole_ref[pl.ds(at, base), :].astype(BF)
            own_ref[r, :, cols] = block[:, 0:width]
            (sib_a_ref, sib_b_ref)[r // 4][r % 4, :, cols] = block[:, width:width2]
    sum_ref[...] = jnp.zeros_like(sum_ref)

    def run(at):
        src = own_start(at, core)
        rs = pl.ds(src, 32)
        scaled = (x_ref[rs, :].astype(F32) - stat_ref[rs, 0:1]) * stat_ref[rs, TILE : TILE + 1]
        incoming = part_ref[pl.ds(at, 32), :].astype(F32)
        sum_ref[0:1, :] += colsum(incoming * scaled)
        sum_ref[1:2, :] += colsum(incoming)

    loop(part_ref.shape[0], 32, run)
    ones = jnp.ones((8, dq_ref.shape[0]), BF)
    qs = dot(ones, dq_ref[...], 1, 0)[0:1, :]
    vs = dot(ones, dkv_ref[width2 : 2 * width2, :], 1, 1)[0:1, :]
    sum_ref[2:5, :] = att_sums_ref[2:5, :]
    sum_ref[6:7, :] = mlp_sums_ref[16:17, :]
    for side, out in ((0, tile_own_ref), (1, tile_sib_ref)):
        sl = slice(side * width, (side + 1) * width)
        sum_ref[5:6, :] = mlp_sums_ref[8 * side : 8 * side + 1, :]
        sum_ref[7:8, 0:width] = qs[:, sl]
        sum_ref[7:8, width : 2 * width] = vs[:, sl]
        out[...] = sum_ref[...].astype(BF)


def final_kernel(info, x_ref, stat_ref, part_ref, recv_ref, dmid_ref, vec_ref, out_ref):
    core = info[1]
    gain = vec_ref[0:1, :]

    def run(at):
        src = own_start(at, core)
        rs = pl.ds(at, 32)
        factor = stat_ref[pl.ds(src, 32), TILE : TILE + 1]
        scaled = (x_ref[pl.ds(src, 32), :].astype(F32) - stat_ref[pl.ds(src, 32), 0:1]) * factor
        incoming = part_ref[rs, :].astype(F32) + recv_ref[rs, :].astype(F32)
        out_ref[rs, :] = (
            dmid_ref[rs, :] + norm_backward(incoming, scaled, factor, gain)
        ).astype(BF)

    loop(part_ref.shape[0], 32, run)


def output_kernel(info, seg_ref, mid_ref, part_ref, recv_ref, vec_ref, out_ref):
    core = info[1]
    bias = vec_ref[6:7, :]
    sub = 32
    lane = lax.broadcasted_iota(jnp.int32, (sub, TILE), 1)
    line = lax.broadcasted_iota(jnp.int32, (sub, TILE), 0)

    def run(at):
        tile_at = pl.multiple_of((2 * (at // TILE) + core) * TILE, TILE)
        seg_tile = jnp.broadcast_to(seg_ref[0:1, pl.ds(tile_at, TILE)], (sub, TILE))
        seg_col = jnp.max(
            jnp.where(lane == line + at % TILE, seg_tile, -2), -1, keepdims=True
        )
        rs = pl.ds(at, sub)
        final = (
            mid_ref[rs, :]
            + (part_ref[rs, :].astype(F32) + recv_ref[rs, :].astype(F32))
            + bias
        )
        out_ref[rs, :] = jnp.where(seg_col >= 0, final, 0.0).astype(BF)

    loop(part_ref.shape[0], sub, run)


def merge_kernel(info, own_ref, got_ref, out_ref):
    core = info[1]
    for j in range(own_ref.shape[0] // TILE):
        sl = slice(j * TILE, (j + 1) * TILE)
        mine = pl.multiple_of((2 * j + core) * TILE, TILE)
        yours = pl.multiple_of((2 * j + 1 - core) * TILE, TILE)
        out_ref[pl.ds(mine, TILE), :] = own_ref[sl, :]
        out_ref[pl.ds(yours, TILE), :] = got_ref[sl, :]


def all_rows(info, own, after=()):
    return call(
        merge_kernel,
        [shape((2 * own.shape[0], own.shape[1]))],
        info,
        own,
        swap_core(own),
        name="merge",
        cost=3,
        after=after,
    )[0]


def scatter_first_kernel(pieces, info, own_ref, *refs):
    got_refs, refs = refs[:pieces], refs[pieces:]
    tiles, (keep_a, send_a, keep_b, send_b) = refs[:-4], refs[-4:]
    base = own_ref.shape[1]
    half = own_ref.shape[2] // 2
    for side, keep, send in ((0, keep_a, send_a), (1, keep_b, send_b)):
        cols = slice(side * half, (side + 1) * half)
        got_cols = cols if pieces == 2 else slice(0, half)
        kept, sent = 0, 0
        for r in range(CHUNKS):
            got = got_refs[r // 4 if pieces == 2 else 2 * side + r // 4]
            value = own_ref[r, :, cols].astype(F32) + got[r % 4, :, got_cols].astype(F32)
            if (r >> side) & 1:
                send[sent * base : (sent + 1) * base, :] = value.astype(BF)
                sent += 1
            else:
                keep[kept * base : (kept + 1) * base, :] = value
                kept += 1
        if tiles:
            value = tiles[0][:, cols].astype(F32) + tiles[1][:, cols].astype(F32)
            send[4 * base : 4 * base + EXTRA, :] = value.astype(BF)
            keep[4 * base : 4 * base + EXTRA, :] = value


def scatter_second_kernel(
    tiled, info, keep_a, got_a, keep_b, got_b, next_a, send_a, next_b, send_b
):
    extra = EXTRA if tiled else 0
    base = (keep_a.shape[0] - extra) // 4
    for keep, got, left, send, order in (
        (keep_a, got_a, next_a, send_a, (0, 1, 0, 1)),
        (keep_b, got_b, next_b, send_b, (0, 1, 0, 1)),
    ):
        kept, sent = 0, 0
        for r in range(4):
            rows = slice(r * base, (r + 1) * base)
            value = keep[rows, :] + got[rows, :].astype(F32)
            if order[r]:
                send[sent * base : (sent + 1) * base, :] = value.astype(BF)
                sent += 1
            else:
                left[kept * base : (kept + 1) * base, :] = value
                kept += 1
        if tiled:
            low = keep[4 * base : 4 * base + extra, :].astype(BF).astype(F32)
            value = low + got[4 * base : 4 * base + extra, :].astype(F32)
            send[2 * base : 2 * base + extra, :] = value.astype(BF)
            left[2 * base : 2 * base + extra, :] = value


def scatter_third_kernel(tiled, info, keep_a, got_a, keep_b, got_b, left, send):
    extra = EXTRA if tiled else 0
    base = (keep_a.shape[0] - extra) // 2
    half = keep_a.shape[1]
    for keep, got, at in ((keep_a, got_a, 0), (keep_b, got_b, half)):
        cols = slice(at, at + half)
        left[0:base, cols] = keep[0:base, :] + got[0:base, :].astype(F32)
        send[0:base, cols] = (
            keep[base : 2 * base, :] + got[base : 2 * base, :].astype(F32)
        ).astype(BF)
        if tiled:
            rows = slice(2 * base, 2 * base + extra)
            value = keep[rows, :].astype(BF).astype(F32) + got[rows, :].astype(F32)
            left[base : base + extra, cols] = value
            send[base : base + extra, cols] = value.astype(BF)


def scatter_big_kernel(info, left, got, fc_ref, proj_ref):
    units = fc_ref.shape[1]
    total = left[...] + got[...].astype(F32)
    fc_ref[...] = total[:, :units]
    proj_ref[...] = jnp.transpose(total[:, units:])


def scatter_small_kernel(info, left, got, qkv_ref, attn_ref, tile_ref):
    base = left.shape[0] - EXTRA
    width = qkv_ref.shape[2]
    total = left[0:base, :] + got[0:base, :].astype(F32)
    for p in range(3):
        qkv_ref[p] = total[:, p * width : (p + 1) * width]
    attn_ref[...] = jnp.transpose(total[:, 3 * width :])
    rows = slice(base, base + EXTRA)
    tile_ref[...] = left[rows, :].astype(BF).astype(F32) + got[rows, :].astype(F32)


def scatter_start(info, own, sib, tiles=(), after=()):
    base, columns = own.shape[1:]
    half = columns // 2
    rows = 4 * base + (EXTRA if tiles else 0)
    return call(
        functools.partial(scatter_first_kernel, len(sib)),
        [shape((rows, half), F32), shape((rows, half))] * 2,
        info,
        own,
        *[swap_core(piece) for piece in sib],
        *tiles,
        name="scatter_first",
        after=after,
    )


def scatter_send(state, bits):
    keep_a, send_a, keep_b, send_b = state
    return keep_a, swap_bit(send_a, bits[0]), keep_b, swap_bit(send_b, bits[1])


def scatter_middle(info, state, tiled, after=()):
    half = state[0].shape[1]
    extra = EXTRA if tiled else 0
    rows = (state[0].shape[0] - extra) // 2 + extra
    return call(
        functools.partial(scatter_second_kernel, tiled),
        [shape((rows, half), F32), shape((rows, half))] * 2,
        info,
        *state,
        name="scatter_second",
        cost=2 if tiled else 0,
        after=after,
    )


def scatter_late(info, state, tiled, after=()):
    half = state[0].shape[1]
    extra = EXTRA if tiled else 0
    rows = (state[0].shape[0] - extra) // 2 + extra
    left, send = call(
        functools.partial(scatter_third_kernel, tiled),
        [shape((rows, 2 * half), F32), shape((rows, 2 * half))],
        info,
        *state,
        name="scatter_third",
        cost=2 if tiled else 0,
        after=after,
    )
    return left, swap_bit(send, 2)


def scatter_plain(own, sib):
    if len(sib) == 4:
        sib = [jnp.concatenate([sib[i], sib[i + 2]], 2) for i in range(2)]
    sib = jnp.concatenate(sib, 0)
    total = own.astype(F32) + swap_core(sib).astype(F32)
    total = total.reshape(total.shape[0] * total.shape[1], total.shape[2])
    return lax.psum_scatter(total, "dp", scatter_dimension=0, tiled=True)


def body(
    inputs,
    segments,
    norm1_gain,
    norm1_shift,
    qkv_weight,
    qv_bias,
    attn_weight,
    attn_bias,
    norm2_gain,
    norm2_shift,
    fc_weight,
    fc_bias,
    proj_weight,
    proj_bias,
    cotangent,
):
    count = lax.axis_size("dp")
    index = lax.axis_index("dp")
    core = lax.axis_index("mp") % 2
    rows, depth = inputs.shape
    local = depth // count
    width = qkv_weight.shape[2]
    heads = width // HD
    units = fc_weight.shape[1]
    width2 = 2 * width
    heads2 = 2 * heads
    own_count = rows // 2
    base = depth // CHUNKS
    flip = index if count == CHUNKS else jnp.zeros_like(index)
    info = jnp.stack([flip, core]).astype(jnp.int32)
    seg_row = segments.reshape(1, rows)

    stat_one = call(
        stats_kernel, [shape((rows, 2 * TILE), F32)], info, inputs, name="stats"
    )[0]

    bias_width = qv_bias.shape[1]
    bias_rows = lax.dynamic_update_slice(
        jnp.zeros((heads, 2 * HD), BF), qv_bias, (0, index * bias_width)
    )
    bias_row = bias_rows.reshape(heads, 2, HD).transpose(1, 0, 2).reshape(1, width2)
    vectors = jnp.stack(
        [norm1_gain, norm1_shift, attn_bias, norm2_gain, norm2_shift, fc_bias[0], proj_bias]
    )
    placed = lax.dynamic_update_slice(
        jnp.zeros((vectors.shape[0], depth), BF), vectors, (0, index * local)
    )
    tile = jnp.concatenate(
        [
            placed,
            jnp.pad(bias_row, ((0, EXTRA - vectors.shape[0] - 1), (0, depth - width2))),
        ],
        0,
    )
    mats = jnp.concatenate(
        [qkv_weight.transpose(1, 0, 2).reshape(local, 3 * width), attn_weight.T], 1
    )
    wide = jnp.concatenate([fc_weight, proj_weight.T], 1)
    if count == CHUNKS:
        blocks = gather_blocks(jnp.concatenate([mats, tile], 0), stat_one)
        own_a = jnp.stack(blocks)
        far = swap_mask(lax.optimization_barrier((wide, blocks[4]))[0], 4)
        wide = lax.optimization_barrier((wide, own_a))[0]
    else:
        full = lax.all_gather(mats, "dp", axis=0, tiled=True).reshape(CHUNKS, base, depth)
        total = jnp.sum(lax.all_gather(tile, "dp", axis=0).astype(F32), 0).astype(BF)
        total = jnp.pad(total[None], ((0, CHUNKS - 1), (0, 0), (0, 0)))
        own_a = jnp.concatenate([full, total], 1)
        own_b = lax.all_gather(wide, "dp", axis=0, tiled=True).reshape(CHUNKS, base, 2 * units)
        own_b = [own_b[r] for r in range(CHUNKS)]
    sib_a = swap_core(own_a)
    weight = shape((depth, width2))
    q, k, v, wq, wk, wv, wo, first_own, vec, vec_sib = call(
        project_kernel,
        [
            shape((heads2, own_count, HD)),
            shape((heads2, rows, HD)),
            shape((heads2, rows, HD)),
            weight,
            weight,
            weight,
            weight,
            shape((own_count, depth)),
            shape((EXTRA, depth), F32),
            shape((EXTRA, depth), F32),
        ],
        info,
        inputs,
        stat_one,
        own_a,
        sib_a,
        scratch=[pltpu.VMEM((rows, depth), BF), pltpu.VMEM((rows, width2), F32)],
        cost=8,
        name="project",
    )
    if count == CHUNKS:
        blocks = gather_blocks(wide, q, far)
    tiles = own_count // TILE
    part, mixed, probs = call(
        attend_kernel,
        [
            shape((own_count, depth)),
            shape((own_count, width2)),
            shape((heads2, TILE, TILE * tiles * (tiles + 1))),
        ],
        info,
        q,
        k,
        v,
        wo,
        seg_row,
        scratch=[
            pltpu.VMEM((heads2 + 1, TILE, rows), F32),
            pltpu.VMEM((heads2, own_count, HD), F32),
        ],
        cost=16,
        name="attend",
    )
    got = swap_chip(part)
    if count == CHUNKS:
        own_b = lax.optimization_barrier((blocks, part))[0]
    sib_b = [swap_core(block) for block in own_b]
    hid = shape((own_count, 2 * units))
    full = shape((depth, 2 * units))
    fc_full, proj_full, dy, dact = call(
        mlp_pre_kernel,
        [full, full, shape((own_count, depth)), hid],
        info,
        seg_row,
        cotangent,
        *own_b,
        *sib_b,
        name="mlp_pre",
    )
    da, act, dhid, second, middle, stat_two = call(
        mlp_kernel,
        [
            shape((own_count, depth)),
            hid,
            hid,
            shape((own_count, depth)),
            shape((own_count, depth), F32),
            shape((own_count, 2 * TILE), F32),
        ],
        info,
        inputs,
        part,
        got,
        vec,
        vec_sib,
        fc_full,
        dact,
        scratch=[pltpu.VMEM((own_count, units), F32)],
        cost=10,
        name="mlp",
    )
    da_got = swap_chip(da)
    mlp_part, grad_own, *grad_sib, mlp_sums = call(
        mlp_grad_kernel,
        [
            shape((own_count, depth)),
            shape((CHUNKS, base, 2 * units)),
            *[shape((CHUNKS // 2, base, units))] * 4,
            shape((24, depth), F32),
        ],
        info,
        act,
        dhid,
        second,
        dy,
        proj_full,
        scratch=[pltpu.VMEM((depth, units), F32)],
        cost=9,
        name="mlp_grad",
    )
    mlp_got = swap_chip(mlp_part)
    exact = count == CHUNKS
    if exact:
        big_state = scatter_start(info, grad_own, grad_sib)
        big_sent = big_state[1]
        big_state = scatter_send(big_state, (0, 1))
    else:
        big = scatter_plain(grad_own, grad_sib)
        fc_weight_grad, proj_weight_grad = big[:, :units], big[:, units:].T

    dmid, branch, att_sums, dq, keep, *send = call(
        attend_back_kernel,
        [
            shape((own_count, depth), F32),
            shape((own_count, depth)),
            shape((8, depth), F32),
            shape((own_count, width2)),
            shape((2 * width2, own_count), F32),
            *[shape((width2, own_count))] * 2,
        ],
        info,
        middle,
        stat_two,
        dy,
        da,
        da_got,
        vec,
        wo,
        mixed,
        q,
        k,
        v,
        probs,
        scratch=[
            pltpu.VMEM((own_count, width2), BF),
            pltpu.VMEM((heads2, own_count, HD), BF),
            pltpu.VMEM((heads2, HD, rows), F32),
            pltpu.VMEM((heads2, HD, rows), F32),
            pltpu.VMEM((heads2, own_count, HD), F32),
            pltpu.VMEM((heads2, TILE, rows), F32),
            pltpu.VMEM((heads2, TILE, rows), BF),
            pltpu.VMEM((heads2, own_count, TILE), F32),
        ],
        cost=18,
        name="attend_back",
        after=(big_sent,) if exact else (),
    )
    keep_got = [swap_core(piece) for piece in send]
    attn_full = call(
        attn_grad_kernel,
        [shape((depth, width2), F32)],
        info,
        branch,
        mixed,
        name="attn_grad",
        after=(mlp_got, big_state[1], big_state[3]) if exact else (),
    )[0]
    if exact:
        big_state = scatter_middle(info, big_state, False, after=(attn_full,))
        big_ready = big_state[0]
        big_state = scatter_send(big_state, (1, 0))
    first_part, dkv = call(
        first_grad_kernel,
        [shape((own_count, depth)), shape((2 * width2, own_count))],
        info,
        dq,
        keep,
        *keep_got,
        wq,
        wk,
        wv,
        name="first_grad",
        after=(big_ready,) if exact else (),
    )
    first_got = swap_chip(first_part)
    qkv_own, *qkv_sib, tile_own, tile_sib = call(
        qkv_grad_kernel,
        [
            shape((CHUNKS, base, 4 * width)),
            *[shape((CHUNKS // 2, base, 4 * width))] * 2,
            *[shape((EXTRA, depth))] * 2,
        ],
        info,
        first_own,
        dq,
        dkv,
        attn_full,
        first_part,
        inputs,
        stat_one,
        mlp_sums,
        att_sums,
        scratch=[pltpu.VMEM((depth, width2), F32), pltpu.VMEM((EXTRA, depth), F32)],
        cost=7,
        name="qkv_grad",
        after=(big_state[1], big_state[3]) if exact else (),
    )
    finish = lambda after: call(
        final_kernel,
        [shape((own_count, depth))],
        info,
        inputs,
        stat_one,
        first_part,
        first_got,
        dmid,
        vec,
        name="final",
        cost=5,
        after=after,
    )[0]
    output = lambda after: call(
        output_kernel,
        [shape((own_count, depth))],
        info,
        seg_row,
        middle,
        mlp_part,
        mlp_got,
        vec,
        name="output",
        after=after,
    )[0]
    tiles = (tile_own, swap_core(tile_sib))
    if exact:
        big_last = scatter_late(info, big_state, False, after=(qkv_own,))
        small_state = scatter_start(info, qkv_own, qkv_sib, tiles, after=(big_last[0],))
        small_sent = small_state[1]
        small_state = scatter_send(small_state, (0, 1))
        out_low = output((small_sent,))
        inputs_low = finish((out_low,))
        small_state = scatter_middle(info, small_state, True, after=(inputs_low, big_last[1]))
        small_sent = small_state[1]
        small_state = scatter_send(small_state, (1, 0))
        outputs = all_rows(info, out_low, (small_sent,))
        fc_weight_grad, proj_weight_grad = call(
            scatter_big_kernel,
            [shape((local, units), F32), shape((units, local), F32)],
            info,
            *big_last,
            name="scatter_big",
            cost=2,
        )
        small_last = scatter_late(info, small_state, True, after=(outputs,))
        inputs_grad = all_rows(info, inputs_low, (small_last[0],))
        qkv_weight_grad, attn_weight_grad, tile = call(
            scatter_small_kernel,
            [
                shape((3, local, width), F32),
                shape((width, local), F32),
                shape((EXTRA, depth), F32),
            ],
            info,
            *small_last,
            name="scatter_small",
            cost=2,
            after=(fc_weight_grad, inputs_grad),
        )
    else:
        inputs_grad = all_rows(info, finish(()))
        outputs = all_rows(info, output(()))
        mine = scatter_plain(qkv_own, qkv_sib)
        qkv_weight_grad = mine[:, : 3 * width].reshape(local, 3, width).transpose(1, 0, 2)
        attn_weight_grad = mine[:, 3 * width :].T
        tile = lax.psum(tiles[0].astype(F32) + tiles[1].astype(F32), "dp")
    tile_got = swap_chip(tile.astype(BF)).astype(F32)
    mask = (jnp.arange(EXTRA) < 2)[:, None]
    tile = jnp.where(mask, tile.astype(BF).astype(F32) + tile_got, tile)
    parts = lax.dynamic_slice(tile, (0, index * local), (7, local))
    bias_sum = tile[7, :width2].reshape(2, heads, HD).transpose(1, 0, 2).reshape(heads, 2 * HD)
    qv_bias_grad = lax.dynamic_slice(bias_sum, (0, index * bias_width), (heads, bias_width))
    return (
        outputs,
        inputs_grad,
        parts[0],
        parts[1],
        qkv_weight_grad,
        qv_bias_grad,
        attn_weight_grad,
        parts[2],
        parts[3],
        parts[4],
        fc_weight_grad,
        parts[5][None],
        proj_weight_grad,
        parts[6],
    )


def solution(mesh):
    return jax.shard_map(
        body,
        mesh=mesh,
        in_specs=(
            P("dp", None),
            P("dp"),
            P("dp"),
            P("dp"),
            P(None, "dp", "mp"),
            P("mp", "dp"),
            P("mp", "dp"),
            P("dp"),
            P("dp"),
            P("dp"),
            P("dp", "mp"),
            P("mp", "dp"),
            P("mp", "dp"),
            P("dp"),
            P("dp", None),
        ),
        out_specs=(
            P("dp", None),
            P("dp", None),
            P("dp"),
            P("dp"),
            P(None, "dp", "mp"),
            P("mp", "dp"),
            P("mp", "dp"),
            P("dp"),
            P("dp"),
            P("dp"),
            P("dp", "mp"),
            P("mp", "dp"),
            P("mp", "dp"),
            P("dp"),
        ),
        check_vma=False,
    )
```

```python
import functools

import jax
import jax.numpy as jnp
from jax import lax
from jax.experimental import pallas as pl
from jax.experimental.pallas import tpu as pltpu
from jax.sharding import PartitionSpec as P

HD = 64
TILE = 128
EXTRA = 16
CHUNKS = 8
EPSILON = 1e-05
NEGATIVE = -1e30
BF = jnp.bfloat16
F32 = jnp.float32
CORE_PAIRS = ((0, 1), (1, 0), (2, 3), (3, 2))
CHIP_PAIRS = ((0, 2), (2, 0), (1, 3), (3, 1))
CURVE = 0.7978845608028654


def dot(left, right, left_dim, right_dim):
    return lax.dot_general(
        left, right, (((left_dim,), (right_dim,)), ((), ())), preferred_element_type=F32
    )


def swap_core(value):
    return lax.ppermute(value, "mp", CORE_PAIRS)


def swap_chip(value):
    return lax.ppermute(value, "mp", CHIP_PAIRS)


def swap_mask(value, mask):
    return lax.ppermute(value, "dp", [(i, i ^ mask) for i in range(CHUNKS)])


def swap_bit(value, bit):
    return swap_mask(value, 1 << bit)


def call(kernel, outs, *args, scratch=(), smem=1, cost=0, name=None, after=()):
    first, behind = len(args), len(args) + len(after)

    def run(*refs):
        kernel(*refs[:first], *refs[behind:])

    specs = [pl.BlockSpec(memory_space=pltpu.SMEM)] * smem
    specs += [pl.BlockSpec(memory_space=pltpu.VMEM)] * (len(args) - smem)
    specs += [pl.BlockSpec(memory_space=pl.ANY)] * len(after)
    return pl.pallas_call(
        run,
        out_shape=outs,
        in_specs=specs,
        out_specs=[pl.BlockSpec(memory_space=pltpu.VMEM)] * len(outs),
        scratch_shapes=list(scratch),
        compiler_params=pltpu.CompilerParams(vmem_limit_bytes=56 * 1024 * 1024),
        cost_estimate=pl.CostEstimate(flops=cost * 10**9, bytes_accessed=1024, transcendentals=0),
        name=name,
    )(*args, *after)


def shape(dims, dtype=BF):
    return jax.ShapeDtypeStruct(tuple(dims), dtype)


def gather_blocks(message, behind, far=None):
    got = {0: message}
    got[4] = swap_mask(message, 4) if far is None else far
    got[2] = swap_mask(message, 2)
    got[1] = swap_mask(message, 1)
    four, two = lax.optimization_barrier((got[4], got[2], behind))[:2]
    got[7] = swap_mask(four, 3)
    got[5] = swap_mask(four, 1)
    got[6] = swap_mask(four, 2)
    got[3] = swap_mask(two, 1)
    return [got[r] for r in range(CHUNKS)]


def loop(count, step, fn, unroll=4):
    def run(i, carry):
        fn(pl.multiple_of(i * step, step))
        return carry

    lax.fori_loop(0, count // step, run, 0, unroll=unroll)


def norm_backward(incoming, scaled, factor, gain):
    weighted = incoming * gain
    first_mean = jnp.mean(weighted, -1, keepdims=True)
    second_mean = jnp.mean(weighted * scaled, -1, keepdims=True)
    return factor * (weighted - first_mean - scaled * second_mean)


def tile_sum(ref, base):
    total = ref[0, base : base + EXTRA, :].astype(F32)
    for r in range(1, CHUNKS):
        total = total + ref[r, base : base + EXTRA, :].astype(F32)
    return total


def own_start(start, core):
    tile = start // TILE
    return pl.multiple_of((2 * tile + core) * TILE + start % TILE, 32)


def colsum(value):
    return jnp.sum(value, 0, keepdims=True)


def spread_stats(value):
    average = jnp.mean(value, -1, keepdims=True)
    centred = value - average
    factor = lax.rsqrt(jnp.mean(centred * centred, -1, keepdims=True) + EPSILON)
    rows = value.shape[0]
    return jnp.concatenate(
        [jnp.broadcast_to(average, (rows, TILE)), jnp.broadcast_to(factor, (rows, TILE))], 1
    )


def stats_kernel(info, x_ref, stat_ref):
    def run(at):
        rs = pl.ds(at, 32)
        stat_ref[rs, :] = spread_stats(x_ref[rs, :].astype(F32))

    loop(x_ref.shape[0], 32, run)


def project_kernel(
    info,
    x_ref,
    stat_ref,
    own_ref,
    sib_ref,
    q_ref,
    k_ref,
    v_ref,
    wq_ref,
    wk_ref,
    wv_ref,
    wo_ref,
    firstown_ref,
    vec_ref,
    vecsib_ref,
    low_ref,
    proj_ref,
):
    flip, core = info[0], info[1]
    width = own_ref.shape[2] // 4
    base = own_ref.shape[1] - EXTRA
    rows = low_ref.shape[0]
    heads = 2 * width // HD
    own_count = rows // 2
    vec_ref[...] = tile_sum(own_ref, base)
    vecsib_ref[...] = tile_sum(sib_ref, base)
    gain, shift = vec_ref[0:1, :], vec_ref[1:2, :]

    def norm(at):
        rs = pl.ds(at, 32)
        scaled = (x_ref[rs, :].astype(F32) - stat_ref[rs, 0:1]) * stat_ref[rs, TILE : TILE + 1]
        low_ref[rs, :] = (scaled * gain + shift).astype(BF)

    loop(rows, 32, norm)
    for r in range(CHUNKS):
        at = pl.multiple_of((r ^ flip) * base, 32)
        for side, ref in ((0, own_ref), (1, sib_ref)):
            for part, out in enumerate((wq_ref, wk_ref, wv_ref, wo_ref)):
                out[pl.ds(at, base), side * width : (side + 1) * width] = ref[
                    r, 0:base, part * width : (part + 1) * width
                ]
    bias_q = jnp.concatenate([vec_ref[7:8, :width], vecsib_ref[7:8, :width]], 1)
    bias_v = jnp.concatenate(
        [vec_ref[7:8, width : 2 * width], vecsib_ref[7:8, width : 2 * width]], 1
    )
    for j in range(own_count // TILE):
        at = own_start(j * TILE, core)
        firstown_ref[j * TILE : (j + 1) * TILE, :] = low_ref[pl.ds(at, TILE), :]
    scale = float(HD) ** -0.5
    proj_ref[0:own_count, :] = dot(firstown_ref[...], wq_ref[...], 1, 0) + bias_q
    for h in range(heads):
        q_ref[h] = (
            proj_ref[0:own_count, h * HD : (h + 1) * HD].astype(BF).astype(F32) * scale
        ).astype(BF)
    proj_ref[...] = dot(low_ref[...], wk_ref[...], 1, 0)
    for h in range(heads):
        k_ref[h] = proj_ref[:, h * HD : (h + 1) * HD].astype(BF)
    proj_ref[...] = dot(low_ref[...], wv_ref[...], 1, 0) + bias_v
    for h in range(heads):
        v_ref[h] = proj_ref[:, h * HD : (h + 1) * HD].astype(BF)


def attend_kernel(
    info, q_ref, k_ref, v_ref, wo_ref, seg_ref, part_ref, mixed_ref, probs_ref, s_ref, o_ref
):
    core = info[1]
    heads, own_count = q_ref.shape[:2]
    lane = lax.broadcasted_iota(jnp.int32, (TILE, TILE), 1)
    line = lax.broadcasted_iota(jnp.int32, (TILE, TILE), 0)
    for j in range(own_count // TILE):
        end = (j + 1) * 2 * TILE
        off = TILE * j * (j + 1)
        at = own_start(j * TILE, core)
        seg_tile = jnp.broadcast_to(seg_ref[0:1, pl.ds(at, TILE)], (TILE, TILE))
        seg_col = jnp.max(jnp.where(lane == line, seg_tile, -2), -1, keepdims=True)
        place = lax.broadcasted_iota(jnp.int32, (TILE, end), 1)
        own_place = at + lax.broadcasted_iota(jnp.int32, (TILE, end), 0)
        allowed = (seg_col == seg_ref[0:1, 0:end]) & (place <= own_place)
        bias = jnp.where(allowed, 0.0, NEGATIVE)
        s_ref[heads, :, 0:end] = bias

        def run(h, carry, j=j, end=end, off=off):
            scores = dot(q_ref[h, j * TILE : (j + 1) * TILE, :], k_ref[h, 0:end, :], 1, 1)
            s_ref[h, :, 0:end] = scores
            for sub in range(4):
                sl = slice(sub * 32, sub * 32 + 32)
                sc = s_ref[h, sl, 0:end] + s_ref[heads, sl, 0:end]
                weights = jnp.exp(sc - jnp.max(sc, -1, keepdims=True))
                inverse = 1.0 / jnp.sum(weights, -1, keepdims=True)
                probs_ref[h, sl, off : off + end] = (weights * inverse).astype(BF)
            o_ref[h, j * TILE : (j + 1) * TILE, :] = dot(
                probs_ref[h, :, off : off + end], v_ref[h, 0:end, :], 1, 0
            )
            return carry

        lax.fori_loop(0, heads, run, 0, unroll=True)
    for h in range(heads):
        mixed_ref[:, h * HD : (h + 1) * HD] = o_ref[h].astype(BF)
    part_ref[...] = dot(mixed_ref[...], wo_ref[...], 1, 1).astype(BF)


def mlp_pre_kernel(info, seg_ref, cot_ref, *refs):
    own_refs, sib_refs = refs[:CHUNKS], refs[CHUNKS : 2 * CHUNKS]
    fc_ref, proj_ref, dy_ref, dact_ref = refs[2 * CHUNKS :]
    flip, core = info[0], info[1]
    own_count = dy_ref.shape[0]
    base = own_refs[0].shape[0]
    units = own_refs[0].shape[1] // 2
    sub = 32
    lane = lax.broadcasted_iota(jnp.int32, (sub, TILE), 1)
    line = lax.broadcasted_iota(jnp.int32, (sub, TILE), 0)

    def mask(at):
        src = own_start(at, core)
        tile_at = pl.multiple_of((2 * (at // TILE) + core) * TILE, TILE)
        seg_tile = jnp.broadcast_to(seg_ref[0:1, pl.ds(tile_at, TILE)], (sub, TILE))
        seg_col = jnp.max(
            jnp.where(lane == line + at % TILE, seg_tile, -2), -1, keepdims=True
        )
        cot = cot_ref[pl.ds(src, sub), :].astype(F32)
        dy_ref[pl.ds(at, sub), :] = jnp.where(seg_col >= 0, cot, 0.0).astype(BF)

    loop(own_count, sub, mask)
    for r in range(CHUNKS):
        at = pl.multiple_of((r ^ flip) * base, 32)
        for side, ref in ((0, own_refs[r]), (1, sib_refs[r])):
            cols = slice(side * units, (side + 1) * units)
            fc_ref[pl.ds(at, base), cols] = ref[:, 0:units]
            proj_ref[pl.ds(at, base), cols] = ref[:, units : 2 * units]
    for side in range(2):
        cols = slice(side * units, (side + 1) * units)
        dact_ref[:, cols] = dot(dy_ref[...], proj_ref[:, cols], 1, 0).astype(BF)


def mlp_kernel(
    info,
    x_ref,
    part_ref,
    recv_ref,
    vec_ref,
    vecsib_ref,
    fc_ref,
    dact_ref,
    da_ref,
    act_ref,
    dhid_ref,
    second_ref,
    mid_ref,
    stat_ref,
    hid_ref,
):
    core = info[1]
    own_count = part_ref.shape[0]
    units = fc_ref.shape[1] // 2
    gain, shift, bias = vec_ref[3:4, :], vec_ref[4:5, :], vec_ref[2:3, :]
    sub = 32

    def first(at):
        src = own_start(at, core)
        rows = pl.ds(at, sub)
        middle = (
            x_ref[pl.ds(src, sub), :].astype(F32)
            + (part_ref[rows, :].astype(F32) + recv_ref[rows, :].astype(F32))
            + bias
        )
        mid_ref[rows, :] = middle
        stats = spread_stats(middle)
        stat_ref[rows, :] = stats
        scaled = (middle - stats[:, 0:1]) * stats[:, TILE : TILE + 1]
        second_ref[rows, :] = (scaled * gain + shift).astype(BF)

    loop(own_count, sub, first)
    for side, biases in ((0, vec_ref), (1, vecsib_ref)):
        cols = slice(side * units, (side + 1) * units)
        hid_ref[...] = dot(second_ref[...], fc_ref[:, cols], 1, 0)
        bias_fc = biases[5:6, :]

        def gelu(at, cols=cols, bias_fc=bias_fc):
            rows = pl.ds(at, 16)
            u = hid_ref[rows, :] + bias_fc
            u2 = u * u
            bend = jnp.tanh(CURVE * u * (1.0 + 0.044715 * u2))
            half = 0.5 * (1.0 + bend)
            act_ref[rows, cols] = (u * half).astype(BF)
            slope = half + (0.5 * CURVE) * u * (1.0 - bend * bend) * (1.0 + 0.134145 * u2)
            dhid_ref[rows, cols] = (dact_ref[rows, cols].astype(F32) * slope).astype(BF)

        loop(own_count, 16, gelu)
    da_ref[...] = dot(dhid_ref[...], fc_ref[...], 1, 1).astype(BF)


def mlp_grad_kernel(
    info,
    act_ref,
    dhid_ref,
    second_ref,
    dy_ref,
    proj_ref,
    part_ref,
    own_ref,
    sib_a_ref,
    sib_b_ref,
    sib_c_ref,
    sib_d_ref,
    sums_ref,
):
    sib_refs = ((sib_a_ref, sib_b_ref), (sib_c_ref, sib_d_ref))
    base, units = own_ref.shape[1], own_ref.shape[2] // 2
    half = units // 2
    part_ref[...] = dot(act_ref[...], proj_ref[...], 1, 1).astype(BF)
    for kind, left, right in ((0, second_ref, dhid_ref), (1, dy_ref, act_ref)):
        for side in range(2):
            value = dot(left[...], right[:, side * units : (side + 1) * units], 0, 0).astype(BF)
            for b in range(CHUNKS):
                block = value[b * base : (b + 1) * base, :]
                if side:
                    sib_refs[kind][0][b] = block[:, :half]
                    sib_refs[kind][1][b] = block[:, half:]
                else:
                    own_ref[b, :, kind * units : (kind + 1) * units] = block
    one = jnp.ones((8, act_ref.shape[0]), BF)
    fc_sums = dot(one, dhid_ref[...], 1, 0)
    sums_ref[0:8, :] = fc_sums[:, 0:units]
    sums_ref[8:16, :] = fc_sums[:, units : 2 * units]
    sums_ref[16:24, :] = dot(one, dy_ref[...], 1, 0)


def attend_back_kernel(
    info,
    mid_ref,
    stat_ref,
    dy_ref,
    da_ref,
    recv_ref,
    vec_ref,
    wo_ref,
    mixed_ref,
    q_ref,
    k_ref,
    v_ref,
    probs_ref,
    dmid_ref,
    branch_ref,
    sums_ref,
    dq_ref,
    keep_ref,
    send_k_ref,
    send_v_ref,
    dm_ref,
    do_ref,
    dkt_ref,
    dvt_ref,
    dqh_ref,
    dp_ref,
    ds_ref,
    delta_ref,
):
    core = info[1]
    own_count = mid_ref.shape[0]
    heads = q_ref.shape[0]
    rows = k_ref.shape[1]
    gain = vec_ref[3:4, :]
    sums_ref[...] = jnp.zeros_like(sums_ref)
    sub = 32

    def first(at):
        rs = pl.ds(at, sub)
        factor = stat_ref[rs, TILE : TILE + 1]
        scaled = (mid_ref[rs, :] - stat_ref[rs, 0:1]) * factor
        incoming = da_ref[rs, :].astype(F32) + recv_ref[rs, :].astype(F32)
        dmid = dy_ref[rs, :].astype(F32) + norm_backward(incoming, scaled, factor, gain)
        dmid_ref[rs, :] = dmid
        low = dmid.astype(BF)
        branch_ref[rs, :] = low
        sums_ref[2:3, :] += colsum(low.astype(F32))
        sums_ref[3:4, :] += colsum(incoming * scaled)
        sums_ref[4:5, :] += colsum(incoming)

    loop(own_count, sub, first)
    dm_ref[...] = dot(branch_ref[...], wo_ref[...], 1, 0).astype(BF)
    for h in range(heads):
        cols = slice(h * HD, (h + 1) * HD)
        do_ref[h] = dm_ref[:, cols]
        delta_ref[h] = jnp.broadcast_to(
            jnp.sum(
                dm_ref[:, cols].astype(F32) * mixed_ref[:, cols].astype(F32), -1, keepdims=True
            ),
            (own_count, TILE),
        )
    scale = float(HD) ** -0.5

    def head(h, carry):
        for j in reversed(range(own_count // TILE)):
            end = (j + 1) * 2 * TILE
            off = TILE * j * (j + 1)
            rs = slice(j * TILE, (j + 1) * TILE)
            dp_ref[h, :, 0:end] = dot(do_ref[h, rs, :], v_ref[h, 0:end, :], 1, 1)
            for s in range(4):
                sl = slice(s * 32, s * 32 + 32)
                delta = delta_ref[h, j * TILE + s * 32 : j * TILE + s * 32 + 32, 0:1]
                p = probs_ref[h, sl, off : off + end].astype(F32)
                ds_ref[h, sl, 0:end] = (p * (dp_ref[h, sl, 0:end] - delta)).astype(BF)
            ds = ds_ref[h, :, 0:end]
            dqh_ref[h, rs, :] = dot(ds, k_ref[h, 0:end, :], 1, 0) * scale
            dk = dot(q_ref[h, rs, :], ds, 0, 0)
            dv = dot(do_ref[h, rs, :], probs_ref[h, :, off : off + end], 0, 0)
            if j == own_count // TILE - 1:
                dkt_ref[h] = dk
                dvt_ref[h] = dv
            else:
                dkt_ref[h, :, 0:end] += dk
                dvt_ref[h, :, 0:end] += dv
        return carry

    lax.fori_loop(0, heads, head, 0, unroll=3)
    width2 = heads * HD
    for h in range(heads):
        dq_ref[:, h * HD : (h + 1) * HD] = dqh_ref[h].astype(BF)
        twin = (h + heads // 2) % heads
        for j in range(own_count // TILE):
            mine = pl.multiple_of((2 * j + core) * TILE, TILE)
            yours = pl.multiple_of((2 * j + 1 - core) * TILE, TILE)
            cols = slice(j * TILE, (j + 1) * TILE)
            for part, ref, send in ((0, dkt_ref, send_k_ref), (1, dvt_ref, send_v_ref)):
                at = part * width2
                keep_ref[at + h * HD : at + (h + 1) * HD, cols] = ref[h, :, pl.ds(mine, TILE)]
                send[twin * HD : (twin + 1) * HD, cols] = ref[h, :, pl.ds(yours, TILE)].astype(BF)


def first_grad_kernel(
    info, dq_ref, keep_ref, got_k_ref, got_v_ref, wq_ref, wk_ref, wv_ref, part_ref, dkv_ref
):
    width2 = dq_ref.shape[1]
    for p, got in enumerate((got_k_ref, got_v_ref)):
        rows = slice(p * width2, (p + 1) * width2)
        dkv_ref[rows, :] = (keep_ref[rows, :] + got[...].astype(F32)).astype(BF)
    part_ref[...] = (
        dot(dq_ref[...], wq_ref[...], 1, 1)
        + dot(dkv_ref[0:width2, :], wk_ref[...], 0, 1)
        + dot(dkv_ref[width2 : 2 * width2, :], wv_ref[...], 0, 1)
    ).astype(BF)


def qkv_grad_kernel(
    info,
    first_ref,
    dq_ref,
    dkv_ref,
    branch_ref,
    mixed_ref,
    part_ref,
    x_ref,
    stat_ref,
    mlp_sums_ref,
    att_sums_ref,
    own_ref,
    sib_a_ref,
    sib_b_ref,
    tile_own_ref,
    tile_sib_ref,
    sum_ref,
):
    core = info[1]
    width2 = dq_ref.shape[1]
    width = width2 // 2
    base = own_ref.shape[1]
    for part in range(4):
        if part == 0:
            whole = dot(first_ref[...], dq_ref[...], 0, 0)
        elif part == 3:
            whole = dot(branch_ref[...], mixed_ref[...], 0, 0)
        else:
            whole = dot(
                first_ref[...], dkv_ref[(part - 1) * width2 : part * width2, :], 0, 1
            )
        whole = whole.astype(BF)
        cols = slice(part * width, (part + 1) * width)
        side_cols = slice(part % 2 * width, (part % 2 + 1) * width)
        for b in range(CHUNKS):
            block = whole[b * base : (b + 1) * base, :]
            own_ref[b, :, cols] = block[:, 0:width]
            (sib_a_ref, sib_b_ref)[part // 2][b, :, side_cols] = block[:, width:width2]
    sum_ref[...] = jnp.zeros_like(sum_ref)

    def run(at):
        src = own_start(at, core)
        rs = pl.ds(src, 32)
        scaled = (x_ref[rs, :].astype(F32) - stat_ref[rs, 0:1]) * stat_ref[rs, TILE : TILE + 1]
        incoming = part_ref[pl.ds(at, 32), :].astype(F32)
        sum_ref[0:1, :] += colsum(incoming * scaled)
        sum_ref[1:2, :] += colsum(incoming)

    loop(part_ref.shape[0], 32, run)
    ones = jnp.ones((8, dq_ref.shape[0]), BF)
    qs = dot(ones, dq_ref[...], 1, 0)[0:1, :]
    vs = dot(ones, dkv_ref[width2 : 2 * width2, :], 1, 1)[0:1, :]
    sum_ref[2:5, :] = att_sums_ref[2:5, :]
    sum_ref[6:7, :] = mlp_sums_ref[16:17, :]
    for side, out in ((0, tile_own_ref), (1, tile_sib_ref)):
        sl = slice(side * width, (side + 1) * width)
        sum_ref[5:6, :] = mlp_sums_ref[8 * side : 8 * side + 1, :]
        sum_ref[7:8, 0:width] = qs[:, sl]
        sum_ref[7:8, width : 2 * width] = vs[:, sl]
        out[...] = sum_ref[...].astype(BF)


def final_kernel(
    info,
    x_ref,
    stat_ref,
    part_ref,
    recv_ref,
    dmid_ref,
    vec_ref,
    seg_ref,
    mid_ref,
    mlp_ref,
    mlp_got_ref,
    out_ref,
):
    core = info[1]
    own_count = part_ref.shape[0]
    gain, bias = vec_ref[0:1, :], vec_ref[6:7, :]
    sub = 32
    lane = lax.broadcasted_iota(jnp.int32, (sub, TILE), 1)
    line = lax.broadcasted_iota(jnp.int32, (sub, TILE), 0)

    def run(at):
        src = own_start(at, core)
        rs = pl.ds(at, sub)
        factor = stat_ref[pl.ds(src, sub), TILE : TILE + 1]
        scaled = (x_ref[pl.ds(src, sub), :].astype(F32) - stat_ref[pl.ds(src, sub), 0:1]) * factor
        incoming = part_ref[rs, :].astype(F32) + recv_ref[rs, :].astype(F32)
        out_ref[pl.ds(own_count + at, sub), :] = (
            dmid_ref[rs, :] + norm_backward(incoming, scaled, factor, gain)
        ).astype(BF)
        tile_at = pl.multiple_of((2 * (at // TILE) + core) * TILE, TILE)
        seg_tile = jnp.broadcast_to(seg_ref[0:1, pl.ds(tile_at, TILE)], (sub, TILE))
        seg_col = jnp.max(
            jnp.where(lane == line + at % TILE, seg_tile, -2), -1, keepdims=True
        )
        final = (
            mid_ref[rs, :]
            + (mlp_ref[rs, :].astype(F32) + mlp_got_ref[rs, :].astype(F32))
            + bias
        )
        out_ref[rs, :] = jnp.where(seg_col >= 0, final, 0.0).astype(BF)

    loop(own_count, sub, run)


def merge_kernel(info, own_ref, got_ref, first_ref, second_ref):
    core = info[1]
    count = first_ref.shape[0] // (2 * TILE)
    for i in range(2 * count):
        out, j = (first_ref, second_ref)[i // count], i % count
        sl = slice(i * TILE, (i + 1) * TILE)
        mine = pl.multiple_of((2 * j + core) * TILE, TILE)
        yours = pl.multiple_of((2 * j + 1 - core) * TILE, TILE)
        out[pl.ds(mine, TILE), :] = own_ref[sl, :]
        out[pl.ds(yours, TILE), :] = got_ref[sl, :]


def all_rows(info, own, after=()):
    return call(
        merge_kernel,
        [shape(own.shape)] * 2,
        info,
        own,
        swap_core(own),
        name="merge",
        cost=4,
        after=after,
    )


def scatter_first_kernel(pieces, info, own_ref, *refs):
    got_refs, refs = refs[:pieces], refs[pieces:]
    tiles, (keep_a, send_a, keep_b, send_b) = refs[:-4], refs[-4:]
    flip = info[0]
    base = own_ref.shape[1]
    half = own_ref.shape[2] // 2
    span = own_ref.shape[2] // pieces
    for side, keep, send in ((0, keep_a, send_a), (1, keep_b, send_b)):
        cols = slice(side * half, (side + 1) * half)
        kept, sent = 0, 0
        for r in range(CHUNKS):
            rows = slice(sent * base, (sent + 1) * base)
            if not (r >> side) & 1:
                rows = slice(kept * base, (kept + 1) * base)
            for p in range(pieces // 2):
                piece = side * (pieces // 2) + p
                value = own_ref[r ^ flip, :, piece * span : (piece + 1) * span].astype(F32)
                value = value + got_refs[piece][r ^ flip].astype(F32)
                if (r >> side) & 1:
                    send[rows, p * span : (p + 1) * span] = value.astype(BF)
                else:
                    keep[rows, p * span : (p + 1) * span] = value
            sent += (r >> side) & 1
            kept += 1 - ((r >> side) & 1)
        if tiles:
            value = tiles[0][:, cols].astype(F32) + tiles[1][:, cols].astype(F32)
            send[4 * base : 4 * base + EXTRA, :] = value.astype(BF)
            keep[4 * base : 4 * base + EXTRA, :] = value


def scatter_second_kernel(
    tiled, info, keep_a, got_a, keep_b, got_b, next_a, send_a, next_b, send_b
):
    extra = EXTRA if tiled else 0
    base = (keep_a.shape[0] - extra) // 4
    for keep, got, left, send, order in (
        (keep_a, got_a, next_a, send_a, (0, 1, 0, 1)),
        (keep_b, got_b, next_b, send_b, (0, 1, 0, 1)),
    ):
        kept, sent = 0, 0
        for r in range(4):
            rows = slice(r * base, (r + 1) * base)
            value = keep[rows, :] + got[rows, :].astype(F32)
            if order[r]:
                send[sent * base : (sent + 1) * base, :] = value.astype(BF)
                sent += 1
            else:
                left[kept * base : (kept + 1) * base, :] = value
                kept += 1
        if tiled:
            low = keep[4 * base : 4 * base + extra, :].astype(BF).astype(F32)
            value = low + got[4 * base : 4 * base + extra, :].astype(F32)
            send[2 * base : 2 * base + extra, :] = value.astype(BF)
            left[2 * base : 2 * base + extra, :] = value


def scatter_third_kernel(tiled, info, keep_a, got_a, keep_b, got_b, left, send):
    extra = EXTRA if tiled else 0
    base = (keep_a.shape[0] - extra) // 2
    half = keep_a.shape[1]
    for keep, got, at in ((keep_a, got_a, 0), (keep_b, got_b, half)):
        cols = slice(at, at + half)
        left[0:base, cols] = keep[0:base, :] + got[0:base, :].astype(F32)
        send[0:base, cols] = (
            keep[base : 2 * base, :] + got[base : 2 * base, :].astype(F32)
        ).astype(BF)
        if tiled:
            rows = slice(2 * base, 2 * base + extra)
            value = keep[rows, :].astype(BF).astype(F32) + got[rows, :].astype(F32)
            left[base : base + extra, cols] = value
            send[base : base + extra, cols] = value.astype(BF)


def scatter_big_kernel(info, left, got, fc_ref, proj_ref):
    units = fc_ref.shape[1]
    total = left[...] + got[...].astype(F32)
    fc_ref[...] = total[:, :units]
    proj_ref[...] = jnp.transpose(total[:, units:])


def scatter_small_kernel(info, left, got, qkv_ref, attn_ref, tile_ref):
    base = left.shape[0] - EXTRA
    width = qkv_ref.shape[2]
    total = left[0:base, :] + got[0:base, :].astype(F32)
    for p in range(3):
        qkv_ref[p] = total[:, p * width : (p + 1) * width]
    attn_ref[...] = jnp.transpose(total[:, 3 * width :])
    rows = slice(base, base + EXTRA)
    tile_ref[...] = left[rows, :].astype(BF).astype(F32) + got[rows, :].astype(F32)


def scatter_start(info, own, sib, tiles=(), after=()):
    base, columns = own.shape[1:]
    half = columns // 2
    rows = 4 * base + (EXTRA if tiles else 0)
    return call(
        functools.partial(scatter_first_kernel, len(sib)),
        [shape((rows, half), F32), shape((rows, half))] * 2,
        info,
        own,
        *[swap_core(piece) for piece in sib],
        *tiles,
        name="scatter_first",
        after=after,
    )


def scatter_send(state, bits):
    keep_a, send_a, keep_b, send_b = state
    return keep_a, swap_bit(send_a, bits[0]), keep_b, swap_bit(send_b, bits[1])


def scatter_middle(info, state, tiled, after=()):
    half = state[0].shape[1]
    extra = EXTRA if tiled else 0
    rows = (state[0].shape[0] - extra) // 2 + extra
    return call(
        functools.partial(scatter_second_kernel, tiled),
        [shape((rows, half), F32), shape((rows, half))] * 2,
        info,
        *state,
        name="scatter_second",
        cost=15 if tiled else 0,
        after=after,
    )


def scatter_late(info, state, tiled, after=()):
    half = state[0].shape[1]
    extra = EXTRA if tiled else 0
    rows = (state[0].shape[0] - extra) // 2 + extra
    left, send = call(
        functools.partial(scatter_third_kernel, tiled),
        [shape((rows, 2 * half), F32), shape((rows, 2 * half))],
        info,
        *state,
        name="scatter_third",
        cost=15 if tiled else 0,
        after=after,
    )
    return left, swap_bit(send, 2)


def scatter_plain(own, sib):
    sib = jnp.concatenate(sib, 2)
    total = own.astype(F32) + swap_core(sib).astype(F32)
    total = total.reshape(total.shape[0] * total.shape[1], total.shape[2])
    return lax.psum_scatter(total, "dp", scatter_dimension=0, tiled=True)


def body(
    inputs,
    segments,
    norm1_gain,
    norm1_shift,
    qkv_weight,
    qv_bias,
    attn_weight,
    attn_bias,
    norm2_gain,
    norm2_shift,
    fc_weight,
    fc_bias,
    proj_weight,
    proj_bias,
    cotangent,
):
    count = lax.axis_size("dp")
    index = lax.axis_index("dp")
    core = lax.axis_index("mp") % 2
    rows, depth = inputs.shape
    local = depth // count
    width = qkv_weight.shape[2]
    heads = width // HD
    units = fc_weight.shape[1]
    width2 = 2 * width
    heads2 = 2 * heads
    own_count = rows // 2
    base = depth // CHUNKS
    flip = index if count == CHUNKS else jnp.zeros_like(index)
    info = jnp.stack([flip, core]).astype(jnp.int32)
    seg_row = segments.reshape(1, rows)

    stat_one = call(
        stats_kernel, [shape((rows, 2 * TILE), F32)], info, inputs, name="stats"
    )[0]

    bias_width = qv_bias.shape[1]
    bias_rows = lax.dynamic_update_slice(
        jnp.zeros((heads, 2 * HD), BF), qv_bias, (0, index * bias_width)
    )
    bias_row = bias_rows.reshape(heads, 2, HD).transpose(1, 0, 2).reshape(1, width2)
    vectors = jnp.stack(
        [norm1_gain, norm1_shift, attn_bias, norm2_gain, norm2_shift, fc_bias[0], proj_bias]
    )
    placed = lax.dynamic_update_slice(
        jnp.zeros((vectors.shape[0], depth), BF), vectors, (0, index * local)
    )
    tile = jnp.concatenate(
        [
            placed,
            jnp.pad(bias_row, ((0, EXTRA - vectors.shape[0] - 1), (0, depth - width2))),
        ],
        0,
    )
    mats = jnp.concatenate(
        [qkv_weight.transpose(1, 0, 2).reshape(local, 3 * width), attn_weight.T], 1
    )
    wide = jnp.concatenate([fc_weight, proj_weight.T], 1)
    if count == CHUNKS:
        blocks = gather_blocks(jnp.concatenate([mats, tile], 0), stat_one)
        own_a = jnp.stack(blocks)
        far = swap_mask(lax.optimization_barrier((wide, blocks[4]))[0], 4)
        wide = lax.optimization_barrier((wide, own_a))[0]
    else:
        full = lax.all_gather(mats, "dp", axis=0, tiled=True).reshape(CHUNKS, base, depth)
        total = jnp.sum(lax.all_gather(tile, "dp", axis=0).astype(F32), 0).astype(BF)
        total = jnp.pad(total[None], ((0, CHUNKS - 1), (0, 0), (0, 0)))
        own_a = jnp.concatenate([full, total], 1)
        own_b = lax.all_gather(wide, "dp", axis=0, tiled=True).reshape(CHUNKS, base, 2 * units)
        own_b = [own_b[r] for r in range(CHUNKS)]
    sib_a = swap_core(own_a)
    weight = shape((depth, width2))
    q, k, v, wq, wk, wv, wo, first_own, vec, vec_sib = call(
        project_kernel,
        [
            shape((heads2, own_count, HD)),
            shape((heads2, rows, HD)),
            shape((heads2, rows, HD)),
            weight,
            weight,
            weight,
            weight,
            shape((own_count, depth)),
            shape((EXTRA, depth), F32),
            shape((EXTRA, depth), F32),
        ],
        info,
        inputs,
        stat_one,
        own_a,
        sib_a,
        scratch=[pltpu.VMEM((rows, depth), BF), pltpu.VMEM((rows, width2), F32)],
        cost=8,
        name="project",
    )
    if count == CHUNKS:
        blocks = gather_blocks(wide, q, far)
    tiles = own_count // TILE
    part, mixed, probs = call(
        attend_kernel,
        [
            shape((own_count, depth)),
            shape((own_count, width2)),
            shape((heads2, TILE, TILE * tiles * (tiles + 1))),
        ],
        info,
        q,
        k,
        v,
        wo,
        seg_row,
        scratch=[
            pltpu.VMEM((heads2 + 1, TILE, rows), F32),
            pltpu.VMEM((heads2, own_count, HD), F32),
        ],
        cost=16,
        name="attend",
    )
    got = swap_chip(part)
    if count == CHUNKS:
        own_b = lax.optimization_barrier((blocks, part))[0]
    sib_b = [swap_core(block) for block in own_b]
    hid = shape((own_count, 2 * units))
    full = shape((depth, 2 * units))
    fc_full, proj_full, dy, dact = call(
        mlp_pre_kernel,
        [full, full, shape((own_count, depth)), hid],
        info,
        seg_row,
        cotangent,
        *own_b,
        *sib_b,
        name="mlp_pre",
    )
    da, act, dhid, second, middle, stat_two = call(
        mlp_kernel,
        [
            shape((own_count, depth)),
            hid,
            hid,
            shape((own_count, depth)),
            shape((own_count, depth), F32),
            shape((own_count, 2 * TILE), F32),
        ],
        info,
        inputs,
        part,
        got,
        vec,
        vec_sib,
        fc_full,
        dact,
        scratch=[pltpu.VMEM((own_count, units), F32)],
        cost=10,
        name="mlp",
    )
    da_got = swap_chip(da)
    mlp_part, grad_own, *grad_sib, mlp_sums = call(
        mlp_grad_kernel,
        [
            shape((own_count, depth)),
            shape((CHUNKS, base, 2 * units)),
            *[shape((CHUNKS, base, units // 2))] * 4,
            shape((24, depth), F32),
        ],
        info,
        act,
        dhid,
        second,
        dy,
        proj_full,
        cost=9,
        name="mlp_grad",
    )
    mlp_got = swap_chip(mlp_part)
    exact = count == CHUNKS
    if exact:
        big_state = scatter_start(info, grad_own, grad_sib)
        big_sent = big_state[1]
        big_state = scatter_send(big_state, (0, 1))
    else:
        big = scatter_plain(grad_own, grad_sib)
        fc_weight_grad, proj_weight_grad = big[:, :units], big[:, units:].T

    dmid, branch, att_sums, dq, keep, *send = call(
        attend_back_kernel,
        [
            shape((own_count, depth), F32),
            shape((own_count, depth)),
            shape((8, depth), F32),
            shape((own_count, width2)),
            shape((2 * width2, own_count), F32),
            *[shape((width2, own_count))] * 2,
        ],
        info,
        middle,
        stat_two,
        dy,
        da,
        da_got,
        vec,
        wo,
        mixed,
        q,
        k,
        v,
        probs,
        scratch=[
            pltpu.VMEM((own_count, width2), BF),
            pltpu.VMEM((heads2, own_count, HD), BF),
            pltpu.VMEM((heads2, HD, rows), F32),
            pltpu.VMEM((heads2, HD, rows), F32),
            pltpu.VMEM((heads2, own_count, HD), F32),
            pltpu.VMEM((heads2, TILE, rows), F32),
            pltpu.VMEM((heads2, TILE, rows), BF),
            pltpu.VMEM((heads2, own_count, TILE), F32),
        ],
        cost=18,
        name="attend_back",
        after=(big_sent,) if exact else (),
    )
    keep_got = [swap_core(piece) for piece in send]
    if exact:
        big_state = scatter_middle(info, big_state, False, after=(dq, mlp_got))
        big_ready = big_state[0]
        big_state = scatter_send(big_state, (1, 0))
    first_part, dkv = call(
        first_grad_kernel,
        [shape((own_count, depth)), shape((2 * width2, own_count))],
        info,
        dq,
        keep,
        *keep_got,
        wq,
        wk,
        wv,
        name="first_grad",
        after=(big_ready,) if exact else (),
    )
    first_got = swap_chip(first_part)
    qkv_own, *qkv_sib, tile_own, tile_sib = call(
        qkv_grad_kernel,
        [
            shape((CHUNKS, base, 4 * width)),
            *[shape((CHUNKS, base, 2 * width))] * 2,
            *[shape((EXTRA, depth))] * 2,
        ],
        info,
        first_own,
        dq,
        dkv,
        branch,
        mixed,
        first_part,
        inputs,
        stat_one,
        mlp_sums,
        att_sums,
        scratch=[pltpu.VMEM((EXTRA, depth), F32)],
        cost=7,
        name="qkv_grad",
        after=(big_state[1], big_state[3]) if exact else (),
    )
    finish = lambda after: call(
        final_kernel,
        [shape((rows, depth))],
        info,
        inputs,
        stat_one,
        first_part,
        first_got,
        dmid,
        vec,
        seg_row,
        middle,
        mlp_part,
        mlp_got,
        name="final",
        cost=7,
        after=after,
    )[0]
    tiles = (tile_own, swap_core(tile_sib))
    if exact:
        big_last = scatter_late(info, big_state, False, after=(qkv_own,))
        small_state = scatter_start(info, qkv_own, qkv_sib, tiles, after=(big_last[0],))
        small_sent = small_state[1]
        small_state = scatter_send(small_state, (0, 1))
        both_low = finish((small_sent,))
        small_state = scatter_middle(info, small_state, True, after=(both_low, big_last[1]))
        small_state = scatter_send(small_state, (1, 0))
        fc_weight_grad, proj_weight_grad = call(
            scatter_big_kernel,
            [shape((local, units), F32), shape((units, local), F32)],
            info,
            *big_last,
            name="scatter_big",
            cost=15,
        )
        small_last = scatter_late(info, small_state, True)
        outputs, inputs_grad = all_rows(info, both_low, (small_last[0],))
        qkv_weight_grad, attn_weight_grad, tile = call(
            scatter_small_kernel,
            [
                shape((3, local, width), F32),
                shape((width, local), F32),
                shape((EXTRA, depth), F32),
            ],
            info,
            *small_last,
            name="scatter_small",
            cost=2,
            after=(fc_weight_grad, inputs_grad),
        )
    else:
        outputs, inputs_grad = all_rows(info, finish(()))
        mine = scatter_plain(qkv_own, qkv_sib)
        qkv_weight_grad = mine[:, : 3 * width].reshape(local, 3, width).transpose(1, 0, 2)
        attn_weight_grad = mine[:, 3 * width :].T
        tile = lax.psum(tiles[0].astype(F32) + tiles[1].astype(F32), "dp")
    tile_got = swap_chip(tile.astype(BF)).astype(F32)
    mask = (jnp.arange(EXTRA) < 2)[:, None]
    tile = jnp.where(mask, tile.astype(BF).astype(F32) + tile_got, tile)
    parts = lax.dynamic_slice(tile, (0, index * local), (7, local))
    bias_sum = tile[7, :width2].reshape(2, heads, HD).transpose(1, 0, 2).reshape(heads, 2 * HD)
    qv_bias_grad = lax.dynamic_slice(bias_sum, (0, index * bias_width), (heads, bias_width))
    return (
        outputs,
        inputs_grad,
        parts[0],
        parts[1],
        qkv_weight_grad,
        qv_bias_grad,
        attn_weight_grad,
        parts[2],
        parts[3],
        parts[4],
        fc_weight_grad,
        parts[5][None],
        proj_weight_grad,
        parts[6],
    )


def solution(mesh):
    return jax.shard_map(
        body,
        mesh=mesh,
        in_specs=(
            P("dp", None),
            P("dp"),
            P("dp"),
            P("dp"),
            P(None, "dp", "mp"),
            P("mp", "dp"),
            P("mp", "dp"),
            P("dp"),
            P("dp"),
            P("dp"),
            P("dp", "mp"),
            P("mp", "dp"),
            P("mp", "dp"),
            P("dp"),
            P("dp", None),
        ),
        out_specs=(
            P("dp", None),
            P("dp", None),
            P("dp"),
            P("dp"),
            P(None, "dp", "mp"),
            P("mp", "dp"),
            P("mp", "dp"),
            P("dp"),
            P("dp"),
            P("dp"),
            P("dp", "mp"),
            P("mp", "dp"),
            P("mp", "dp"),
            P("dp"),
        ),
        check_vma=False,
    )
```

```python
import functools

import jax
import jax.numpy as jnp
from jax import lax
from jax.experimental import pallas as pl
from jax.experimental.pallas import tpu as pltpu
from jax.sharding import PartitionSpec as P

HD = 64
TILE = 128
EXTRA = 16
CHUNKS = 8
EPSILON = 1e-05
NEGATIVE = -1e30
BF = jnp.bfloat16
F32 = jnp.float32
CORE_PAIRS = ((0, 1), (1, 0), (2, 3), (3, 2))
CHIP_PAIRS = ((0, 2), (2, 0), (1, 3), (3, 1))
CURVE = 0.7978845608028654


def dot(left, right, left_dim, right_dim):
    return lax.dot_general(
        left, right, (((left_dim,), (right_dim,)), ((), ())), preferred_element_type=F32
    )


def swap_core(value):
    return lax.ppermute(value, "mp", CORE_PAIRS)


def swap_chip(value):
    return lax.ppermute(value, "mp", CHIP_PAIRS)


def swap_mask(value, mask):
    return lax.ppermute(value, "dp", [(i, i ^ mask) for i in range(CHUNKS)])


def swap_bit(value, bit):
    return swap_mask(value, 1 << bit)


def call(kernel, outs, *args, scratch=(), smem=1, cost=0, name=None, after=()):
    first, behind = len(args), len(args) + len(after)

    def run(*refs):
        kernel(*refs[:first], *refs[behind:])

    specs = [pl.BlockSpec(memory_space=pltpu.SMEM)] * smem
    specs += [pl.BlockSpec(memory_space=pltpu.VMEM)] * (len(args) - smem)
    specs += [pl.BlockSpec(memory_space=pl.ANY)] * len(after)
    return pl.pallas_call(
        run,
        out_shape=outs,
        in_specs=specs,
        out_specs=[pl.BlockSpec(memory_space=pltpu.VMEM)] * len(outs),
        scratch_shapes=list(scratch),
        compiler_params=pltpu.CompilerParams(vmem_limit_bytes=56 * 1024 * 1024),
        cost_estimate=pl.CostEstimate(flops=cost * 10**9, bytes_accessed=1024, transcendentals=0),
        name=name,
    )(*args, *after)


def shape(dims, dtype=BF):
    return jax.ShapeDtypeStruct(tuple(dims), dtype)


def gather_blocks(message, behind, far=None):
    got = {0: message}
    got[4] = swap_mask(message, 4) if far is None else far
    got[2] = swap_mask(message, 2)
    got[1] = swap_mask(message, 1)
    four, two = lax.optimization_barrier((got[4], got[2], behind))[:2]
    got[7] = swap_mask(four, 3)
    got[5] = swap_mask(four, 1)
    got[6] = swap_mask(four, 2)
    got[3] = swap_mask(two, 1)
    return [got[r] for r in range(CHUNKS)]


def loop(count, step, fn, unroll=4):
    def run(i, carry):
        fn(pl.multiple_of(i * step, step))
        return carry

    lax.fori_loop(0, count // step, run, 0, unroll=unroll)


def norm_backward(incoming, scaled, factor, gain):
    weighted = incoming * gain
    first_mean = jnp.mean(weighted, -1, keepdims=True)
    second_mean = jnp.mean(weighted * scaled, -1, keepdims=True)
    return factor * (weighted - first_mean - scaled * second_mean)


def tile_sum(ref, base):
    total = ref[0, base : base + EXTRA, :].astype(F32)
    for r in range(1, CHUNKS):
        total = total + ref[r, base : base + EXTRA, :].astype(F32)
    return total


def own_start(start, core):
    tile = start // TILE
    return pl.multiple_of((2 * tile + core) * TILE + start % TILE, 32)


def fold(value):
    return jnp.sum(value.reshape(value.shape[0] // 8, 8, value.shape[1]), 0)


def colsum(value):
    return jnp.sum(value, 0, keepdims=True)


def spread_stats(value):
    average = jnp.mean(value, -1, keepdims=True)
    centred = value - average
    factor = lax.rsqrt(jnp.mean(centred * centred, -1, keepdims=True) + EPSILON)
    rows = value.shape[0]
    return jnp.concatenate(
        [jnp.broadcast_to(average, (rows, TILE)), jnp.broadcast_to(factor, (rows, TILE))], 1
    )


def stats_kernel(info, x_ref, stat_ref):
    def run(at):
        rs = pl.ds(at, 32)
        stat_ref[rs, :] = spread_stats(x_ref[rs, :].astype(F32))

    loop(x_ref.shape[0], 32, run)


def project_kernel(
    info,
    x_ref,
    stat_ref,
    own_ref,
    sib_ref,
    q_ref,
    k_ref,
    v_ref,
    wq_ref,
    wk_ref,
    wv_ref,
    wo_ref,
    firstown_ref,
    vec_ref,
    vecsib_ref,
    low_ref,
    proj_ref,
):
    flip, core = info[0], info[1]
    width = own_ref.shape[2] // 4
    base = own_ref.shape[1] - EXTRA
    rows = low_ref.shape[0]
    heads = 2 * width // HD
    own_count = rows // 2
    vec_ref[...] = tile_sum(own_ref, base)
    vecsib_ref[...] = tile_sum(sib_ref, base)
    gain, shift = vec_ref[0:1, :], vec_ref[1:2, :]

    def norm(at):
        rs = pl.ds(at, 32)
        scaled = (x_ref[rs, :].astype(F32) - stat_ref[rs, 0:1]) * stat_ref[rs, TILE : TILE + 1]
        low_ref[rs, :] = (scaled * gain + shift).astype(BF)

    loop(rows, 32, norm)
    for r in range(CHUNKS):
        at = pl.multiple_of((r ^ flip) * base, 32)
        for side, ref in ((0, own_ref), (1, sib_ref)):
            for part, out in enumerate((wq_ref, wk_ref, wv_ref, wo_ref)):
                out[pl.ds(at, base), side * width : (side + 1) * width] = ref[
                    r, 0:base, part * width : (part + 1) * width
                ]
    bias_q = jnp.concatenate([vec_ref[7:8, :width], vecsib_ref[7:8, :width]], 1)
    bias_v = jnp.concatenate(
        [vec_ref[7:8, width : 2 * width], vecsib_ref[7:8, width : 2 * width]], 1
    )
    for j in range(own_count // TILE):
        at = own_start(j * TILE, core)
        firstown_ref[j * TILE : (j + 1) * TILE, :] = low_ref[pl.ds(at, TILE), :]
    scale = float(HD) ** -0.5
    proj_ref[0:own_count, :] = dot(firstown_ref[...], wq_ref[...], 1, 0) + bias_q
    for h in range(heads):
        q_ref[h] = (
            proj_ref[0:own_count, h * HD : (h + 1) * HD].astype(BF).astype(F32) * scale
        ).astype(BF)
    proj_ref[...] = dot(low_ref[...], wk_ref[...], 1, 0)
    for h in range(heads):
        k_ref[h] = proj_ref[:, h * HD : (h + 1) * HD].astype(BF)
    proj_ref[...] = dot(low_ref[...], wv_ref[...], 1, 0) + bias_v
    for h in range(heads):
        v_ref[h] = proj_ref[:, h * HD : (h + 1) * HD].astype(BF)


def attend_kernel(
    info, q_ref, k_ref, v_ref, wo_ref, seg_ref, part_ref, mixed_ref, probs_ref, s_ref, o_ref
):
    core = info[1]
    heads, own_count = q_ref.shape[:2]
    lane = lax.broadcasted_iota(jnp.int32, (TILE, TILE), 1)
    line = lax.broadcasted_iota(jnp.int32, (TILE, TILE), 0)
    for j in range(own_count // TILE):
        end = (j + 1) * 2 * TILE
        off = TILE * j * (j + 1)
        at = own_start(j * TILE, core)
        seg_tile = jnp.broadcast_to(seg_ref[0:1, pl.ds(at, TILE)], (TILE, TILE))
        seg_col = jnp.max(jnp.where(lane == line, seg_tile, -2), -1, keepdims=True)
        place = lax.broadcasted_iota(jnp.int32, (TILE, end), 1)
        own_place = at + lax.broadcasted_iota(jnp.int32, (TILE, end), 0)
        allowed = (seg_col == seg_ref[0:1, 0:end]) & (place <= own_place)
        bias = jnp.where(allowed, 0.0, NEGATIVE)
        s_ref[heads, :, 0:end] = bias

        def run(h, carry, j=j, end=end, off=off):
            scores = dot(q_ref[h, j * TILE : (j + 1) * TILE, :], k_ref[h, 0:end, :], 1, 1)
            s_ref[h, :, 0:end] = scores
            for sub in range(4):
                sl = slice(sub * 32, sub * 32 + 32)
                sc = s_ref[h, sl, 0:end] + s_ref[heads, sl, 0:end]
                weights = jnp.exp(sc - jnp.max(sc, -1, keepdims=True))
                inverse = 1.0 / jnp.sum(weights, -1, keepdims=True)
                probs_ref[h, sl, off : off + end] = (weights * inverse).astype(BF)
            o_ref[h, j * TILE : (j + 1) * TILE, :] = dot(
                probs_ref[h, :, off : off + end], v_ref[h, 0:end, :], 1, 0
            )
            return carry

        lax.fori_loop(0, heads, run, 0, unroll=True)
    for h in range(heads):
        mixed_ref[:, h * HD : (h + 1) * HD] = o_ref[h].astype(BF)
    part_ref[...] = dot(mixed_ref[...], wo_ref[...], 1, 1).astype(BF)


def mlp_pre_kernel(info, seg_ref, cot_ref, *refs):
    own_refs, sib_refs = refs[:CHUNKS], refs[CHUNKS : 2 * CHUNKS]
    fc_ref, proj_ref, dy_ref, dact_ref = refs[2 * CHUNKS :]
    flip, core = info[0], info[1]
    own_count = dy_ref.shape[0]
    base = own_refs[0].shape[0]
    units = own_refs[0].shape[1] // 2
    sub = 32
    lane = lax.broadcasted_iota(jnp.int32, (sub, TILE), 1)
    line = lax.broadcasted_iota(jnp.int32, (sub, TILE), 0)

    def mask(at):
        src = own_start(at, core)
        tile_at = pl.multiple_of((2 * (at // TILE) + core) * TILE, TILE)
        seg_tile = jnp.broadcast_to(seg_ref[0:1, pl.ds(tile_at, TILE)], (sub, TILE))
        seg_col = jnp.max(
            jnp.where(lane == line + at % TILE, seg_tile, -2), -1, keepdims=True
        )
        cot = cot_ref[pl.ds(src, sub), :].astype(F32)
        dy_ref[pl.ds(at, sub), :] = jnp.where(seg_col >= 0, cot, 0.0).astype(BF)

    loop(own_count, sub, mask)
    for r in range(CHUNKS):
        at = pl.multiple_of((r ^ flip) * base, 32)
        for side, ref in ((0, own_refs[r]), (1, sib_refs[r])):
            cols = slice(side * units, (side + 1) * units)
            fc_ref[pl.ds(at, base), cols] = ref[:, 0:units]
            proj_ref[pl.ds(at, base), cols] = ref[:, units : 2 * units]
    for side in range(2):
        cols = slice(side * units, (side + 1) * units)
        dact_ref[:, cols] = dot(dy_ref[...], proj_ref[:, cols], 1, 0).astype(BF)


def mlp_kernel(
    info,
    x_ref,
    part_ref,
    recv_ref,
    vec_ref,
    vecsib_ref,
    fc_ref,
    dact_ref,
    da_ref,
    act_ref,
    dhid_ref,
    second_ref,
    mid_ref,
    stat_ref,
    hid_ref,
):
    core = info[1]
    own_count = part_ref.shape[0]
    units = fc_ref.shape[1] // 2
    gain, shift, bias = vec_ref[3:4, :], vec_ref[4:5, :], vec_ref[2:3, :]
    sub = 32

    def first(at):
        src = own_start(at, core)
        rows = pl.ds(at, sub)
        middle = (
            x_ref[pl.ds(src, sub), :].astype(F32)
            + (part_ref[rows, :].astype(F32) + recv_ref[rows, :].astype(F32))
            + bias
        )
        mid_ref[rows, :] = middle
        stats = spread_stats(middle)
        stat_ref[rows, :] = stats
        scaled = (middle - stats[:, 0:1]) * stats[:, TILE : TILE + 1]
        second_ref[rows, :] = (scaled * gain + shift).astype(BF)

    loop(own_count, sub, first)
    for side, biases in ((0, vec_ref), (1, vecsib_ref)):
        cols = slice(side * units, (side + 1) * units)
        hid_ref[...] = dot(second_ref[...], fc_ref[:, cols], 1, 0)
        bias_fc = biases[5:6, :]

        def gelu(at, cols=cols, bias_fc=bias_fc):
            rows = pl.ds(at, 16)
            u = hid_ref[rows, :] + bias_fc
            u2 = u * u
            bend = jnp.tanh(CURVE * u * (1.0 + 0.044715 * u2))
            half = 0.5 * (1.0 + bend)
            act_ref[rows, cols] = (u * half).astype(BF)
            slope = half + (0.5 * CURVE) * u * (1.0 - bend * bend) * (1.0 + 0.134145 * u2)
            dhid_ref[rows, cols] = (dact_ref[rows, cols].astype(F32) * slope).astype(BF)

        loop(own_count, 16, gelu)
    da_ref[...] = dot(dhid_ref[...], fc_ref[...], 1, 1).astype(BF)


def mlp_grad_kernel(
    info,
    act_ref,
    dhid_ref,
    second_ref,
    dy_ref,
    proj_ref,
    part_ref,
    own_ref,
    sib_a_ref,
    sib_b_ref,
    sib_c_ref,
    sib_d_ref,
    sums_ref,
):
    sib_refs = ((sib_a_ref, sib_b_ref), (sib_c_ref, sib_d_ref))
    base, units = own_ref.shape[1], own_ref.shape[2] // 2
    half = units // 2
    part_ref[...] = dot(act_ref[...], proj_ref[...], 1, 1).astype(BF)
    for kind, left, right in ((0, second_ref, dhid_ref), (1, dy_ref, act_ref)):
        for side in range(2):
            value = dot(left[...], right[:, side * units : (side + 1) * units], 0, 0).astype(BF)
            for b in range(CHUNKS):
                block = value[b * base : (b + 1) * base, :]
                if side:
                    sib_refs[kind][0][b] = block[:, :half]
                    sib_refs[kind][1][b] = block[:, half:]
                else:
                    own_ref[b, :, kind * units : (kind + 1) * units] = block
    one = jnp.ones((8, act_ref.shape[0]), BF)
    fc_sums = dot(one, dhid_ref[...], 1, 0)
    sums_ref[0:8, :] = fc_sums[:, 0:units]
    sums_ref[8:16, :] = fc_sums[:, units : 2 * units]
    sums_ref[16:24, :] = dot(one, dy_ref[...], 1, 0)


def attend_back_kernel(
    info,
    mid_ref,
    stat_ref,
    dy_ref,
    da_ref,
    recv_ref,
    vec_ref,
    wo_ref,
    mixed_ref,
    q_ref,
    k_ref,
    v_ref,
    probs_ref,
    dmid_ref,
    branch_ref,
    sums_ref,
    dq_ref,
    keep_ref,
    send_k_ref,
    send_v_ref,
    dm_ref,
    do_ref,
    dkt_ref,
    dvt_ref,
    dqh_ref,
    dp_ref,
    ds_ref,
    delta_ref,
    acc_ref,
):
    core = info[1]
    own_count = mid_ref.shape[0]
    heads = q_ref.shape[0]
    rows = k_ref.shape[1]
    gain = vec_ref[3:4, :]
    sums_ref[...] = jnp.zeros_like(sums_ref)
    sub = 32

    def first(at):
        rs = pl.ds(at, sub)
        factor = stat_ref[rs, TILE : TILE + 1]
        scaled = (mid_ref[rs, :] - stat_ref[rs, 0:1]) * factor
        incoming = da_ref[rs, :].astype(F32) + recv_ref[rs, :].astype(F32)
        dmid = dy_ref[rs, :].astype(F32) + norm_backward(incoming, scaled, factor, gain)
        dmid_ref[rs, :] = dmid
        low = dmid.astype(BF)
        branch_ref[rs, :] = low
        acc_ref[0] += fold(low.astype(F32))
        acc_ref[1] += fold(incoming * scaled)
        acc_ref[2] += fold(incoming)

    acc_ref[...] = jnp.zeros_like(acc_ref)
    loop(own_count, sub, first)
    for i in range(3):
        sums_ref[2 + i : 3 + i, :] = colsum(acc_ref[i])
    dm_ref[...] = dot(branch_ref[...], wo_ref[...], 1, 0).astype(BF)
    for h in range(heads):
        cols = slice(h * HD, (h + 1) * HD)
        do_ref[h] = dm_ref[:, cols]
        delta_ref[h] = jnp.broadcast_to(
            jnp.sum(
                dm_ref[:, cols].astype(F32) * mixed_ref[:, cols].astype(F32), -1, keepdims=True
            ),
            (own_count, TILE),
        )
    scale = float(HD) ** -0.5

    def head(h, carry):
        for j in reversed(range(own_count // TILE)):
            end = (j + 1) * 2 * TILE
            off = TILE * j * (j + 1)
            rs = slice(j * TILE, (j + 1) * TILE)
            dp_ref[h, :, 0:end] = dot(do_ref[h, rs, :], v_ref[h, 0:end, :], 1, 1)
            for s in range(4):
                sl = slice(s * 32, s * 32 + 32)
                delta = delta_ref[h, j * TILE + s * 32 : j * TILE + s * 32 + 32, 0:1]
                p = probs_ref[h, sl, off : off + end].astype(F32)
                ds_ref[h, sl, 0:end] = (p * (dp_ref[h, sl, 0:end] - delta)).astype(BF)
            ds = ds_ref[h, :, 0:end]
            dqh_ref[h, rs, :] = dot(ds, k_ref[h, 0:end, :], 1, 0) * scale
            dk = dot(q_ref[h, rs, :], ds, 0, 0)
            dv = dot(do_ref[h, rs, :], probs_ref[h, :, off : off + end], 0, 0)
            if j == own_count // TILE - 1:
                dkt_ref[h] = dk
                dvt_ref[h] = dv
            else:
                dkt_ref[h, :, 0:end] += dk
                dvt_ref[h, :, 0:end] += dv
        return carry

    lax.fori_loop(0, heads, head, 0, unroll=True)
    width2 = heads * HD
    for h in range(heads):
        dq_ref[:, h * HD : (h + 1) * HD] = dqh_ref[h].astype(BF)
        twin = (h + heads // 2) % heads
        for j in range(own_count // TILE):
            mine = pl.multiple_of((2 * j + core) * TILE, TILE)
            yours = pl.multiple_of((2 * j + 1 - core) * TILE, TILE)
            cols = slice(j * TILE, (j + 1) * TILE)
            for part, ref, send in ((0, dkt_ref, send_k_ref), (1, dvt_ref, send_v_ref)):
                at = part * width2
                keep_ref[at + h * HD : at + (h + 1) * HD, cols] = ref[h, :, pl.ds(mine, TILE)]
                send[twin * HD : (twin + 1) * HD, cols] = ref[h, :, pl.ds(yours, TILE)].astype(BF)


def first_grad_kernel(
    info, dq_ref, keep_ref, got_k_ref, got_v_ref, wq_ref, wk_ref, wv_ref, part_ref, dkv_ref
):
    width2 = dq_ref.shape[1]
    for p, got in enumerate((got_k_ref, got_v_ref)):
        rows = slice(p * width2, (p + 1) * width2)
        dkv_ref[rows, :] = (keep_ref[rows, :] + got[...].astype(F32)).astype(BF)
    part_ref[...] = (
        dot(dq_ref[...], wq_ref[...], 1, 1)
        + dot(dkv_ref[0:width2, :], wk_ref[...], 0, 1)
        + dot(dkv_ref[width2 : 2 * width2, :], wv_ref[...], 0, 1)
    ).astype(BF)


def qkv_grad_kernel(
    info,
    first_ref,
    dq_ref,
    dkv_ref,
    branch_ref,
    mixed_ref,
    part_ref,
    x_ref,
    stat_ref,
    mlp_sums_ref,
    att_sums_ref,
    own_ref,
    sib_a_ref,
    sib_b_ref,
    tile_own_ref,
    tile_sib_ref,
    sum_ref,
    acc_ref,
):
    core = info[1]
    width2 = dq_ref.shape[1]
    width = width2 // 2
    base = own_ref.shape[1]
    for part in range(4):
        if part == 0:
            whole = dot(first_ref[...], dq_ref[...], 0, 0)
        elif part == 3:
            whole = dot(branch_ref[...], mixed_ref[...], 0, 0)
        else:
            whole = dot(
                first_ref[...], dkv_ref[(part - 1) * width2 : part * width2, :], 0, 1
            )
        whole = whole.astype(BF)
        cols = slice(part * width, (part + 1) * width)
        side_cols = slice(part % 2 * width, (part % 2 + 1) * width)
        for b in range(CHUNKS):
            block = whole[b * base : (b + 1) * base, :]
            own_ref[b, :, cols] = block[:, 0:width]
            (sib_a_ref, sib_b_ref)[part // 2][b, :, side_cols] = block[:, width:width2]
    sum_ref[...] = jnp.zeros_like(sum_ref)

    def run(at):
        src = own_start(at, core)
        rs = pl.ds(src, 32)
        scaled = (x_ref[rs, :].astype(F32) - stat_ref[rs, 0:1]) * stat_ref[rs, TILE : TILE + 1]
        incoming = part_ref[pl.ds(at, 32), :].astype(F32)
        acc_ref[0] += fold(incoming * scaled)
        acc_ref[1] += fold(incoming)

    acc_ref[...] = jnp.zeros_like(acc_ref)
    loop(part_ref.shape[0], 32, run)
    for i in range(2):
        sum_ref[i : i + 1, :] = colsum(acc_ref[i])
    ones = jnp.ones((8, dq_ref.shape[0]), BF)
    qs = dot(ones, dq_ref[...], 1, 0)[0:1, :]
    vs = dot(ones, dkv_ref[width2 : 2 * width2, :], 1, 1)[0:1, :]
    sum_ref[2:5, :] = att_sums_ref[2:5, :]
    sum_ref[6:7, :] = mlp_sums_ref[16:17, :]
    for side, out in ((0, tile_own_ref), (1, tile_sib_ref)):
        sl = slice(side * width, (side + 1) * width)
        sum_ref[5:6, :] = mlp_sums_ref[8 * side : 8 * side + 1, :]
        sum_ref[7:8, 0:width] = qs[:, sl]
        sum_ref[7:8, width : 2 * width] = vs[:, sl]
        out[...] = sum_ref[...].astype(BF)


def final_kernel(
    info,
    x_ref,
    stat_ref,
    part_ref,
    recv_ref,
    dmid_ref,
    vec_ref,
    seg_ref,
    mid_ref,
    mlp_ref,
    mlp_got_ref,
    out_ref,
):
    core = info[1]
    own_count = part_ref.shape[0]
    gain, bias = vec_ref[0:1, :], vec_ref[6:7, :]
    sub = 32
    lane = lax.broadcasted_iota(jnp.int32, (sub, TILE), 1)
    line = lax.broadcasted_iota(jnp.int32, (sub, TILE), 0)

    def run(at):
        src = own_start(at, core)
        rs = pl.ds(at, sub)
        factor = stat_ref[pl.ds(src, sub), TILE : TILE + 1]
        scaled = (x_ref[pl.ds(src, sub), :].astype(F32) - stat_ref[pl.ds(src, sub), 0:1]) * factor
        incoming = part_ref[rs, :].astype(F32) + recv_ref[rs, :].astype(F32)
        out_ref[pl.ds(own_count + at, sub), :] = (
            dmid_ref[rs, :] + norm_backward(incoming, scaled, factor, gain)
        ).astype(BF)
        tile_at = pl.multiple_of((2 * (at // TILE) + core) * TILE, TILE)
        seg_tile = jnp.broadcast_to(seg_ref[0:1, pl.ds(tile_at, TILE)], (sub, TILE))
        seg_col = jnp.max(
            jnp.where(lane == line + at % TILE, seg_tile, -2), -1, keepdims=True
        )
        final = (
            mid_ref[rs, :]
            + (mlp_ref[rs, :].astype(F32) + mlp_got_ref[rs, :].astype(F32))
            + bias
        )
        out_ref[rs, :] = jnp.where(seg_col >= 0, final, 0.0).astype(BF)

    loop(own_count, sub, run)


def merge_kernel(info, own_ref, got_ref, first_ref, second_ref):
    core = info[1]
    count = first_ref.shape[0] // (2 * TILE)
    for i in range(2 * count):
        out, j = (first_ref, second_ref)[i // count], i % count
        sl = slice(i * TILE, (i + 1) * TILE)
        mine = pl.multiple_of((2 * j + core) * TILE, TILE)
        yours = pl.multiple_of((2 * j + 1 - core) * TILE, TILE)
        out[pl.ds(mine, TILE), :] = own_ref[sl, :]
        out[pl.ds(yours, TILE), :] = got_ref[sl, :]


def all_rows(info, own, after=()):
    return call(
        merge_kernel,
        [shape(own.shape)] * 2,
        info,
        own,
        swap_core(own),
        name="merge",
        cost=4,
        after=after,
    )


def scatter_first_kernel(pieces, info, own_ref, *refs):
    got_refs, refs = refs[:pieces], refs[pieces:]
    tiles, (keep_a, send_a, keep_b, send_b) = refs[:-4], refs[-4:]
    flip = info[0]
    base = own_ref.shape[1]
    half = own_ref.shape[2] // 2
    span = own_ref.shape[2] // pieces
    for side, keep, send in ((0, keep_a, send_a), (1, keep_b, send_b)):
        cols = slice(side * half, (side + 1) * half)
        kept, sent = 0, 0
        for r in range(CHUNKS):
            rows = slice(sent * base, (sent + 1) * base)
            if not (r >> side) & 1:
                rows = slice(kept * base, (kept + 1) * base)
            for p in range(pieces // 2):
                piece = side * (pieces // 2) + p
                value = own_ref[r ^ flip, :, piece * span : (piece + 1) * span].astype(F32)
                value = value + got_refs[piece][r ^ flip].astype(F32)
                if (r >> side) & 1:
                    send[rows, p * span : (p + 1) * span] = value.astype(BF)
                else:
                    keep[rows, p * span : (p + 1) * span] = value
            sent += (r >> side) & 1
            kept += 1 - ((r >> side) & 1)
        if tiles:
            value = tiles[0][:, cols].astype(F32) + tiles[1][:, cols].astype(F32)
            send[4 * base : 4 * base + EXTRA, :] = value.astype(BF)
            keep[4 * base : 4 * base + EXTRA, :] = value


def scatter_second_kernel(
    tiled, info, keep_a, got_a, keep_b, got_b, next_a, send_a, next_b, send_b
):
    extra = EXTRA if tiled else 0
    base = (keep_a.shape[0] - extra) // 4
    for keep, got, left, send, order in (
        (keep_a, got_a, next_a, send_a, (0, 1, 0, 1)),
        (keep_b, got_b, next_b, send_b, (0, 1, 0, 1)),
    ):
        kept, sent = 0, 0
        for r in range(4):
            rows = slice(r * base, (r + 1) * base)
            value = keep[rows, :] + got[rows, :].astype(F32)
            if order[r]:
                send[sent * base : (sent + 1) * base, :] = value.astype(BF)
                sent += 1
            else:
                left[kept * base : (kept + 1) * base, :] = value
                kept += 1
        if tiled:
            low = keep[4 * base : 4 * base + extra, :].astype(BF).astype(F32)
            value = low + got[4 * base : 4 * base + extra, :].astype(F32)
            send[2 * base : 2 * base + extra, :] = value.astype(BF)
            left[2 * base : 2 * base + extra, :] = value


def scatter_third_kernel(tiled, info, keep_a, got_a, keep_b, got_b, left, send):
    extra = EXTRA if tiled else 0
    base = (keep_a.shape[0] - extra) // 2
    half = keep_a.shape[1]
    for keep, got, at in ((keep_a, got_a, 0), (keep_b, got_b, half)):
        cols = slice(at, at + half)
        left[0:base, cols] = keep[0:base, :] + got[0:base, :].astype(F32)
        send[0:base, cols] = (
            keep[base : 2 * base, :] + got[base : 2 * base, :].astype(F32)
        ).astype(BF)
        if tiled:
            rows = slice(2 * base, 2 * base + extra)
            value = keep[rows, :].astype(BF).astype(F32) + got[rows, :].astype(F32)
            left[base : base + extra, cols] = value
            send[base : base + extra, cols] = value.astype(BF)


def scatter_big_kernel(info, left, got, fc_ref, proj_ref):
    units = fc_ref.shape[1]
    total = left[...] + got[...].astype(F32)
    fc_ref[...] = total[:, :units]
    proj_ref[...] = jnp.transpose(total[:, units:])


def scatter_small_kernel(info, left, got, qkv_ref, attn_ref, tile_ref, tile_low_ref):
    base = left.shape[0] - EXTRA
    width = qkv_ref.shape[2]
    total = left[0:base, :] + got[0:base, :].astype(F32)
    for p in range(3):
        qkv_ref[p] = total[:, p * width : (p + 1) * width]
    attn_ref[...] = jnp.transpose(total[:, 3 * width :])
    rows = slice(base, base + EXTRA)
    tile = left[rows, :].astype(BF).astype(F32) + got[rows, :].astype(F32)
    tile_ref[...] = tile
    tile_low_ref[...] = tile.astype(BF)


def scatter_start(info, own, sib, tiles=(), after=()):
    base, columns = own.shape[1:]
    half = columns // 2
    rows = 4 * base + (EXTRA if tiles else 0)
    return call(
        functools.partial(scatter_first_kernel, len(sib)),
        [shape((rows, half), F32), shape((rows, half))] * 2,
        info,
        own,
        *[swap_core(piece) for piece in sib],
        *tiles,
        name="scatter_first",
        after=after,
    )


def scatter_send(state, bits):
    keep_a, send_a, keep_b, send_b = state
    return keep_a, swap_bit(send_a, bits[0]), keep_b, swap_bit(send_b, bits[1])


def scatter_middle(info, state, tiled, after=()):
    half = state[0].shape[1]
    extra = EXTRA if tiled else 0
    rows = (state[0].shape[0] - extra) // 2 + extra
    return call(
        functools.partial(scatter_second_kernel, tiled),
        [shape((rows, half), F32), shape((rows, half))] * 2,
        info,
        *state,
        name="scatter_second",
        cost=15 if tiled else 0,
        after=after,
    )


def scatter_late(info, state, tiled, after=()):
    half = state[0].shape[1]
    extra = EXTRA if tiled else 0
    rows = (state[0].shape[0] - extra) // 2 + extra
    left, send = call(
        functools.partial(scatter_third_kernel, tiled),
        [shape((rows, 2 * half), F32), shape((rows, 2 * half))],
        info,
        *state,
        name="scatter_third",
        cost=15 if tiled else 0,
        after=after,
    )
    return left, swap_bit(send, 2)


def scatter_plain(own, sib):
    sib = jnp.concatenate(sib, 2)
    total = own.astype(F32) + swap_core(sib).astype(F32)
    total = total.reshape(total.shape[0] * total.shape[1], total.shape[2])
    return lax.psum_scatter(total, "dp", scatter_dimension=0, tiled=True)


def body(
    inputs,
    segments,
    norm1_gain,
    norm1_shift,
    qkv_weight,
    qv_bias,
    attn_weight,
    attn_bias,
    norm2_gain,
    norm2_shift,
    fc_weight,
    fc_bias,
    proj_weight,
    proj_bias,
    cotangent,
):
    count = lax.axis_size("dp")
    index = lax.axis_index("dp")
    core = lax.axis_index("mp") % 2
    rows, depth = inputs.shape
    local = depth // count
    width = qkv_weight.shape[2]
    heads = width // HD
    units = fc_weight.shape[1]
    width2 = 2 * width
    heads2 = 2 * heads
    own_count = rows // 2
    base = depth // CHUNKS
    flip = index if count == CHUNKS else jnp.zeros_like(index)
    info = jnp.stack([flip, core]).astype(jnp.int32)
    seg_row = segments.reshape(1, rows)

    stat_one = call(
        stats_kernel, [shape((rows, 2 * TILE), F32)], info, inputs, name="stats"
    )[0]

    bias_width = qv_bias.shape[1]
    bias_rows = lax.dynamic_update_slice(
        jnp.zeros((heads, 2 * HD), BF), qv_bias, (0, index * bias_width)
    )
    bias_row = bias_rows.reshape(heads, 2, HD).transpose(1, 0, 2).reshape(1, width2)
    vectors = jnp.stack(
        [norm1_gain, norm1_shift, attn_bias, norm2_gain, norm2_shift, fc_bias[0], proj_bias]
    )
    placed = lax.dynamic_update_slice(
        jnp.zeros((vectors.shape[0], depth), BF), vectors, (0, index * local)
    )
    tile = jnp.concatenate(
        [
            placed,
            jnp.pad(bias_row, ((0, EXTRA - vectors.shape[0] - 1), (0, depth - width2))),
        ],
        0,
    )
    mats = jnp.concatenate(
        [qkv_weight.transpose(1, 0, 2).reshape(local, 3 * width), attn_weight.T], 1
    )
    wide = jnp.concatenate([fc_weight, proj_weight.T], 1)
    if count == CHUNKS:
        blocks = gather_blocks(jnp.concatenate([mats, tile], 0), stat_one)
        own_a = jnp.stack(blocks)
        far = swap_mask(lax.optimization_barrier((wide, blocks[4]))[0], 4)
        wide = lax.optimization_barrier((wide, own_a))[0]
    else:
        full = lax.all_gather(mats, "dp", axis=0, tiled=True).reshape(CHUNKS, base, depth)
        total = jnp.sum(lax.all_gather(tile, "dp", axis=0).astype(F32), 0).astype(BF)
        total = jnp.pad(total[None], ((0, CHUNKS - 1), (0, 0), (0, 0)))
        own_a = jnp.concatenate([full, total], 1)
        own_b = lax.all_gather(wide, "dp", axis=0, tiled=True).reshape(CHUNKS, base, 2 * units)
        own_b = [own_b[r] for r in range(CHUNKS)]
    sib_a = swap_core(own_a)
    weight = shape((depth, width2))
    q, k, v, wq, wk, wv, wo, first_own, vec, vec_sib = call(
        project_kernel,
        [
            shape((heads2, own_count, HD)),
            shape((heads2, rows, HD)),
            shape((heads2, rows, HD)),
            weight,
            weight,
            weight,
            weight,
            shape((own_count, depth)),
            shape((EXTRA, depth), F32),
            shape((EXTRA, depth), F32),
        ],
        info,
        inputs,
        stat_one,
        own_a,
        sib_a,
        scratch=[pltpu.VMEM((rows, depth), BF), pltpu.VMEM((rows, width2), F32)],
        cost=8,
        name="project",
    )
    if count == CHUNKS:
        blocks = gather_blocks(wide, q, far)
    tiles = own_count // TILE
    part, mixed, probs = call(
        attend_kernel,
        [
            shape((own_count, depth)),
            shape((own_count, width2)),
            shape((heads2, TILE, TILE * tiles * (tiles + 1))),
        ],
        info,
        q,
        k,
        v,
        wo,
        seg_row,
        scratch=[
            pltpu.VMEM((heads2 + 1, TILE, rows), F32),
            pltpu.VMEM((heads2, own_count, HD), F32),
        ],
        cost=16,
        name="attend",
    )
    got = swap_chip(part)
    if count == CHUNKS:
        own_b = lax.optimization_barrier((blocks, part))[0]
    sib_b = [swap_core(block) for block in own_b]
    hid = shape((own_count, 2 * units))
    full = shape((depth, 2 * units))
    fc_full, proj_full, dy, dact = call(
        mlp_pre_kernel,
        [full, full, shape((own_count, depth)), hid],
        info,
        seg_row,
        cotangent,
        *own_b,
        *sib_b,
        name="mlp_pre",
    )
    da, act, dhid, second, middle, stat_two = call(
        mlp_kernel,
        [
            shape((own_count, depth)),
            hid,
            hid,
            shape((own_count, depth)),
            shape((own_count, depth), F32),
            shape((own_count, 2 * TILE), F32),
        ],
        info,
        inputs,
        part,
        got,
        vec,
        vec_sib,
        fc_full,
        dact,
        scratch=[pltpu.VMEM((own_count, units), F32)],
        cost=10,
        name="mlp",
    )
    da_got = swap_chip(da)
    mlp_part, grad_own, *grad_sib, mlp_sums = call(
        mlp_grad_kernel,
        [
            shape((own_count, depth)),
            shape((CHUNKS, base, 2 * units)),
            *[shape((CHUNKS, base, units // 2))] * 4,
            shape((24, depth), F32),
        ],
        info,
        act,
        dhid,
        second,
        dy,
        proj_full,
        cost=9,
        name="mlp_grad",
    )
    mlp_got = swap_chip(mlp_part)
    exact = count == CHUNKS
    if exact:
        big_state = scatter_start(info, grad_own, grad_sib)
        big_sent = big_state[1]
        big_state = scatter_send(big_state, (0, 1))
    else:
        big = scatter_plain(grad_own, grad_sib)
        fc_weight_grad, proj_weight_grad = big[:, :units], big[:, units:].T

    dmid, branch, att_sums, dq, keep, *send = call(
        attend_back_kernel,
        [
            shape((own_count, depth), F32),
            shape((own_count, depth)),
            shape((8, depth), F32),
            shape((own_count, width2)),
            shape((2 * width2, own_count), F32),
            *[shape((width2, own_count))] * 2,
        ],
        info,
        middle,
        stat_two,
        dy,
        da,
        da_got,
        vec,
        wo,
        mixed,
        q,
        k,
        v,
        probs,
        scratch=[
            pltpu.VMEM((own_count, width2), BF),
            pltpu.VMEM((heads2, own_count, HD), BF),
            pltpu.VMEM((heads2, HD, rows), F32),
            pltpu.VMEM((heads2, HD, rows), F32),
            pltpu.VMEM((heads2, own_count, HD), F32),
            pltpu.VMEM((heads2, TILE, rows), F32),
            pltpu.VMEM((heads2, TILE, rows), BF),
            pltpu.VMEM((heads2, own_count, TILE), F32),
            pltpu.VMEM((3, 8, depth), F32),
        ],
        cost=18,
        name="attend_back",
        after=(big_sent,) if exact else (),
    )
    keep_got = [swap_core(piece) for piece in send]
    if exact:
        big_state = scatter_middle(info, big_state, False, after=(dq, mlp_got))
        big_ready = big_state[0]
        big_state = scatter_send(big_state, (1, 0))
    first_part, dkv = call(
        first_grad_kernel,
        [shape((own_count, depth)), shape((2 * width2, own_count))],
        info,
        dq,
        keep,
        *keep_got,
        wq,
        wk,
        wv,
        name="first_grad",
        after=(big_ready,) if exact else (),
    )
    first_got = swap_chip(first_part)
    qkv_own, *qkv_sib, tile_own, tile_sib = call(
        qkv_grad_kernel,
        [
            shape((CHUNKS, base, 4 * width)),
            *[shape((CHUNKS, base, 2 * width))] * 2,
            *[shape((EXTRA, depth))] * 2,
        ],
        info,
        first_own,
        dq,
        dkv,
        branch,
        mixed,
        first_part,
        inputs,
        stat_one,
        mlp_sums,
        att_sums,
        scratch=[pltpu.VMEM((EXTRA, depth), F32), pltpu.VMEM((2, 8, depth), F32)],
        cost=7,
        name="qkv_grad",
        after=(big_state[1], big_state[3]) if exact else (),
    )
    finish = lambda after: call(
        final_kernel,
        [shape((rows, depth))],
        info,
        inputs,
        stat_one,
        first_part,
        first_got,
        dmid,
        vec,
        seg_row,
        middle,
        mlp_part,
        mlp_got,
        name="final",
        cost=7,
        after=after,
    )[0]
    tiles = (tile_own, swap_core(tile_sib))
    if exact:
        big_last = scatter_late(info, big_state, False, after=(qkv_own,))
        small_state = scatter_start(info, qkv_own, qkv_sib, tiles, after=(big_last[0],))
        small_sent = small_state[1]
        small_state = scatter_send(small_state, (0, 1))
        both_low = finish((small_sent,))
        small_state = scatter_middle(info, small_state, True, after=(both_low, big_last[1]))
        small_state = scatter_send(small_state, (1, 0))
        fc_weight_grad, proj_weight_grad = call(
            scatter_big_kernel,
            [shape((local, units), F32), shape((units, local), F32)],
            info,
            *big_last,
            name="scatter_big",
            cost=15,
        )
        small_last = scatter_late(info, small_state, True)
        outputs, inputs_grad = all_rows(info, both_low, (small_last[0],))
        qkv_weight_grad, attn_weight_grad, tile, tile_low = call(
            scatter_small_kernel,
            [
                shape((3, local, width), F32),
                shape((width, local), F32),
                shape((EXTRA, depth), F32),
                shape((EXTRA, depth)),
            ],
            info,
            *small_last,
            name="scatter_small",
            cost=2,
            after=(fc_weight_grad, inputs_grad),
        )
    else:
        outputs, inputs_grad = all_rows(info, finish(()))
        mine = scatter_plain(qkv_own, qkv_sib)
        qkv_weight_grad = mine[:, : 3 * width].reshape(local, 3, width).transpose(1, 0, 2)
        attn_weight_grad = mine[:, 3 * width :].T
        tile = lax.psum(tiles[0].astype(F32) + tiles[1].astype(F32), "dp")
        tile_low = tile.astype(BF)
    tile_got = swap_chip(tile_low).astype(F32)
    mask = (jnp.arange(EXTRA) < 2)[:, None]
    tile = jnp.where(mask, tile_low.astype(F32) + tile_got, tile)
    parts = lax.dynamic_slice(tile, (0, index * local), (7, local))
    bias_sum = tile[7, :width2].reshape(2, heads, HD).transpose(1, 0, 2).reshape(heads, 2 * HD)
    qv_bias_grad = lax.dynamic_slice(bias_sum, (0, index * bias_width), (heads, bias_width))
    return (
        outputs,
        inputs_grad,
        parts[0],
        parts[1],
        qkv_weight_grad,
        qv_bias_grad,
        attn_weight_grad,
        parts[2],
        parts[3],
        parts[4],
        fc_weight_grad,
        parts[5][None],
        proj_weight_grad,
        parts[6],
    )


def solution(mesh):
    return jax.shard_map(
        body,
        mesh=mesh,
        in_specs=(
            P("dp", None),
            P("dp"),
            P("dp"),
            P("dp"),
            P(None, "dp", "mp"),
            P("mp", "dp"),
            P("mp", "dp"),
            P("dp"),
            P("dp"),
            P("dp"),
            P("dp", "mp"),
            P("mp", "dp"),
            P("mp", "dp"),
            P("dp"),
            P("dp", None),
        ),
        out_specs=(
            P("dp", None),
            P("dp", None),
            P("dp"),
            P("dp"),
            P(None, "dp", "mp"),
            P("mp", "dp"),
            P("mp", "dp"),
            P("dp"),
            P("dp"),
            P("dp"),
            P("dp", "mp"),
            P("mp", "dp"),
            P("mp", "dp"),
            P("dp"),
        ),
        check_vma=False,
    )
```
